32 devices in a mesh: dp: 8 (over y, x, core), tensor: 4 (over z).
Axes of the slice: x: 2, y: 2, z: 4, core: 2. Of those that a mesh axis runs over, the one named last changes fastest.
Arguments:
- tokens: bfloat16 [16384, 768], P(('dp', 'tensor')), may hold values from -6 to 6
- cotangent: bfloat16 [16384, 768], P(('dp', 'tensor')), may hold values from -6 to 6, as said below
- segment: int32 [32, 512], P(('dp', 'tensor')), may hold values from 0 to 11, never falling along the last dimension, each value on 1 to 202 neighbouring positions
- projection: float32 [64, 32], replicated, may hold values from -5 to 5
- first_gain: float32 [768], replicated, may hold values from 0.5 to 1.5
- first_bias: float32 [768], replicated, may hold values from -4 to 4
- w_query: bfloat16 [768, 768], replicated, may hold values from -0.109375 to 0.109375
- w_key: bfloat16 [768, 768], replicated, may hold values from -0.109375 to 0.109375
- w_value: bfloat16 [768, 768], replicated, may hold values from -0.21875 to 0.21875
- w_out: bfloat16 [768, 768], replicated, may hold values from -1.25 to 1.25
- b_query: float32 [768], replicated, may hold values from -4 to 4
- b_key: float32 [768], replicated, may hold values from -4 to 4
- b_value: float32 [768], replicated, may hold values from -4 to 4
- b_out: float32 [768], replicated, may hold values from -4 to 4
- second_gain: float32 [768], replicated, may hold values from 0.5 to 1.5
- second_bias: float32 [768], replicated, may hold values from -4 to 4
- w_up: bfloat16 [768, 3072], P(None, 'tensor'), may hold values from -0.21875 to 0.21875
- b_up: float32 [3072], P('tensor'), may hold values from -4 to 4
- w_down: bfloat16 [3072, 768], P('tensor'), may hold values from -0.109375 to 0.109375
- b_down: float32 [768], replicated, may hold values from -4 to 4
Outputs:
- output: bfloat16 [16384, 768], P(('dp', 'tensor'))
- grad_tokens: bfloat16 [16384, 768], P(('dp', 'tensor'))
- grad_first_gain: float32 [768], replicated
- grad_first_bias: float32 [768], replicated
- grad_w_query: float32 [768, 768], replicated
- grad_w_key: float32 [768, 768], replicated
- grad_w_value: float32 [768, 768], replicated
- grad_w_out: float32 [768, 768], replicated
- grad_b_query: float32 [768], replicated
- grad_b_key: float32 [768], replicated
- grad_b_value: float32 [768], replicated
- grad_b_out: float32 [768], replicated
- grad_second_gain: float32 [768], replicated
- grad_second_bias: float32 [768], replicated
- grad_w_up: float32 [768, 3072], P(None, 'tensor')
- grad_b_up: float32 [3072], P('tensor')
- grad_w_down: float32 [3072, 768], P('tensor')
- grad_b_down: float32 [768], replicated
The draws below stay inside these ranges and needn't reach their ends.
Inputs may be any that keep to these rules, and one draw needn't show every extreme that they name: `segment`: within each row of 512 tokens, molecule numbers never fall; each molecule has 1 to 202 tokens and one has exactly 202. `cotangent`: gradient rows of order one.
All inputs are finite; a program needn't handle non-finite values.
Results may differ from the reference program's by a relative error of at most 0.01.
Values may be sent and summed in bfloat16 or wider, within the bound.
No kernel may reach another device: no remote copies, remote signals or barrier semaphores. Data moves between devices by JAX's collectives and lax.ppermute only.
A program may use at most 192 MiB of HBM per device.

```python
import math
import jax
import jax.numpy as jnp
import numpy as np
from jax import lax

D = 768
HEADS = 12
HEAD_DIM = 64
FEAT = 32
FF = 3072
ROWS = 512
LONGEST = 202
SEGS = 12
BLOCKS = 32
TOKENS = 16384


def draw_cotangent(key, part):
    key = jax.random.fold_in(key, 7)
    blocks_at = (jnp.arange(TOKENS) // ROWS).astype(jnp.float32)
    growth = 0.5 + blocks_at / max(BLOCKS - 1, 1)
    drawn = jnp.clip(jax.random.normal(key, (TOKENS, D), jnp.float32), -4.0, 4.0)
    return (drawn * growth[:, None]).astype(jnp.bfloat16)


def block_scale(stream_key, shape, pieces, smallest, largest):
    def one(axis_at, blocks):
        draws = jax.random.uniform(jax.random.fold_in(jax.random.fold_in(stream_key, 6), axis_at), (blocks,), jnp.float32, smallest / len(pieces), largest / len(pieces))
        return jnp.repeat(jnp.exp(draws), shape[axis_at] // blocks).reshape((-1,) + (1,) * (len(shape) - axis_at - 1))

    loudness = one(*pieces[0])
    for cut in pieces[1:]:
        loudness = loudness * one(*cut)
    return loudness


def length_profile(amount, total, most, slope):
    weights = [(1 << 20) // math.isqrt(standing ** slope) + 1 for standing in range(2, amount + 1)]
    surplus, holding = total - most - (amount - 1), [1] * (amount - 1)
    while surplus > 0:
        free = [i for i in range(amount - 1) if holding[i] < most]
        mass, left = sum([weights[i] for i in free]), surplus
        for i in free:
            more = min(most - holding[i], max(1, left * weights[i] // mass), surplus)
            holding[i] = holding[i] + more
            surplus = surplus - more
    return np.array([most] + holding)


def ragged_sizes(stream_key, number_of, total, limit, lean):
    if number_of == 2:
        one = jax.random.randint(stream_key, (), max(1, total - limit), min(limit, total - 1) + 1)
        return jnp.stack([one, total - one])
    sizes = jnp.asarray(length_profile(number_of, total, limit, lean), jnp.int32)
    twos = (number_of - 1) // 2
    giver, sink = sizes[1:1 + 2 * twos:2], sizes[2:2 + 2 * twos:2]
    slack = jnp.minimum(giver - 1, limit - sink)
    moved = jax.random.randint(jax.random.fold_in(stream_key, 1), (twos,), 0, 1 << 20) % (slack + 1)
    sizes = sizes.at[1:1 + 2 * twos:2].set(giver - moved).at[2:2 + 2 * twos:2].set(sink + moved)
    return sizes[jax.random.permutation(jax.random.fold_in(stream_key, 2), number_of)]


def scatter_about(key, dims, width, limit, pieces=(), held_as=jnp.bfloat16):
    values = width * jax.random.normal(key, dims, jnp.float32)
    if pieces:
        values = values * block_scale(key, dims, pieces, -0.22, 0.18)
    return jnp.clip(values, -limit, limit).astype(held_as)


def setup_inputs(seed: int = 0) -> dict:
    splits = jax.random.split(jax.random.key(seed), 21)
    return {
        "tokens": scatter_about(splits[0], (TOKENS, D), 1.0, 6.0, ((0, 32),)),
        "cotangent": draw_cotangent(jax.random.fold_in(splits[20], 71), 0),
        "segment": jax.vmap(lambda own: jnp.searchsorted(jnp.cumsum(ragged_sizes(own, SEGS, ROWS, LONGEST, 1)), jnp.arange(ROWS), side="right"))(jax.random.split(splits[2], BLOCKS)).reshape((BLOCKS, ROWS)).astype(jnp.int32),
        "projection": scatter_about(splits[3], (HEAD_DIM, FEAT), 1.0, 5.0, (), jnp.float32),
        "first_gain": jnp.clip(1.0 + 0.1 * jax.random.normal(splits[4], (D,), jnp.float32), 0.5, 1.5),
        "first_bias": scatter_about(splits[5], (D,), 0.3, 4.0, (), jnp.float32),
        "w_query": scatter_about(splits[6], (D, D), (4 * D) ** -0.5, 0.109375),
        "w_key": scatter_about(splits[7], (D, D), (4 * D) ** -0.5, 0.109375),
        "w_value": scatter_about(splits[8], (D, D), D ** -0.5, 0.21875),
        "w_out": scatter_about(splits[9], (D, D), (D // 32) ** -0.5, 1.25),
        "b_query": scatter_about(splits[10], (D,), 0.3, 4.0, (), jnp.float32),
        "b_key": scatter_about(splits[11], (D,), 0.3, 4.0, (), jnp.float32),
        "b_value": scatter_about(splits[12], (D,), 0.3, 4.0, (), jnp.float32),
        "b_out": scatter_about(splits[13], (D,), 0.3, 4.0, (), jnp.float32),
        "second_gain": jnp.clip(1.0 + 0.1 * jax.random.normal(splits[14], (D,), jnp.float32), 0.5, 1.5),
        "second_bias": scatter_about(splits[15], (D,), 0.3, 4.0, (), jnp.float32),
        "w_up": scatter_about(splits[16], (D, FF), D ** -0.5, 0.21875, ((1, 4),)),
        "b_up": scatter_about(splits[17], (FF,), 0.3, 4.0, ((0, 4),), jnp.float32),
        "w_down": scatter_about(splits[18], (FF, D), FF ** -0.5, 0.109375, ((0, 4),)),
        "b_down": scatter_about(splits[19], (D,), 0.3, 4.0, (), jnp.float32),
    }


highest_precision = lax.Precision.HIGHEST

@jax.custom_vjp
def low(v):
    return lax.optimization_barrier(v.astype(jnp.bfloat16)).astype(jnp.float32)

@jax.custom_vjp
def low_back(v):
    return v

def low_keep(v):
    return (low(v), None)

def low_pass(kept, grad):
    return (grad,)

def back_keep(v):
    return (v, None)

def back_low(kept, grad):
    return (low(grad),)
low.defvjp(low_keep, low_pass)
low_back.defvjp(back_keep, back_low)

def layer_norm(inputs, gain, shift):
    average = lax.optimization_barrier(jnp.mean(inputs, -1, keepdims=True))
    centred = inputs - average
    spread = lax.optimization_barrier(jnp.mean(centred * centred, -1, keepdims=True))
    return centred * lax.rsqrt(spread + 1e-05) * gain + shift

def positions(labels):
    places = jnp.arange(labels.shape[0], dtype=jnp.int32)
    matches = labels[:, None] == labels[None, :]
    before = places[None, :] < places[:, None]
    return lax.optimization_barrier(jnp.sum((matches & before).astype(jnp.int32), axis=1))

def rotate(inputs, places):
    split_at = inputs.shape[-1] // 2
    ladder = jnp.arange(split_at).astype(jnp.float32)
    speeds = jnp.exp(ladder * (-2.0 * math.log(10000.0) / inputs.shape[-1]))
    angles = places.astype(jnp.float32)[:, None] * speeds[None, :]
    cosine = jnp.cos(angles)[:, None, :]
    sine_part = jnp.sin(angles)[:, None, :]
    lower_half = inputs[..., :split_at]
    upper_half = inputs[..., split_at:]
    return jnp.concatenate([lower_half * cosine - upper_half * sine_part, upper_half * cosine + lower_half * sine_part], -1)

def features(inputs, projection):
    scaled = inputs * inputs.shape[-1] ** (-0.25)
    projected = jnp.einsum('rhd,df->rhf', scaled, projection, precision=highest_precision)
    return jnp.exp(projected - 0.5 * lax.optimization_barrier(jnp.sum(scaled * scaled, -1, keepdims=True))) * projection.shape[-1] ** (-0.5)

def attend(queries, key_rows, value_rows, labels, projection):
    row_count = queries.shape[0]
    places = positions(labels)
    query_feature_map = features(rotate(queries.reshape(row_count, HEADS, -1), places), projection)
    key_feature_map = features(rotate(key_rows.reshape(row_count, HEADS, -1), places), projection)
    value_heads = value_rows.reshape(row_count, HEADS, -1)
    attention_scores = jnp.einsum('otg,atg->toa', query_feature_map, key_feature_map, precision=highest_precision)
    matches = (labels[:, None] == labels[None, :]).astype(attention_scores.dtype)
    weights = attention_scores * matches[None]
    totals = lax.optimization_barrier(jnp.sum(weights, -1))
    mixture = jnp.einsum('hqk,khd->qhd', weights, value_heads, precision=highest_precision)
    return (mixture / jnp.transpose(totals)[:, :, None]).reshape(row_count, -1)

def matmul(left, right):
    return jnp.dot(left, right, preferred_element_type=jnp.float32, precision=highest_precision)

def block_row_span(tokens_in, labels_in, params, projection):
    first_gain, first_bias, w_query, w_key, w_value, w_out, b_query, b_key, b_value, b_out, second_gain, second_bias, w_up, b_up, w_down, b_down = params
    blocks_in = labels_in.shape[0]
    block_len = labels_in.shape[1]
    normed = low(layer_norm(tokens_in, first_gain, first_bias))
    queries = low_back(matmul(normed, w_query) + b_query)
    key_rows = low_back(matmul(normed, w_key) + b_key)
    value_rows = low_back(matmul(normed, w_value) + b_value)

    def one_block(member):
        return attend(member[0], member[1], member[2], member[3], projection)
    context = lax.map(jax.checkpoint(one_block), (queries.reshape(blocks_in, block_len, D), key_rows.reshape(blocks_in, block_len, D), value_rows.reshape(blocks_in, block_len, D), labels_in))
    context = low(context.reshape(-1, D))
    attended = low_back(matmul(context, w_out) + b_out)
    middle = tokens_in + attended
    second = low(layer_norm(middle, second_gain, second_bias))
    inner_rows = low_back(matmul(second, w_up) + b_up)
    hidden = low(jax.nn.gelu(inner_rows, approximate=False))
    branch = low_back(matmul(hidden, w_down) + b_down)
    return middle + branch

def reference(tokens, cotangent, segment, projection, first_gain, first_bias, w_query, w_key, w_value, w_out, b_query, b_key, b_value, b_out, second_gain, second_bias, w_up, b_up, w_down, b_down):
    params = tuple((member.astype(jnp.float32) for member in (first_gain, first_bias, w_query, w_key, w_value, w_out, b_query, b_key, b_value, b_out, second_gain, second_bias, w_up, b_up, w_down, b_down)))
    groups = BLOCKS // 8

    def forward(token_rows, weights_in):
        stacked = token_rows.reshape(groups, 8 * ROWS, D)
        labels_all = segment.reshape(groups, 8, ROWS)

        def one_group(member):
            return block_row_span(member[0], member[1], weights_in, projection)
        result = lax.map(jax.checkpoint(one_group), (stacked, labels_all))
        return result.reshape(-1, D)
    result, pullback = jax.vjp(forward, tokens.astype(jnp.float32), params)
    token_grad, grads = pullback(cotangent.astype(jnp.float32))
    return (result.astype(jnp.bfloat16), token_grad.astype(jnp.bfloat16), grads[0], grads[1], grads[2], grads[3], grads[4], grads[5], grads[6], grads[7], grads[8], grads[9], grads[10], grads[11], grads[12], grads[13], grads[14], grads[15])
```

```python
from functools import partial
import math

import jax
import jax.numpy as jnp
import ml_dtypes
import numpy as np
from jax import lax
from jax.experimental import pallas as pl
from jax.experimental.pallas import tpu as pltpu
from jax.sharding import PartitionSpec as P

HEADS = 12
HD = 64
FEAT = 32
EPS = 1e-05
F32 = jnp.float32
BF16 = jnp.bfloat16
ANY = pl.BlockSpec(memory_space=pl.ANY)
SMEM = pl.BlockSpec(memory_space=pltpu.SMEM)
SCALE = HD ** -0.25


def nn(a, b):
    return lax.dot_general(a, b, (((1,), (0,)), ((), ())), preferred_element_type=F32)


def nt(a, b):
    return lax.dot_general(a, b, (((1,), (1,)), ((), ())), preferred_element_type=F32)


def split(v):
    high = v.astype(BF16)
    return high, (v - high.astype(F32)).astype(BF16)


def rotary_table(length):
    half = HD // 2
    rate = np.exp(np.arange(half) * (-2.0 * math.log(10000.0) / HD))
    angle = np.arange(length)[:, None] * rate[None, :]
    lane = np.arange(128)
    cos = np.tile(np.cos(angle), (1, 4)) * SCALE
    sin = np.tile(np.sin(angle), (1, 4)) * SCALE
    first = (lane % HD < half)[None, :]
    table = np.concatenate([cos, -sin * first, sin * ~first], 1).astype(np.float32)
    parts = []
    for _ in range(3):
        part = table.astype(ml_dtypes.bfloat16)
        parts.append(part)
        table = table - part.astype(np.float32)
    return np.stack(parts)


def lane_mask(head_in_group):
    lane = lax.broadcasted_iota(jnp.int32, (1, 128), 1)
    return jnp.where(lane // FEAT == head_in_group, 1.0, 0.0).astype(BF16)


def norm_parts(v):
    centred = v - jnp.mean(v, -1, keepdims=True)
    scale = lax.rsqrt(jnp.mean(centred * centred, -1, keepdims=True) + EPS)
    return centred * scale, scale


def norm_back(grad, hat, scale, gain):
    hat_grad = grad * gain
    return scale * (
        hat_grad
        - jnp.mean(hat_grad, -1, keepdims=True)
        - hat * jnp.mean(hat_grad * hat, -1, keepdims=True)
    )


def label_column(seg):
    rows = seg.shape[1]
    return jnp.transpose(jnp.broadcast_to(seg[...].astype(F32), (128, rows)))


def block_projection(proj):
    tall = jnp.concatenate([proj[...]] * 4, axis=0)
    wide = jnp.concatenate([tall] * 4, axis=1)
    group = lax.broadcasted_iota(jnp.int32, (256, 128), 0) // HD
    feat = lax.broadcasted_iota(jnp.int32, (256, 128), 1) // FEAT
    return jnp.where(group == feat, wide, 0.0), jnp.where(group == feat, 1.0, 0.0).astype(BF16)


def turn(u, cos, sin_a, sin_b):
    return u * cos + pltpu.roll(u, 96, 1) * sin_a + pltpu.roll(u, 32, 1) * sin_b


def turn_back(u, cos, sin_a, sin_b):
    return u * cos - pltpu.roll(u, 96, 1) * sin_a - pltpu.roll(u, 32, 1) * sin_b


class Feed:
    def __init__(self, pairs, sems):
        self.copies = [pltpu.make_async_copy(src, dst, sems.at[n]) for n, (src, dst) in enumerate(pairs)]
        for copy in self.copies:
            copy.start()
        self.left = list(range(len(self.copies)))

    def need(self, *which):
        for n in which:
            if n in self.left:
                self.copies[n].wait()
                self.left.remove(n)


class Drain:
    def __init__(self, sems):
        self.sems, self.copies = sems, []

    def put(self, src, dst):
        copy = pltpu.make_async_copy(src, dst, self.sems.at[len(self.copies)])
        copy.start()
        self.copies.append(copy)

    def end(self):
        for copy in self.copies:
            copy.wait()


def call(kernel, name, ins, outs, scratch, n_in, n_out, limit, smem=0, cost=0, trans=0, moved=0):
    return pl.pallas_call(
        kernel,
        out_shape=outs,
        in_specs=[SMEM] * smem + [ANY] * (len(ins) - smem),
        out_specs=[ANY] * len(outs),
        scratch_shapes=list(scratch) + [pltpu.SemaphoreType.DMA((n_in,)), pltpu.SemaphoreType.DMA((n_out,))],
        compiler_params=pltpu.CompilerParams(vmem_limit_bytes=limit << 20),
        cost_estimate=pl.CostEstimate(flops=cost, bytes_accessed=moved, transcendentals=trans),
        name=name,
    )(*ins)


FWD_IN = 16
FWD_OUT = 10


def attn_fwd_kernel(*refs):
    ins, outs = refs[:FWD_IN], refs[FWD_IN:FWD_IN + FWD_OUT]
    held = refs[FWD_IN + FWD_OUT:FWD_IN + FWD_OUT + FWD_IN]
    res = refs[2 * FWD_IN + FWD_OUT:2 * FWD_IN + 2 * FWD_OUT]
    col_s, in_sem, out_sem = refs[2 * FWD_IN + 2 * FWD_OUT:]
    feed = Feed(list(zip(ins, held)), in_sem)
    drain = Drain(out_sem)
    tok, seg, fg, fb, wv, wq, bq, wk, bk, tab, proj, wo, bv, bo, sg, sb = (held[n] for n in range(16))
    normed_o, s_o, f_o, v_o, c0_o, ctx_o, dinv_o, mid_o, sec_o, rot_o = res
    rows, width = tok.shape
    feed.need(1, 9)
    col_s[...] = label_column(seg)
    seg_row = seg[...].astype(F32)
    less = jnp.where(seg_row < col_s[:, :1], 1.0, 0.0)
    start = jnp.sum(less, axis=1, keepdims=True)
    place = lax.broadcasted_iota(jnp.int32, (rows, 1), 0).astype(F32) - start
    length = tab.shape[1]
    ladder = lax.broadcasted_iota(jnp.int32, (rows, length), 1).astype(F32)
    one_hot = jnp.where(ladder == place, 1.0, 0.0).astype(BF16)
    rot_o[...] = nn(one_hot, tab[0]) + nn(one_hot, tab[1]) + nn(one_hot, tab[2])

    feed.need(*range(12))
    p_wide, blocks = block_projection(proj)
    p_hi, p_lo = split(p_wide)
    halves = blocks * 0.5

    tile = 256

    def first(i, _):
        at = pl.ds(pl.multiple_of(i * tile, tile), tile)
        x = tok[at, :].astype(F32)
        hat, _scale = norm_parts(x)
        normed = (hat * fg[...] + fb[...]).astype(BF16)
        normed_o[at, :] = normed
        v_o[at, :] = nn(normed, wv[...]).astype(BF16)
        cos, sin_a, sin_b = rot_o[at, 0:128], rot_o[at, 128:256], rot_o[at, 256:384]
        for which, (w, b) in enumerate(((wq, bq), (wk, bk))):
            u = nn(normed, w[...]) + b[...]
            for j in range(width // 128):
                lanes = slice(128 * j, 128 * j + 128)
                s_o[which, at, lanes] = turn(u[:, lanes], cos, sin_a, sin_b)
            for g in range(width // 256):
                s = s_o[which, at, 256 * g:256 * g + 256]
                s_hi, s_lo = split(s)
                q_hi, q_lo = split(s * s)
                e = nn(s_hi, p_hi) + nn(s_lo, p_hi) + nn(s_hi, p_lo) - nn(q_hi, halves) - nn(q_lo, halves)
                f_o[which, at, 128 * g:128 * g + 128] = (jnp.exp(e) * FEAT ** -0.5).astype(BF16)
        return 0

    lax.fori_loop(0, rows // tile, first, 0)
    drain.put(rot_o, outs[9])
    drain.put(normed_o, outs[0])
    drain.put(s_o, outs[1])
    drain.put(f_o, outs[2])
    drain.put(v_o, outs[3])
    feed.need(*range(16))

    ones = jnp.ones((rows, 128), BF16)
    even = lax.broadcasted_iota(jnp.int32, (1, 128), 1) < HD

    def second(i, _):
        at = pl.ds(pl.multiple_of(i * tile, tile), tile)
        same = col_s[at, :1] == seg_row
        for j in range(HEADS // 2):
            g = j // 2
            vals = jnp.concatenate([v_o[:, 128 * j:128 * j + 128], ones], 1)
            qf = f_o[0, at, 128 * g:128 * g + 128]
            kf = f_o[1, :, 128 * g:128 * g + 128]
            res = []
            for h in range(2):
                scores = nt(qf * lane_mask(2 * (j % 2) + h), kf)
                weights = jnp.where(same, scores, 0.0).astype(BF16)
                res.append(nn(weights, vals))
            num = jnp.where(even, res[0][:, :128], res[1][:, :128])
            inv = 1.0 / jnp.where(even, res[0][:, 128:], res[1][:, 128:])
            lanes = slice(128 * j, 128 * j + 128)
            ctx = num * inv
            dinv_o[at, lanes] = inv
            c0_o[at, lanes] = ctx
            ctx_o[at, lanes] = (ctx + bv[:, lanes]).astype(BF16)
        middle = tok[at, :].astype(F32) + nn(ctx_o[at, :], wo[...]) + bo[...]
        mid_o[at, :] = middle
        hat, _scale = norm_parts(middle)
        sec_o[at, :] = (hat * sg[...] + sb[...]).astype(BF16)
        return 0

    lax.fori_loop(0, rows // tile, second, 0)
    for n in (8, 7, 4, 5, 6):
        drain.put(res[n], outs[n])
    drain.end()


def attn_fwd(tok, seg, tab, proj, fg, fb, wq, wk, wv, wo, bq, bk, bv, bo, sg, sb):
    rows, width = tok.shape
    sd = jax.ShapeDtypeStruct
    outs = (
        sd((rows, width), BF16),
        sd((2, rows, width), F32),
        sd((2, rows, HEADS * FEAT), BF16),
        sd((rows, width), BF16),
        sd((rows, width), F32),
        sd((rows, width), BF16),
        sd((rows, width), F32),
        sd((rows, width), F32),
        sd((rows, width), BF16),
        sd((rows, 384), F32),
    )
    ins = (tok, seg, fg, fb, wv, wq, bq, wk, bk, tab, proj, wo, bv, bo, sg, sb)
    scratch = [pltpu.VMEM(v.shape, v.dtype) for v in ins + outs] + [pltpu.VMEM((rows, 128), F32)]
    return call(attn_fwd_kernel, "attn_fwd", ins, outs, scratch, len(ins), len(outs), 40,
                cost=5_000_000_000, moved=20_000_000)


FFN_STEP = 256


def ffn_kernel(first, last, *refs):
    n_in = 8 if first else 10
    place, ins, refs = refs[0], refs[1:1 + n_in], refs[1 + n_in:]
    outs, refs = refs[:5], refs[5:]
    sec, cot, wu, wd, bu, oacc, sacc, oout, gup, gdn, gb, secT, in_sem, out_sem = refs
    x, y, c = place[0], place[1], place[2]
    rows, width = sec.shape
    quarter = width // 4

    def part(a, core):
        return pl.ds(pl.multiple_of((2 * a + core) * quarter, quarter), quarter)

    if first:
        sec_i, cot_i, wu_i, wd_i, bu_i, oacc_i, bd_i = ins[:7]
        pairs = [(wu_i, wu), (sec_i, sec), (bu_i, bu.at[0:1]), (cot_i, cot), (wd_i, wd), (oacc_i, oacc), (bd_i, bu.at[8:9])]
        early, more = (0, 1, 2), (3, 4)
    else:
        sec_i, cot_i, own, own_x, own_y, far, far_x, far_y, oacc_i, sacc_i = ins
        up, down = pl.ds(0, quarter), pl.ds(quarter, quarter)
        pairs = [
            (own.at[up], wu.at[part(x, c)]), (own_x, wu.at[part(1 - x, c)]),
            (far.at[up], wu.at[part(x, 1 - c)]), (far_x, wu.at[part(1 - x, 1 - c)]),
            (sec_i, sec), (own.at[pl.ds(2 * quarter, 16)], bu),
            (cot_i, cot),
            (own.at[down], wd.at[part(y, c)]), (own_y, wd.at[part(1 - y, c)]),
            (far.at[down], wd.at[part(y, 1 - c)]), (far_y, wd.at[part(1 - y, 1 - c)]),
            (oacc_i, oacc), (sacc_i, sacc),
        ]
        early, more = tuple(range(6)), tuple(range(6, 11))
    feed = Feed(pairs, in_sem)
    drain = Drain(out_sem)
    feed.need(*early)
    if first:
        bias = bu[0:1, :]
    else:
        bias = bu[0:1, :].astype(F32) + bu[1:2, :].astype(F32) + bu[2:3, :].astype(F32)
    secT[...] = jnp.transpose(sec[...])
    for n, at in enumerate(range(0, width, FFN_STEP)):
        cs = slice(at, at + FFN_STEP)
        inner = nn(sec[...], wu[:, cs]) + bias[:, cs]
        cdf = 0.5 + 0.5 * lax.erf(inner * math.sqrt(0.5))
        slope = cdf + inner * (jnp.exp(-0.5 * inner * inner) * (1.0 / math.sqrt(2.0 * math.pi)))
        hidden = (inner * cdf).astype(BF16)
        feed.need(*more)
        grad = (nt(cot[...], wd[cs, :]) * slope).astype(BF16)
        gb[:, cs] = jnp.sum(grad.astype(F32), 0, keepdims=True)
        more_out = nn(hidden, wd[cs, :])
        more_sg = nt(grad, wu[:, cs])
        feed.need(*range(len(pairs)))
        if n == 0 and first:
            oacc[...] = oacc[...] + bu[8:9, :] + more_out
            sacc[...] = more_sg
        else:
            oacc[...] += more_out
            sacc[...] += more_sg
        gdn[cs, :] = nn(jnp.transpose(hidden), cot[...]).astype(BF16)
        gup[:, cs] = nn(secT[...], grad).astype(BF16)
    half = width // 2
    mine = pl.ds(pl.multiple_of(c * half, half), half)
    other = pl.ds(pl.multiple_of((1 - c) * half, half), half)
    drain.put(gup.at[other], outs[2].at[0])
    drain.put(gdn.at[other], outs[2].at[1])
    drain.put(gup.at[mine], outs[3].at[0])
    drain.put(gdn.at[mine], outs[3].at[1])
    drain.put(sacc, outs[1])
    if last:
        oout[...] = oacc[...].astype(BF16)
        drain.put(oout, outs[0])
    else:
        drain.put(oacc, outs[0])
    drain.put(gb, outs[4])
    drain.end()


def ffn(first, last, place, *ins):
    rows, width = ins[0].shape
    sd = jax.ShapeDtypeStruct
    v = pltpu.VMEM
    outs = (
        sd((rows, width), BF16 if last else F32),
        sd((rows, width), F32),
        sd((2, width // 2, width), BF16),
        sd((2, width // 2, width), BF16),
        sd((1, width), F32),
    )
    scratch = [
        v((rows, width), BF16), v((rows, width), BF16), v((width, width), BF16), v((width, width), BF16),
        v((16, width), F32 if first else BF16), v((rows, width), F32), v((rows, width), F32), v((rows, width), BF16),
        v((width, width), BF16), v((width, width), BF16), v((1, width), F32), v((width, rows), BF16),
    ]
    return call(partial(ffn_kernel, first, last), "ffn", (place,) + ins, outs, scratch, 13, 7, 32, smem=1,
                cost=3_600_000_000, moved=12_000_000)


BWD_IN = 20


def attn_bwd_kernel(place, *refs):
    ins, outs = refs[:BWD_IN], refs[BWD_IN:BWD_IN + 4]
    held, refs = refs[BWD_IN + 4:2 * BWD_IN + 4], refs[2 * BWD_IN + 4:]
    gtok_s, gw_s, vec, col_s, cg_s, qg_s, de_s, mg_s, tr_s, in_sem, out_sem = refs
    sgrad, mid, sg, cot, ctx, wo, seg, dinv, c0, vals, f, s, rot, proj, normed, tok, fg, wq, wk, wv = held
    c = place[2]
    feed = Feed(list(zip(ins, held)), in_sem)
    drain = Drain(out_sem)
    rows, width = tok.shape
    half = width // 2
    mine = pl.ds(pl.multiple_of(c * half, half), half)
    other = pl.ds(pl.multiple_of((1 - c) * half, half), half)
    feed.need(0, 1, 2, 3)
    hat, scale = norm_parts(mid[...])
    up = sgrad[...]
    vec[...] = jnp.zeros_like(vec)
    vec[0:1, :] = jnp.sum(up * hat, 0, keepdims=True)
    vec[1:2, :] = jnp.sum(up, 0, keepdims=True)
    g = cot[...].astype(F32)
    vec[2:3, :] = jnp.sum(g, 0, keepdims=True)
    mg = g + norm_back(up, hat, scale, sg[...])
    mg_s[...] = mg
    og = mg.astype(BF16)
    vec[3:4, :] = jnp.sum(og.astype(F32), 0, keepdims=True)
    feed.need(4, 5)
    tr_s[...] = jnp.transpose(ctx[...])
    gw_s[3] = nn(tr_s[...], og).astype(BF16)
    drain.put(gw_s.at[3, other], outs[1].at[3])
    drain.put(gw_s.at[3, mine], outs[2].at[3])
    cg_s[...] = nt(og, wo[...])

    feed.need(*range(11))
    col_s[...] = label_column(seg)
    seg_row = seg[...].astype(F32)
    ones = jnp.ones((rows, 128), BF16)
    lane = lax.broadcasted_iota(jnp.int32, (1, 128), 1)
    tile = 256

    def heads(i, _):
        at = pl.ds(pl.multiple_of(i * tile, tile), tile)
        same = col_s[at, :1] == seg_row
        for j in range(HEADS // 2):
            gr = j // 2
            lanes = slice(128 * j, 128 * j + 128)
            flanes = slice(128 * gr, 128 * gr + 128)
            v_all = jnp.concatenate([vals[:, lanes], ones], 1)
            v_at = jnp.concatenate([vals[at, lanes], ones[:tile]], 1)

            def scaled(span):
                low = (cg_s[span, lanes] * dinv[span, lanes]).astype(BF16)
                less = -(low.astype(F32) * c0[span, lanes])
                hi = less.astype(BF16).astype(F32)
                return low, hi, pltpu.roll(less - hi, 64, 1)

            g_all, hi_all, lo_all = scaled(slice(None))
            g_at, hi_at, lo_at = scaled(at)
            qf_all, kf_all = f[0, :, flanes], f[1, :, flanes]
            kf_at = f[1, at, flanes]
            res_v, dq, dk = [], None, None
            for h in range(2):
                fm = lane_mask(2 * (j % 2) + h)
                own = lane // HD == h
                vm = own.astype(F32).astype(BF16)
                wT = jnp.where(same, nt(kf_at * fm, qf_all), 0.0).astype(BF16)
                res_v.append(nn(wT, g_all))
                ga = jnp.concatenate([g_all * vm, jnp.where(own, hi_all, lo_all).astype(BF16)], 1)
                dwT = jnp.where(same, nt(v_at, ga), 0.0).astype(BF16)
                gk = nn(dwT, qf_all) * fm.astype(F32)
                dk = gk if dk is None else dk + gk
                gt = jnp.concatenate([g_at * vm, jnp.where(own, hi_at, lo_at).astype(BF16)], 1)
                dw = jnp.where(same, nt(gt, v_all), 0.0).astype(BF16)
                gq = nn(dw, kf_all) * fm.astype(F32)
                dq = gq if dq is None else dq + gq
            qg_s[2, at, lanes] = jnp.where(lane < HD, res_v[0], res_v[1]).astype(BF16)
            if j % 2 == 0:
                de_s[0, at, flanes] = dq
                de_s[1, at, flanes] = dk
            else:
                de_s[0, at, flanes] = (de_s[0, at, flanes] + dq) * f[0, at, flanes].astype(F32)
                de_s[1, at, flanes] = (de_s[1, at, flanes] + dk) * f[1, at, flanes].astype(F32)
        return 0

    lax.fori_loop(0, rows // tile, heads, 0)
    feed.need(*range(BWD_IN))

    tr_s[...] = jnp.transpose(normed[...])
    gw_s[2] = nn(tr_s[...], qg_s[2]).astype(BF16)
    drain.put(gw_s.at[2, other], outs[1].at[2])
    drain.put(gw_s.at[2, mine], outs[2].at[2])

    p_wide, blocks = block_projection(proj)
    p_hi, p_lo = split(p_wide)

    def back(i, _):
        at = pl.ds(pl.multiple_of(i * tile, tile), tile)
        cos, sin_a, sin_b = rot[at, 0:128], rot[at, 128:256], rot[at, 256:384]
        for which in range(2):
            for gr in range(width // 256):
                d_hi, d_lo = split(de_s[which, at, 128 * gr:128 * gr + 128])
                s_at = s[which, at, 256 * gr:256 * gr + 256]
                ds = nt(d_hi, p_hi) + nt(d_lo, p_hi) + nt(d_hi, p_lo) - s_at * (nt(d_hi, blocks) + nt(d_lo, blocks))
                for k in range(2):
                    du = turn_back(ds[:, 128 * k:128 * k + 128], cos, sin_a, sin_b)
                    lanes = slice(256 * gr + 128 * k, 256 * gr + 128 * k + 128)
                    qg_s[which, at, lanes] = du.astype(BF16)
        return 0

    lax.fori_loop(0, rows // tile, back, 0)

    for which in range(2):
        gw_s[which] = nn(tr_s[...], qg_s[which]).astype(BF16)
        drain.put(gw_s.at[which, other], outs[1].at[which])
        drain.put(gw_s.at[which, mine], outs[2].at[which])
    for which in range(3):
        vec[4 + which:5 + which, :] = jnp.sum(qg_s[which].astype(F32), 0, keepdims=True)
    hat1, scale1 = norm_parts(tok[...].astype(F32))
    ng = nt(qg_s[0], wq[...]) + nt(qg_s[1], wk[...]) + nt(qg_s[2], wv[...])
    vec[7:8, :] = jnp.sum(ng * hat1, 0, keepdims=True)
    vec[8:9, :] = jnp.sum(ng, 0, keepdims=True)
    gtok_s[...] = (mg_s[...] + norm_back(ng, hat1, scale1, fg[...])).astype(BF16)
    drain.put(gtok_s, outs[0])
    drain.put(vec, outs[3])
    drain.end()


def attn_bwd(place, sgrad, mid, sg, cot, ctx, wo, seg, dinv, c0, vals, f, s, rot, proj, normed, tok, fg, wq, wk, wv):
    rows, width = tok.shape
    sd = jax.ShapeDtypeStruct
    ins = (sgrad, mid, sg, cot, ctx, wo, seg, dinv, c0, vals, f, s, rot, proj, normed, tok, fg, wq, wk, wv)
    outs = (
        sd((rows, width), BF16),
        sd((4, width // 2, width), BF16),
        sd((4, width // 2, width), BF16),
        sd((16, width), F32),
    )
    scratch = [pltpu.VMEM(v.shape, v.dtype) for v in ins] + [
        pltpu.VMEM((rows, width), BF16),
        pltpu.VMEM((4, width, width), BF16),
        pltpu.VMEM((16, width), F32),
        pltpu.VMEM((rows, 128), F32),
        pltpu.VMEM((rows, width), F32),
        pltpu.VMEM((3, rows, width), BF16),
        pltpu.VMEM((2, rows, HEADS * FEAT), F32),
        pltpu.VMEM((rows, width), F32),
        pltpu.VMEM((width, rows), BF16),
    ]
    return call(attn_bwd_kernel, "attn_bwd", (place,) + ins, outs, scratch, BWD_IN, 10, 54, smem=1,
                cost=20_000_000_000, moved=30_000_000)


def add_low(a, b):
    return (a.astype(F32) + b.astype(F32)).astype(BF16)


class Links:
    def __init__(self):
        self.dp, self.ring = lax.axis_size("dp"), lax.axis_size("tensor")
        self.at = lax.axis_index("dp")
        self.z = lax.axis_index("tensor")
        self.bits = [1 << n for n in range(1, self.dp.bit_length() - 1)]

    def side(self, bit):
        return (self.at // bit) % 2

    def swap(self, v, bit):
        return lax.ppermute(v, "dp", [(i, i ^ bit) for i in range(self.dp)])

    def shift(self, v):
        return lax.ppermute(v, "tensor", [(i, (i + 1) % self.ring) for i in range(self.ring)])

    def halve(self, v, bit):
        send = lax.dynamic_index_in_dim(v, 1 - self.side(bit), v.ndim - 3, keepdims=False)
        keep = lax.dynamic_index_in_dim(v, self.side(bit), v.ndim - 3, keepdims=False)
        return add_low(keep, self.swap(send, bit))


def cut_rows(v):
    return v.reshape(v.shape[:-2] + (2, v.shape[-2] // 2, v.shape[-1]))


def sum_halves(links, a, b):
    for up, down in zip(links.bits, links.bits[::-1]):
        a, b = links.halve(cut_rows(a), up), links.halve(cut_rows(b), down)
    return a, b


def spread_rows(links, v, lead, upwards):
    n = links.dp.bit_length() - 1
    rows, width = v.shape[-2:]
    v = v.reshape((2,) * n + lead + (rows, width))
    axes = list(range(n))[::-1]
    order = [axes[0]] + (axes[1:] if upwards else axes[1:][::-1])
    perm = [n + i for i in range(len(lead))] + order + [n + len(lead), n + len(lead) + 1]
    return v.transpose(perm).reshape(lead + (rows << n, width))


def body(tokens, cotangent, segment, projection, first_gain, first_bias, w_query, w_key, w_value, w_out,
         b_query, b_key, b_value, b_out, second_gain, second_bias, w_up, b_up, w_down, b_down):
    links = Links()
    rows, width = tokens.shape
    low_bit, top_bit = links.bits[0], links.bits[-1]
    core, x, y = links.side(1), links.side(low_bit), links.side(top_bit)
    place = jnp.stack([x, y, core]).astype(jnp.int32)
    quarter = width // 4

    def line(v):
        return v.reshape(1, -1)

    bias_parts, left = [], b_up
    for _ in range(3):
        part = lax.reduce_precision(left, 8, 7)
        bias_parts.append(part.astype(BF16))
        left = left - part
    share = jnp.concatenate([
        lax.dynamic_slice_in_dim(w_up, (2 * x + core) * quarter, quarter, 0),
        lax.dynamic_slice_in_dim(w_down, (2 * y + core) * quarter, quarter, 0),
        jnp.stack(bias_parts + [jnp.zeros_like(bias_parts[0])] * 13),
    ])
    slices = []
    for _ in range(links.ring - 1):
        share = links.shift(share)
        far = links.swap(share, 1)
        own_x = links.swap(share[:quarter], low_bit)
        own_y = links.swap(share[quarter:2 * quarter], top_bit)
        slices.append((share, own_x, own_y, far, links.swap(own_x, 1), links.swap(own_y, 1)))

    table = jnp.asarray(rotary_table(256))
    normed, s, f, vals, c0, ctx, dinv, mid, second, rot = attn_fwd(
        tokens, segment, table, projection, line(first_gain), line(first_bias), w_query, w_key, w_value, w_out,
        line(b_query), line(b_key), line(b_value), line(b_out), line(second_gain), line(second_bias))

    sums, slopes = [], []
    out, sgrad, send, keep, slope = ffn(True, False, place, second, cotangent, w_up, w_down, line(b_up), mid, line(b_down), mid)
    sums.append(add_low(keep, links.swap(send, 1)))
    slopes.append(slope)
    for n, parts in enumerate(slices):
        out, sgrad, send, keep, slope = ffn(False, n == len(slices) - 1, place, second, cotangent, *parts, out, sgrad)
        sums.append(add_low(keep, links.swap(send, 1)))
        slopes.append(slope)

    total = sums[1]
    for n in list(range(2, links.ring)) + [0]:
        total = add_low(links.shift(total), sums[n])
    up_part, down_part = sum_halves(links, total[0], total[1])
    both = lax.all_gather(jnp.stack([up_part, down_part]), "dp", axis=0)
    grad_w_up = spread_rows(links, both[:, 0], (), True).astype(F32)
    grad_w_down = spread_rows(links, both[:, 1], (), False).astype(F32)

    grad_tokens, send, keep, vec = attn_bwd(
        place, sgrad, mid, line(second_gain), cotangent, ctx, w_out, segment, dinv, c0, vals, f, s, rot, projection,
        normed, tokens, line(first_gain), w_query, w_key, w_value)
    mats = add_low(keep, links.swap(send, 1))
    a, b = sum_halves(links, mats[:2], mats[2:])
    a = a.reshape(links.ring, -1, width)
    b = b.reshape(links.ring, -1, width)
    ab = jnp.stack([a, b], 1)

    def piece(n):
        return lax.dynamic_index_in_dim(ab, (links.z - n) % links.ring, 0, keepdims=False)

    total = piece(1)
    for n in list(range(2, links.ring)) + [0]:
        total = add_low(links.shift(total), piece(n))
    whole = lax.all_gather(total, ("dp", "tensor"), axis=0)
    whole = whole.reshape(links.dp, 2, links.ring // 2, 2, -1, width)
    whole = whole.transpose(0, 3, 1, 2, 4, 5).reshape(links.dp, 2, 2, -1, width)
    first_two = spread_rows(links, whole[:, 0], (2,), True).astype(F32)
    last_two = spread_rows(links, whole[:, 1], (2,), False).astype(F32)

    slope_all = jnp.zeros((links.ring, width), F32)
    for n, slope in enumerate(slopes):
        slope_all = lax.dynamic_update_slice_in_dim(slope_all, slope, (links.z - n) % links.ring, 0)
    vec = lax.psum(jnp.concatenate([vec, slope_all]), ("dp", "tensor"))
    grad_b_up = lax.dynamic_index_in_dim(vec, 16 + links.z, 0, keepdims=False)
    return (
        out, grad_tokens, vec[7], vec[8], first_two[0], first_two[1], last_two[0], last_two[1],
        vec[4], vec[5], vec[6], vec[3], vec[0], vec[1], grad_w_up, grad_b_up, grad_w_down, vec[2],
    )


def solution(mesh):
    rows = P(("dp", "tensor"), None)
    whole = P()
    return jax.shard_map(
        body,
        mesh=mesh,
        in_specs=(rows,) * 3 + (whole,) * 13 + (P(None, "tensor"), P("tensor"), P("tensor", None), whole),
        out_specs=(rows,) * 2 + (whole,) * 12 + (P(None, "tensor"), P("tensor"), P("tensor", None), whole),
        check_vma=False,
    )
```

```python
from functools import partial
import math

import jax
import jax.numpy as jnp
import ml_dtypes
import numpy as np
from jax import lax
from jax.experimental import pallas as pl
from jax.experimental.pallas import tpu as pltpu
from jax.sharding import PartitionSpec as P

HEADS = 12
HD = 64
FEAT = 32
EPS = 1e-05
F32 = jnp.float32
BF16 = jnp.bfloat16
ANY = pl.BlockSpec(memory_space=pl.ANY)
VM = pl.BlockSpec(memory_space=pltpu.VMEM)
SMEM = pl.BlockSpec(memory_space=pltpu.SMEM)
SCALE = HD ** -0.25


def nn(a, b):
    return lax.dot_general(a, b, (((1,), (0,)), ((), ())), preferred_element_type=F32)


def nt(a, b):
    return lax.dot_general(a, b, (((1,), (1,)), ((), ())), preferred_element_type=F32)


def split(v):
    high = v.astype(BF16)
    return high, (v - high.astype(F32)).astype(BF16)


def rotary_table(length):
    half = HD // 2
    rate = np.exp(np.arange(half) * (-2.0 * math.log(10000.0) / HD))
    angle = np.arange(length)[:, None] * rate[None, :]
    lane = np.arange(128)
    cos = np.tile(np.cos(angle), (1, 4)) * SCALE
    sin = np.tile(np.sin(angle), (1, 4)) * SCALE
    first = (lane % HD < half)[None, :]
    table = np.concatenate([cos, -sin * first, sin * ~first], 1).astype(np.float32)
    parts = []
    for _ in range(3):
        part = table.astype(ml_dtypes.bfloat16)
        parts.append(part)
        table = table - part.astype(np.float32)
    return np.stack(parts)


def lane_mask(head_in_group):
    lane = lax.broadcasted_iota(jnp.int32, (1, 128), 1)
    return jnp.where(lane // FEAT == head_in_group, 1.0, 0.0).astype(BF16)


def norm_parts(v):
    centred = v - jnp.mean(v, -1, keepdims=True)
    scale = lax.rsqrt(jnp.mean(centred * centred, -1, keepdims=True) + EPS)
    return centred * scale, scale


def norm_back(grad, hat, scale, gain):
    hat_grad = grad * gain
    return scale * (
        hat_grad
        - jnp.mean(hat_grad, -1, keepdims=True)
        - hat * jnp.mean(hat_grad * hat, -1, keepdims=True)
    )


def label_column(seg):
    rows = seg.shape[1]
    return jnp.transpose(jnp.broadcast_to(seg[...].astype(F32), (128, rows)))


def block_projection(proj):
    tall = jnp.concatenate([proj[...]] * 4, axis=0)
    wide = jnp.concatenate([tall] * 4, axis=1)
    group = lax.broadcasted_iota(jnp.int32, (256, 128), 0) // HD
    feat = lax.broadcasted_iota(jnp.int32, (256, 128), 1) // FEAT
    return jnp.where(group == feat, wide, 0.0), jnp.where(group == feat, 1.0, 0.0).astype(BF16)


def turn(u, cos, sin_a, sin_b):
    return u * cos + pltpu.roll(u, 96, 1) * sin_a + pltpu.roll(u, 32, 1) * sin_b


def turn_back(u, cos, sin_a, sin_b):
    return u * cos - pltpu.roll(u, 96, 1) * sin_a - pltpu.roll(u, 32, 1) * sin_b


class Feed:
    def __init__(self, pairs, sems):
        self.copies = [pltpu.make_async_copy(src, dst, sems.at[n]) for n, (src, dst) in enumerate(pairs)]
        for copy in self.copies:
            copy.start()
        self.left = list(range(len(self.copies)))

    def need(self, *which):
        for n in which or list(self.left):
            if n in self.left:
                self.copies[n].wait()
                self.left.remove(n)


def call(kernel, name, ins, outs, scratch, limit, loads, smem=0, far=(), alias=None, flops=0, moved=0):
    specs = [SMEM if n < smem else ANY if n in far else VM for n in range(len(ins))]
    return pl.pallas_call(
        kernel,
        out_shape=outs,
        in_specs=specs,
        out_specs=[VM] * len(outs),
        scratch_shapes=list(scratch) + [pltpu.SemaphoreType.DMA((loads,))],
        input_output_aliases=alias or {},
        compiler_params=pltpu.CompilerParams(vmem_limit_bytes=limit << 20),
        cost_estimate=pl.CostEstimate(flops=flops, bytes_accessed=moved, transcendentals=0),
        name=name,
    )(*ins)


TILE = 256


def attn_fwd_kernel(seg, fg, fb, bq, bk, bv, bo, sg, sb, proj, tok_i, wv_i, wq_i, tab_i, wk_i, wo_i,
                    normed_o, s_o, f_o, v_o, c0_o, ctx_o, dinv_o, mid_o, sec_o, rot_o,
                    col_s, tok, wv, wq, tab, wk, wo, sems):
    feed = Feed([(tab_i, tab), (tok_i, tok), (wv_i, wv), (wq_i, wq), (wk_i, wk), (wo_i, wo)], sems)
    rows, width = tok.shape
    col_s[...] = label_column(seg)
    seg_row = seg[...].astype(F32)
    less = jnp.where(seg_row < col_s[:, :1], 1.0, 0.0)
    start = jnp.sum(less, axis=1, keepdims=True)
    place = lax.broadcasted_iota(jnp.int32, (rows, 1), 0).astype(F32) - start
    length = tab.shape[1]
    ladder = lax.broadcasted_iota(jnp.int32, (rows, length), 1).astype(F32)
    one_hot = jnp.where(ladder == place, 1.0, 0.0).astype(BF16)
    p_wide, blocks = block_projection(proj)
    p_hi, p_lo = split(p_wide)
    halves = blocks * 0.5
    feed.need(0)
    rot_o[...] = nn(one_hot, tab[0]) + nn(one_hot, tab[1]) + nn(one_hot, tab[2])
    feed.need(1, 2, 3, 4)

    def first(i, _):
        at = pl.ds(pl.multiple_of(i * TILE, TILE), TILE)
        x = tok[at, :].astype(F32)
        hat, _scale = norm_parts(x)
        normed = (hat * fg[...] + fb[...]).astype(BF16)
        normed_o[at, :] = normed
        v_o[at, :] = nn(normed, wv[...]).astype(BF16)
        cos, sin_a, sin_b = rot_o[at, 0:128], rot_o[at, 128:256], rot_o[at, 256:384]
        for which, (w, b) in enumerate(((wq, bq), (wk, bk))):
            u = nn(normed, w[...]) + b[...]
            for j in range(width // 128):
                lanes = slice(128 * j, 128 * j + 128)
                s_o[which, at, lanes] = turn(u[:, lanes], cos, sin_a, sin_b)
            for g in range(width // 256):
                s = s_o[which, at, 256 * g:256 * g + 256]
                s_hi, s_lo = split(s)
                q_hi, q_lo = split(s * s)
                e = nn(s_hi, p_hi) + nn(s_lo, p_hi) + nn(s_hi, p_lo) - nn(q_hi, halves) - nn(q_lo, halves)
                f_o[which, at, 128 * g:128 * g + 128] = (jnp.exp(e) * FEAT ** -0.5).astype(BF16)
        return 0

    lax.fori_loop(0, rows // TILE, first, 0)
    feed.need()

    ones = jnp.ones((rows, 128), BF16)
    even = lax.broadcasted_iota(jnp.int32, (1, 128), 1) < HD

    def second(i, _):
        at = pl.ds(pl.multiple_of(i * TILE, TILE), TILE)
        same = col_s[at, :1] == seg_row
        for j in range(HEADS // 2):
            g = j // 2
            vals = jnp.concatenate([v_o[:, 128 * j:128 * j + 128], ones], 1)
            qf = f_o[0, at, 128 * g:128 * g + 128]
            kf = f_o[1, :, 128 * g:128 * g + 128]
            res = []
            for h in range(2):
                scores = nt(qf * lane_mask(2 * (j % 2) + h), kf)
                weights = jnp.where(same, scores, 0.0).astype(BF16)
                res.append(nn(weights, vals))
            num = jnp.where(even, res[0][:, :128], res[1][:, :128])
            inv = 1.0 / jnp.where(even, res[0][:, 128:], res[1][:, 128:])
            lanes = slice(128 * j, 128 * j + 128)
            ctx = num * inv
            dinv_o[at, lanes] = inv
            c0_o[at, lanes] = ctx
            ctx_o[at, lanes] = (ctx + bv[:, lanes]).astype(BF16)
        middle = tok[at, :].astype(F32) + nn(ctx_o[at, :], wo[...]) + bo[...]
        mid_o[at, :] = middle
        hat, _scale = norm_parts(middle)
        sec_o[at, :] = (hat * sg[...] + sb[...]).astype(BF16)
        return 0

    lax.fori_loop(0, rows // TILE, second, 0)


def attn_fwd(tok, seg, tab, proj, fg, fb, wq, wk, wv, wo, bq, bk, bv, bo, sg, sb):
    rows, width = tok.shape
    sd, v = jax.ShapeDtypeStruct, pltpu.VMEM
    outs = (
        sd((rows, width), BF16),
        sd((2, rows, width), F32),
        sd((2, rows, HEADS * FEAT), BF16),
        sd((rows, width), BF16),
        sd((rows, width), F32),
        sd((rows, width), BF16),
        sd((rows, width), F32),
        sd((rows, width), F32),
        sd((rows, width), BF16),
        sd((rows, 384), F32),
    )
    near = (seg, fg, fb, bq, bk, bv, bo, sg, sb, proj)
    far = (tok, wv, wq, tab, wk, wo)
    scratch = [v((rows, 128), F32)] + [v(a.shape, a.dtype) for a in far]
    return call(attn_fwd_kernel, "attn_fwd", near + far, outs, scratch, 24, len(far),
                far=range(len(near), len(near) + len(far)), flops=5_000_000_000, moved=8_000_000)


FFN_STEP = 256


def ffn_kernel(first, last, place, sec, cot, *refs):
    n_in = 5 if first else 8
    ins, refs = refs[:n_in], refs[n_in:]
    out_o, sg_o, send_o, keep_o, gb_o, wu, wd, secT, hidT, acc, sems = refs
    x, y, c = place[0], place[1], place[2]
    rows, width = sec.shape
    quarter, half = width // 4, width // 2

    def part(a, core):
        return pl.ds(pl.multiple_of((2 * a + core) * quarter, quarter), quarter)

    if first:
        bu, oacc, bd, wu_i, wd_i = ins
        feed = Feed([(wu_i, wu), (wd_i, wd)], sems)
        bias = bu[...]
        early = (0,)
    else:
        own, own_x, own_y, far, far_x, far_y, oacc, sacc = ins
        up, down = pl.ds(0, quarter), pl.ds(quarter, quarter)
        feed = Feed([
            (own.at[up], wu.at[part(x, c)]), (own_x, wu.at[part(1 - x, c)]),
            (far.at[up], wu.at[part(x, 1 - c)]), (far_x, wu.at[part(1 - x, 1 - c)]),
            (own.at[down], wd.at[part(y, c)]), (own_y, wd.at[part(1 - y, c)]),
            (far.at[down], wd.at[part(y, 1 - c)]), (far_y, wd.at[part(1 - y, 1 - c)]),
        ], sems)
        tail = own[2 * quarter:2 * quarter + 16, :].astype(F32)
        bias = tail[0:1, :] + tail[1:2, :] + tail[2:3, :]
        early = (0, 1, 2, 3)
    mine = pl.ds(pl.multiple_of(c * half, half), half)
    other = pl.ds(pl.multiple_of((1 - c) * half, half), half)
    secT[...] = jnp.transpose(sec[...])
    feed.need(*early)
    cut = FFN_STEP // 2
    for n, at in enumerate(range(0, width, FFN_STEP)):
        cs = slice(at, at + FFN_STEP)
        inner = nn(sec[...], wu[:, cs]) + bias[:, cs]
        cdf = 0.5 + 0.5 * lax.erf(inner * math.sqrt(0.5))
        slope = cdf + inner * (jnp.exp(-0.5 * inner * inner) * (1.0 / math.sqrt(2.0 * math.pi)))
        hidden = (inner * cdf).astype(BF16)
        feed.need()
        grad = (nt(cot[...], wd[cs, :]) * slope).astype(BF16)
        gb_o[:, cs] = jnp.sum(grad.astype(F32), 0, keepdims=True)
        more_out = nn(hidden, wd[cs, :])
        more_sg = nt(grad, wu[:, cs])
        if n == 0:
            acc[...] = oacc[...] + more_out + (bd[...] if first else 0.0)
            sg_o[...] = more_sg if first else sacc[...] + more_sg
        else:
            acc[...] += more_out
            sg_o[...] += more_sg
        hidT[...] = jnp.transpose(hidden)
        piece = slice(n * cut, n * cut + cut)
        keep_o[1, piece, :] = nn(hidT[pl.ds(pl.multiple_of(c * cut, cut), cut), :], cot[...]).astype(BF16)
        send_o[1, piece, :] = nn(hidT[pl.ds(pl.multiple_of((1 - c) * cut, cut), cut), :], cot[...]).astype(BF16)
        keep_o[0, :, cs] = nn(secT[mine, :], grad).astype(BF16)
        send_o[0, :, cs] = nn(secT[other, :], grad).astype(BF16)
    out_o[...] = acc[...].astype(out_o.dtype)


def ffn(first, last, place, sec, cot, *ins):
    rows, width = sec.shape
    sd, v = jax.ShapeDtypeStruct, pltpu.VMEM
    outs = (
        sd((rows, width), BF16 if last else F32),
        sd((rows, width), F32),
        sd((2, width // 2, width), BF16),
        sd((2, width // 2, width), BF16),
        sd((1, width), F32),
    )
    scratch = [v((width, width), BF16), v((width, width), BF16), v((width, rows), BF16), v((FFN_STEP, rows), BF16),
               v((rows, width), F32)]
    return call(partial(ffn_kernel, first, last), "ffn", (place, sec, cot) + ins, outs, scratch, 16, 8, smem=1,
                far=(6, 7) if first else tuple(range(3, 9))[1:], alias=None if first else {10: 1},
                flops=3_600_000_000, moved=12_000_000)


def value_bwd_kernel(place, sgrad, mid, sg, cot, ctx, seg, dinv, c0, f, normed, wo_i,
                     send_o, keep_o, low_o, hi_o, lo_o, gv_o, mg_o, normT_o, vec,
                     wo, col_s, tr_s, cg_s, sems):
    feed = Feed([(wo_i, wo)], sems)
    c = place[2]
    rows, width = mid.shape
    half = width // 2
    mine = pl.ds(pl.multiple_of(c * half, half), half)
    other = pl.ds(pl.multiple_of((1 - c) * half, half), half)
    hat, scale = norm_parts(mid[...])
    up = sgrad[...]
    vec[...] = jnp.zeros_like(vec)
    vec[0:1, :] = jnp.sum(up * hat, 0, keepdims=True)
    vec[1:2, :] = jnp.sum(up, 0, keepdims=True)
    g = cot[...].astype(F32)
    vec[2:3, :] = jnp.sum(g, 0, keepdims=True)
    mg = g + norm_back(up, hat, scale, sg[...])
    mg_o[...] = mg
    og = mg.astype(BF16)
    vec[3:4, :] = jnp.sum(og.astype(F32), 0, keepdims=True)
    tr_s[...] = jnp.transpose(ctx[...])
    normT_o[...] = jnp.transpose(normed[...])
    feed.need()
    cg_s[...] = nt(og, wo[...])
    keep_o[1] = nn(tr_s[mine, :], og).astype(BF16)
    send_o[1] = nn(tr_s[other, :], og).astype(BF16)
    for j in range(HEADS // 2):
        lanes = slice(128 * j, 128 * j + 128)
        low = (cg_s[:, lanes] * dinv[:, lanes]).astype(BF16)
        low_o[:, lanes] = low
        less = -(low.astype(F32) * c0[:, lanes])
        hi = less.astype(BF16)
        hi_o[:, lanes] = hi
        lo_o[:, lanes] = pltpu.roll(less - hi.astype(F32), 64, 1).astype(BF16)

    col_s[...] = label_column(seg)
    seg_row = seg[...].astype(F32)
    lane = lax.broadcasted_iota(jnp.int32, (1, 128), 1)

    def heads(i, _):
        at = pl.ds(pl.multiple_of(i * TILE, TILE), TILE)
        same = col_s[at, :1] == seg_row
        for j in range(HEADS // 2):
            lanes = slice(128 * j, 128 * j + 128)
            flanes = slice(128 * (j // 2), 128 * (j // 2) + 128)
            res = []
            for h in range(2):
                fm = lane_mask(2 * (j % 2) + h)
                wT = jnp.where(same, nt(f[1, at, flanes] * fm, f[0, :, flanes]), 0.0).astype(BF16)
                res.append(nn(wT, low_o[:, lanes]))
            gv_o[at, lanes] = jnp.where(lane < HD, res[0], res[1]).astype(BF16)
        return 0

    lax.fori_loop(0, rows // TILE, heads, 0)
    vec[6:7, :] = jnp.sum(gv_o[...].astype(F32), 0, keepdims=True)
    keep_o[0] = nn(normT_o[mine, :], gv_o[...]).astype(BF16)
    send_o[0] = nn(normT_o[other, :], gv_o[...]).astype(BF16)


def value_bwd(place, sgrad, mid, sg, cot, ctx, seg, dinv, c0, f, normed, wo):
    rows, width = mid.shape
    sd, v = jax.ShapeDtypeStruct, pltpu.VMEM
    ins = (place, sgrad, mid, sg, cot, ctx, seg, dinv, c0, f, normed, wo)
    outs = (
        sd((2, width // 2, width), BF16),
        sd((2, width // 2, width), BF16),
        sd((rows, width), BF16),
        sd((rows, width), BF16),
        sd((rows, width), BF16),
        sd((rows, width), BF16),
        sd((rows, width), F32),
        sd((width, rows), BF16),
        sd((16, width), F32),
    )
    scratch = [v((width, width), BF16), v((rows, 128), F32), v((width, rows), BF16), v((rows, width), F32)]
    return call(value_bwd_kernel, "value_bwd", ins, outs, scratch, 16, 1, smem=1, far=(11,),
                flops=8_000_000_000, moved=8_000_000)


def key_bwd_kernel(place, seg, low, hi, lo, vals, f, s, rot, proj, normT,
                   send_o, keep_o, grads_o, vec, col_s, de_s, sems):
    c = place[2]
    rows, width = low.shape
    half = width // 2
    mine = pl.ds(pl.multiple_of(c * half, half), half)
    other = pl.ds(pl.multiple_of((1 - c) * half, half), half)
    col_s[...] = label_column(seg)
    seg_row = seg[...].astype(F32)
    ones = jnp.ones((rows, 128), BF16)
    lane = lax.broadcasted_iota(jnp.int32, (1, 128), 1)

    def heads(i, _):
        at = pl.ds(pl.multiple_of(i * TILE, TILE), TILE)
        same = col_s[at, :1] == seg_row
        for j in range(HEADS // 2):
            gr = j // 2
            lanes = slice(128 * j, 128 * j + 128)
            flanes = slice(128 * gr, 128 * gr + 128)
            v_all = jnp.concatenate([vals[:, lanes], ones], 1)
            v_at = jnp.concatenate([vals[at, lanes], ones[:TILE]], 1)
            qf_all, kf_all = f[0, :, flanes], f[1, :, flanes]
            dq, dk = None, None
            for h in range(2):
                fm = lane_mask(2 * (j % 2) + h).astype(F32)
                own = jnp.where(lane // HD == h, 1.0, 0.0).astype(BF16)
                rest = 1.0 - own

                def pair(span):
                    return jnp.concatenate([low[span, lanes] * own, hi[span, lanes] * own + lo[span, lanes] * rest], 1)

                dwT = jnp.where(same, nt(v_at, pair(slice(None))), 0.0).astype(BF16)
                gk = nn(dwT, qf_all) * fm
                dk = gk if dk is None else dk + gk
                dw = jnp.where(same, nt(pair(at), v_all), 0.0).astype(BF16)
                gq = nn(dw, kf_all) * fm
                dq = gq if dq is None else dq + gq
            if j % 2 == 0:
                de_s[0, at, flanes] = dq
                de_s[1, at, flanes] = dk
            else:
                de_s[0, at, flanes] = (de_s[0, at, flanes] + dq) * f[0, at, flanes].astype(F32)
                de_s[1, at, flanes] = (de_s[1, at, flanes] + dk) * f[1, at, flanes].astype(F32)
        return 0

    lax.fori_loop(0, rows // TILE, heads, 0)
    p_wide, blocks = block_projection(proj)
    p_hi, p_lo = split(p_wide)

    def back(i, _):
        at = pl.ds(pl.multiple_of(i * TILE, TILE), TILE)
        cos, sin_a, sin_b = rot[at, 0:128], rot[at, 128:256], rot[at, 256:384]
        for which in range(2):
            for gr in range(width // 256):
                d_hi, d_lo = split(de_s[which, at, 128 * gr:128 * gr + 128])
                s_at = s[which, at, 256 * gr:256 * gr + 256]
                ds = nt(d_hi, p_hi) + nt(d_lo, p_hi) + nt(d_hi, p_lo) - s_at * (nt(d_hi, blocks) + nt(d_lo, blocks))
                for k in range(2):
                    du = turn_back(ds[:, 128 * k:128 * k + 128], cos, sin_a, sin_b)
                    lanes = slice(256 * gr + 128 * k, 256 * gr + 128 * k + 128)
                    grads_o[which, at, lanes] = du.astype(BF16)
        return 0

    lax.fori_loop(0, rows // TILE, back, 0)
    vec[...] = jnp.zeros_like(vec)
    for which in range(2):
        vec[4 + which:5 + which, :] = jnp.sum(grads_o[which].astype(F32), 0, keepdims=True)
        keep_o[which] = nn(normT[mine, :], grads_o[which]).astype(BF16)
        send_o[which] = nn(normT[other, :], grads_o[which]).astype(BF16)


def key_bwd(place, seg, low, hi, lo, vals, f, s, rot, proj, normT):
    rows, width = low.shape
    sd, v = jax.ShapeDtypeStruct, pltpu.VMEM
    outs = (
        sd((2, width // 2, width), BF16),
        sd((2, width // 2, width), BF16),
        sd((2, rows, width), BF16),
        sd((16, width), F32),
    )
    scratch = [v((rows, 128), F32), v((2, rows, HEADS * FEAT), F32)]
    return call(key_bwd_kernel, "key_bwd", (place, seg, low, hi, lo, vals, f, s, rot, proj, normT), outs, scratch, 16, 1,
                smem=1, flops=16_000_000_000, moved=8_000_000)


def token_bwd_kernel(grads, gv, mg, fg, tok, wq_i, wk_i, wv_i, gtok_o, vec, wq, wk, wv, sems):
    feed = Feed([(wv_i, wv), (wq_i, wq), (wk_i, wk)], sems)
    hat, scale = norm_parts(tok[...].astype(F32))
    feed.need(0)
    ng = nt(gv[...], wv[...])
    feed.need()
    ng = ng + nt(grads[0], wq[...]) + nt(grads[1], wk[...])
    vec[...] = jnp.zeros_like(vec)
    vec[7:8, :] = jnp.sum(ng * hat, 0, keepdims=True)
    vec[8:9, :] = jnp.sum(ng, 0, keepdims=True)
    gtok_o[...] = (mg[...] + norm_back(ng, hat, scale, fg[...])).astype(BF16)


def token_bwd(grads, gv, mg, fg, tok, wq, wk, wv):
    rows, width = tok.shape
    sd, v = jax.ShapeDtypeStruct, pltpu.VMEM
    outs = (sd((rows, width), BF16), sd((16, width), F32))
    return call(token_bwd_kernel, "token_bwd", (grads, gv, mg, fg, tok, wq, wk, wv), outs,
                [v((width, width), BF16)] * 3, 16, 3, far=(5, 6, 7), flops=1_800_000_000, moved=8_000_000)


def add_low(*parts):
    total = parts[0].astype(F32)
    for part in parts[1:]:
        total = total + part.astype(F32)
    return total.astype(BF16)


def ordered(first, then):
    return lax.optimization_barrier((first, then))[1]


class Links:
    def __init__(self):
        self.dp, self.ring = lax.axis_size("dp"), lax.axis_size("tensor")
        self.at = lax.axis_index("dp")
        self.z = lax.axis_index("tensor")
        self.bits = [1 << n for n in range(1, self.dp.bit_length() - 1)]

    def side(self, bit):
        return (self.at // bit) % 2

    def swap(self, v, bit):
        return lax.ppermute(v, "dp", [(i, i ^ bit) for i in range(self.dp)])

    def shift(self, v, by=1):
        return lax.ppermute(v, "tensor", [(i, (i + by) % self.ring) for i in range(self.ring)])

    def halve(self, v, bit):
        rows = v.shape[-2] // 2
        send = lax.dynamic_slice_in_dim(v, (1 - self.side(bit)) * rows, rows, v.ndim - 2)
        keep = lax.dynamic_slice_in_dim(v, self.side(bit) * rows, rows, v.ndim - 2)
        return add_low(keep, self.swap(send, bit))

    def join(self, v, bit):
        got = self.swap(v, bit)
        low = self.side(bit) == 0
        return jnp.concatenate([jnp.where(low, v, got), jnp.where(low, got, v)], v.ndim - 2)


def sum_halves(links, a, b, bits):
    for up, down in bits:
        a, b = links.halve(a, up), links.halve(b, down)
    return a, b


def sum_ring(links, ab):
    def piece(n):
        return lax.dynamic_index_in_dim(ab, (links.z + n) % links.ring, 0, keepdims=False)

    return add_low(piece(0), *[links.shift(piece(n), n) for n in range(1, links.ring)])


def spread_rows(links, v, lead, upwards):
    n = links.dp.bit_length() - 1
    rows, width = v.shape[-2:]
    v = v.reshape((2,) * n + lead + (rows, width))
    axes = list(range(n))[::-1]
    order = [axes[0]] + (axes[1:] if upwards else axes[1:][::-1])
    perm = [n + i for i in range(len(lead))] + order + [n + len(lead), n + len(lead) + 1]
    return v.transpose(perm).reshape(lead + (rows << n, width))


def gather_pair(links, total):
    width = total.shape[-1]
    whole = lax.all_gather(total, ("dp", "tensor"), axis=0)
    whole = whole.reshape(links.dp, links.ring, 2, -1, width).transpose(0, 2, 1, 3, 4).reshape(links.dp, 2, -1, width)
    return (spread_rows(links, whole[:, 0], (), True).astype(F32), spread_rows(links, whole[:, 1], (), False).astype(F32))


def body(tokens, cotangent, segment, projection, first_gain, first_bias, w_query, w_key, w_value, w_out,
         b_query, b_key, b_value, b_out, second_gain, second_bias, w_up, b_up, w_down, b_down):
    links = Links()
    rows, width = tokens.shape
    pairs = list(zip(links.bits, links.bits[::-1]))
    low_bit, top_bit = links.bits[0], links.bits[-1]
    core, x, y = links.side(1), links.side(low_bit), links.side(top_bit)
    place = jnp.stack([x, y, core]).astype(jnp.int32)
    quarter = width // 4

    def line(v):
        return v.reshape(1, -1)

    bias_parts, left = [], b_up
    for _ in range(3):
        part = lax.reduce_precision(left, 8, 7)
        bias_parts.append(part.astype(BF16))
        left = left - part
    share = jnp.concatenate([
        lax.dynamic_slice_in_dim(w_up, (2 * x + core) * quarter, quarter, 0),
        lax.dynamic_slice_in_dim(w_down, (2 * y + core) * quarter, quarter, 0),
        jnp.stack(bias_parts + [jnp.zeros_like(bias_parts[0])] * 13),
    ])
    share = links.shift(share)
    table = jnp.asarray(rotary_table(256))
    normed, s, f, vals, c0, ctx, dinv, mid, second, rot = attn_fwd(
        tokens, segment, table, projection, line(first_gain), line(first_bias), w_query, w_key, w_value, w_out,
        line(b_query), line(b_key), line(b_value), line(b_out), line(second_gain), line(second_bias))

    def arrive(share):
        own_x = links.swap(share[:quarter], low_bit)
        own_y = links.swap(share[quarter:2 * quarter], top_bit)
        return share, own_x, own_y, links.swap(share, 1), links.swap(own_x, 1), links.swap(own_y, 1)

    share = ordered(second, share)
    parts = arrive(share)
    sums, slopes = [], []
    out, sgrad, send, keep, slope = ffn(True, False, place, second, cotangent, line(b_up), mid, line(b_down), w_up, w_down)
    sums.append(add_low(keep, links.swap(send, 1)))
    slopes.append(slope)
    for n in range(1, links.ring):
        last = n == links.ring - 1
        if not last:
            share = ordered(out, links.shift(share))
            later = arrive(share)
        out, sgrad, send, keep, slope = ffn(False, last, place, second, cotangent, *parts, out, sgrad)
        sums.append(add_low(keep, links.swap(send, 1)))
        slopes.append(slope)
        parts = later

    ring = links.shift(sums[1])
    send_v, keep_v, low, hi, lo, gv, mg, normT, vec_v = value_bwd(
        place, sgrad, mid, line(second_gain), cotangent, ctx, segment, dinv, c0, f, normed, w_out)
    ring = ordered(gv, ring)
    ring = links.shift(add_low(ring, sums[2])) if links.ring > 2 else ring
    ov = add_low(keep_v, links.swap(send_v, 1))
    ov_sent = [links.halve(ov[0], pairs[0][0]), links.halve(ov[1], pairs[0][1])]
    low = ordered(ov, low)
    send_k, keep_k, grads, vec_k = key_bwd(place, segment, low, hi, lo, vals, f, s, rot, projection, normT)
    ov_sent, ring = ordered(grads, (ov_sent, ring))
    qk = add_low(keep_k, links.swap(send_k, 1))
    gtok, vec_t = token_bwd(grads, gv, mg, line(first_gain), tokens, w_query, w_key, w_value)

    qk_a, qk_b = sum_halves(links, qk[0], qk[1], pairs)
    ov_a, ov_b = sum_halves(links, *ov_sent, pairs[1:])
    for n in list(range(3, links.ring)) + [0]:
        ring = add_low(ring, sums[n])
        if n:
            ring = links.shift(ring)
    ff_a, ff_b = sum_halves(links, ring[0], ring[1], pairs)

    def by_ring(a, b):
        return sum_ring(links, jnp.stack([a.reshape(links.ring, -1, width), b.reshape(links.ring, -1, width)], 1))

    grad_w_value, grad_w_out = gather_pair(links, by_ring(ov_a, ov_b))
    grad_w_query, grad_w_key = gather_pair(links, by_ring(qk_a, qk_b))

    for up, down in pairs[::-1]:
        ff_a, ff_b = links.join(ff_a, up), links.join(ff_b, down)
    grad_w_up = links.join(ff_a, 1).astype(F32)
    steps = width // FFN_STEP
    other_b = links.swap(ff_b, 1)
    both = [v.reshape(steps, FFN_STEP // 2, width) for v in (jnp.where(core == 0, ff_b, other_b), jnp.where(core == 0, other_b, ff_b))]
    grad_w_down = jnp.stack(both, 1).reshape(width, width).astype(F32)

    slope_all = jnp.zeros((links.ring, width), F32)
    for n, slope in enumerate(slopes):
        slope_all = lax.dynamic_update_slice_in_dim(slope_all, slope, (links.z - n) % links.ring, 0)
    vec = lax.psum(jnp.concatenate([vec_v + vec_k + vec_t, slope_all]), ("dp", "tensor"))
    grad_b_up = lax.dynamic_index_in_dim(vec, 16 + links.z, 0, keepdims=False)
    return (
        out, gtok, vec[7], vec[8], grad_w_query, grad_w_key, grad_w_value, grad_w_out,
        vec[4], vec[5], vec[6], vec[3], vec[0], vec[1], grad_w_up, grad_b_up, grad_w_down, vec[2],
    )


def solution(mesh):
    rows = P(("dp", "tensor"), None)
    whole = P()
    return jax.shard_map(
        body,
        mesh=mesh,
        in_specs=(rows,) * 3 + (whole,) * 13 + (P(None, "tensor"), P("tensor"), P("tensor", None), whole),
        out_specs=(rows,) * 2 + (whole,) * 12 + (P(None, "tensor"), P("tensor"), P("tensor", None), whole),
        check_vma=False,
    )
```

```python
from functools import partial
import math

import jax
import jax.numpy as jnp
import ml_dtypes
import numpy as np
from jax import lax
from jax.experimental import pallas as pl
from jax.experimental.pallas import tpu as pltpu
from jax.sharding import PartitionSpec as P

HEADS = 12
HD = 64
FEAT = 32
EPS = 1e-05
F32 = jnp.float32
BF16 = jnp.bfloat16
ANY = pl.BlockSpec(memory_space=pltpu.HBM)
VM = pl.BlockSpec(memory_space=pltpu.VMEM)
SMEM = pl.BlockSpec(memory_space=pltpu.SMEM)
SCALE = HD ** -0.25


def nn(a, b):
    return lax.dot_general(a, b, (((1,), (0,)), ((), ())), preferred_element_type=F32)


def nt(a, b):
    return lax.dot_general(a, b, (((1,), (1,)), ((), ())), preferred_element_type=F32)


def split(v):
    high = v.astype(BF16)
    return high, (v - high.astype(F32)).astype(BF16)


def rotary_table(length):
    half = HD // 2
    rate = np.exp(np.arange(half) * (-2.0 * math.log(10000.0) / HD))
    angle = np.arange(length)[:, None] * rate[None, :]
    lane = np.arange(128)
    cos = np.tile(np.cos(angle), (1, 4)) * SCALE
    sin = np.tile(np.sin(angle), (1, 4)) * SCALE
    first = (lane % HD < half)[None, :]
    table = np.concatenate([cos, -sin * first, sin * ~first], 1).astype(np.float32)
    parts = []
    for _ in range(3):
        part = table.astype(ml_dtypes.bfloat16)
        parts.append(part)
        table = table - part.astype(np.float32)
    return np.stack(parts)


def lane_mask(head_in_group):
    lane = lax.broadcasted_iota(jnp.int32, (1, 128), 1)
    return jnp.where(lane // FEAT == head_in_group, 1.0, 0.0).astype(BF16)


def norm_parts(v):
    centred = v - jnp.mean(v, -1, keepdims=True)
    scale = lax.rsqrt(jnp.mean(centred * centred, -1, keepdims=True) + EPS)
    return centred * scale, scale


def norm_back(grad, hat, scale, gain):
    hat_grad = grad * gain
    return scale * (
        hat_grad
        - jnp.mean(hat_grad, -1, keepdims=True)
        - hat * jnp.mean(hat_grad * hat, -1, keepdims=True)
    )


def label_column(seg):
    rows = seg.shape[1]
    return jnp.transpose(jnp.broadcast_to(seg[...].astype(F32), (128, rows)))


def block_projection(proj):
    tall = jnp.concatenate([proj[...]] * 4, axis=0)
    wide = jnp.concatenate([tall] * 4, axis=1)
    group = lax.broadcasted_iota(jnp.int32, (256, 128), 0) // HD
    feat = lax.broadcasted_iota(jnp.int32, (256, 128), 1) // FEAT
    return jnp.where(group == feat, wide, 0.0), jnp.where(group == feat, 1.0, 0.0).astype(BF16)


def turn(u, cos, sin_a, sin_b):
    return u * cos + pltpu.roll(u, 96, 1) * sin_a + pltpu.roll(u, 32, 1) * sin_b


def turn_back(u, cos, sin_a, sin_b):
    return u * cos - pltpu.roll(u, 96, 1) * sin_a - pltpu.roll(u, 32, 1) * sin_b


class Feed:
    def __init__(self, pairs, sems):
        self.sems, self.copies, self.left = sems, [], []
        for src, dst in pairs:
            self.add(src, dst)

    def add(self, src, dst):
        copy = pltpu.make_async_copy(src, dst, self.sems.at[len(self.copies)])
        copy.start()
        self.left.append(len(self.copies))
        self.copies.append(copy)

    def need(self, *which):
        for n in which or list(self.left):
            if n in self.left:
                self.copies[n].wait()
                self.left.remove(n)


def call(kernel, name, ins, outs, scratch, limit, sems, flops, smem=0, far=(), far_out=(), alias=None):
    return pl.pallas_call(
        kernel,
        out_shape=outs,
        in_specs=[SMEM if n < smem else ANY if n in far else VM for n in range(len(ins))],
        out_specs=[ANY if n in far_out else VM for n in range(len(outs))],
        scratch_shapes=list(scratch) + ([pltpu.SemaphoreType.DMA((sems,))] if sems else []),
        input_output_aliases=alias or {},
        compiler_params=pltpu.CompilerParams(vmem_limit_bytes=limit << 20),
        cost_estimate=pl.CostEstimate(flops=flops, bytes_accessed=1000, transcendentals=0),
        name=name,
    )(*ins)


TILE = 256


def attn_fwd_kernel(seg, fg, fb, bq, bk, bv, bo, sg, sb, proj, tok_i, wv_i, wq_i, tab_i, wk_i, wo_i,
                    normed_i, s_i, f_i, v_i, rot_i, c0_o, ctx_o, dinv_o, mid_o, sec_o,
                    col_s, normed_o, s_o, f_o, v_o, rot_o, tok, wv, wq, tab, wk, wo, sems):
    feed = Feed([(tab_i, tab), (tok_i, tok), (wv_i, wv), (wq_i, wq), (wk_i, wk), (wo_i, wo)], sems)
    rows, width = tok.shape
    col_s[...] = label_column(seg)
    seg_row = seg[...].astype(F32)
    less = jnp.where(seg_row < col_s[:, :1], 1.0, 0.0)
    start = jnp.sum(less, axis=1, keepdims=True)
    place = lax.broadcasted_iota(jnp.int32, (rows, 1), 0).astype(F32) - start
    length = tab.shape[1]
    ladder = lax.broadcasted_iota(jnp.int32, (rows, length), 1).astype(F32)
    one_hot = jnp.where(ladder == place, 1.0, 0.0).astype(BF16)
    p_wide, blocks = block_projection(proj)
    p_hi, p_lo = split(p_wide)
    halves = blocks * 0.5
    feed.need(0)
    rot_o[...] = nn(one_hot, tab[0]) + nn(one_hot, tab[1]) + nn(one_hot, tab[2])
    feed.need(1, 2, 3, 4)

    def first(i, _):
        at = pl.ds(pl.multiple_of(i * TILE, TILE), TILE)
        x = tok[at, :].astype(F32)
        hat, _scale = norm_parts(x)
        normed = (hat * fg[...] + fb[...]).astype(BF16)
        normed_o[at, :] = normed
        v_o[at, :] = nn(normed, wv[...]).astype(BF16)
        cos, sin_a, sin_b = rot_o[at, 0:128], rot_o[at, 128:256], rot_o[at, 256:384]
        for which, (w, b) in enumerate(((wq, bq), (wk, bk))):
            u = nn(normed, w[...]) + b[...]
            for j in range(width // 128):
                lanes = slice(128 * j, 128 * j + 128)
                s_o[which, at, lanes] = turn(u[:, lanes], cos, sin_a, sin_b)
            for g in range(width // 256):
                s = s_o[which, at, 256 * g:256 * g + 256]
                s_hi, s_lo = split(s)
                q_hi, q_lo = split(s * s)
                e = nn(s_hi, p_hi) + nn(s_lo, p_hi) + nn(s_hi, p_lo) - nn(q_hi, halves) - nn(q_lo, halves)
                f_o[which, at, 128 * g:128 * g + 128] = (jnp.exp(e) * FEAT ** -0.5).astype(BF16)
        return 0

    lax.fori_loop(0, rows // TILE, first, 0)
    feed.need()
    for held, kept in ((normed_o, normed_i), (s_o, s_i), (f_o, f_i), (v_o, v_i), (rot_o, rot_i)):
        feed.add(held, kept)

    ones = jnp.ones((rows, 128), BF16)
    even = lax.broadcasted_iota(jnp.int32, (1, 128), 1) < HD

    def second(i, _):
        at = pl.ds(pl.multiple_of(i * TILE, TILE), TILE)
        same = col_s[at, :1] == seg_row
        for j in range(HEADS // 2):
            g = j // 2
            vals = jnp.concatenate([v_o[:, 128 * j:128 * j + 128], ones], 1)
            qf = f_o[0, at, 128 * g:128 * g + 128]
            kf = f_o[1, :, 128 * g:128 * g + 128]
            res = []
            for h in range(2):
                scores = nt(qf * lane_mask(2 * (j % 2) + h), kf)
                weights = jnp.where(same, scores, 0.0).astype(BF16)
                res.append(nn(weights, vals))
            num = jnp.where(even, res[0][:, :128], res[1][:, :128])
            inv = 1.0 / jnp.where(even, res[0][:, 128:], res[1][:, 128:])
            lanes = slice(128 * j, 128 * j + 128)
            ctx = num * inv
            dinv_o[at, lanes] = inv
            c0_o[at, lanes] = ctx
            ctx_o[at, lanes] = (ctx + bv[:, lanes]).astype(BF16)
        middle = tok[at, :].astype(F32) + nn(ctx_o[at, :], wo[...]) + bo[...]
        mid_o[at, :] = middle
        hat, _scale = norm_parts(middle)
        sec_o[at, :] = (hat * sg[...] + sb[...]).astype(BF16)
        return 0

    lax.fori_loop(0, rows // TILE, second, 0)
    feed.need()


def attn_fwd(tok, seg, tab, proj, fg, fb, wq, wk, wv, wo, bq, bk, bv, bo, sg, sb):
    rows, width = tok.shape
    sd, v = jax.ShapeDtypeStruct, pltpu.VMEM
    outs = (
        sd((rows, width), BF16),
        sd((2, rows, width), F32),
        sd((2, rows, HEADS * FEAT), BF16),
        sd((rows, width), BF16),
        sd((rows, 384), F32),
        sd((rows, width), F32),
        sd((rows, width), BF16),
        sd((rows, width), F32),
        sd((rows, width), F32),
        sd((rows, width), BF16),
    )
    near = (seg, fg, fb, bq, bk, bv, bo, sg, sb, proj)
    far = (tok, wv, wq, tab, wk, wo)
    scratch = [v((rows, 128), F32)] + [v(a.shape, a.dtype) for a in outs[:5] + far]
    return call(attn_fwd_kernel, "attn_fwd", near + far, outs, scratch, 52, len(far) + 5, 5520000000,
                far=range(len(near), len(near) + len(far)), far_out=range(5))


FFN_STEP = 256


def ffn_kernel(first, last, place, sec, cot, *refs):
    n_in = 5 if first else 8
    ins, refs = refs[:n_in], refs[n_in:]
    out_o, sg_o, send_o, keep_o, gb_o, wu, wd, secT, hidT, acc, sems = refs
    x, y, c = place[0], place[1], place[2]
    rows, width = sec.shape
    quarter, half = width // 4, width // 2

    def part(a, core):
        return pl.ds(pl.multiple_of((2 * a + core) * quarter, quarter), quarter)

    if first:
        bu, oacc, bd, wu_i, wd_i = ins
        feed = Feed([(wu_i, wu), (wd_i, wd)], sems)
        bias = bu[...]
        early = (0,)
    else:
        own, own_x, own_y, far, far_x, far_y, oacc, sacc = ins
        up, down = pl.ds(0, quarter), pl.ds(quarter, quarter)
        feed = Feed([
            (own.at[up], wu.at[part(x, c)]), (own_x, wu.at[part(1 - x, c)]),
            (far.at[up], wu.at[part(x, 1 - c)]), (far_x, wu.at[part(1 - x, 1 - c)]),
            (own.at[down], wd.at[part(y, c)]), (own_y, wd.at[part(1 - y, c)]),
            (far.at[down], wd.at[part(y, 1 - c)]), (far_y, wd.at[part(1 - y, 1 - c)]),
        ], sems)
        tail = own[2 * quarter:2 * quarter + 16, :].astype(F32)
        bias = tail[0:1, :] + tail[1:2, :] + tail[2:3, :]
        early = (0, 1, 2, 3)
    mine = pl.ds(pl.multiple_of(c * half, half), half)
    other = pl.ds(pl.multiple_of((1 - c) * half, half), half)
    secT[...] = jnp.transpose(sec[...])
    feed.need(*early)
    cut = FFN_STEP // 2
    for n, at in enumerate(range(0, width, FFN_STEP)):
        cs = slice(at, at + FFN_STEP)
        inner = nn(sec[...], wu[:, cs]) + bias[:, cs]
        cdf = 0.5 + 0.5 * lax.erf(inner * math.sqrt(0.5))
        slope = cdf + inner * (jnp.exp(-0.5 * inner * inner) * (1.0 / math.sqrt(2.0 * math.pi)))
        hidden = (inner * cdf).astype(BF16)
        feed.need()
        grad = (nt(cot[...], wd[cs, :]) * slope).astype(BF16)
        gb_o[:, cs] = jnp.sum(grad.astype(F32), 0, keepdims=True)
        more_out = nn(hidden, wd[cs, :])
        more_sg = nt(grad, wu[:, cs])
        if n == 0:
            acc[...] = oacc[...] + more_out + (bd[...] if first else 0.0)
            sg_o[...] = more_sg if first else sacc[...] + more_sg
        else:
            acc[...] += more_out
            sg_o[...] += more_sg
        hidT[...] = jnp.transpose(hidden)
        piece = slice(n * cut, n * cut + cut)
        keep_o[1, piece, :] = nn(hidT[pl.ds(pl.multiple_of(c * cut, cut), cut), :], cot[...]).astype(BF16)
        send_o[1, piece, :] = nn(hidT[pl.ds(pl.multiple_of((1 - c) * cut, cut), cut), :], cot[...]).astype(BF16)
        keep_o[0, :, cs] = nn(secT[mine, :], grad).astype(BF16)
        send_o[0, :, cs] = nn(secT[other, :], grad).astype(BF16)
    out_o[...] = acc[...].astype(out_o.dtype)


def ffn(first, last, place, sec, cot, *ins):
    rows, width = sec.shape
    sd, v = jax.ShapeDtypeStruct, pltpu.VMEM
    outs = (
        sd((rows, width), BF16 if last else F32),
        sd((rows, width), F32),
        sd((2, width // 2, width), BF16),
        sd((2, width // 2, width), BF16),
        sd((1, width), F32),
    )
    scratch = [v((width, width), BF16), v((width, width), BF16), v((width, rows), BF16), v((FFN_STEP, rows), BF16),
               v((rows, width), F32)]
    return call(partial(ffn_kernel, first, last), "ffn", (place, sec, cot) + ins, outs, scratch, 14, 8, 2760000000, smem=1,
                far=(6, 7) if first else (), alias=None if first else {10: 1})


def out_bwd_kernel(place, sgrad, mid, sg, cot, ctx, dinv, c0, wo_i,
                   send_o, keep_o, low_o, hi_o, lo_o, mg_o, vec, wo, tr_s, cg_s, sems):
    feed = Feed([(wo_i, wo)], sems)
    c = place[2]
    rows, width = mid.shape
    half = width // 2
    tr_s[...] = jnp.transpose(ctx[...])
    hat, scale = norm_parts(mid[...])
    up = sgrad[...]
    vec[...] = jnp.zeros_like(vec)
    vec[0:1, :] = jnp.sum(up * hat, 0, keepdims=True)
    vec[1:2, :] = jnp.sum(up, 0, keepdims=True)
    g = cot[...].astype(F32)
    vec[2:3, :] = jnp.sum(g, 0, keepdims=True)
    mg = g + norm_back(up, hat, scale, sg[...])
    mg_o[...] = mg
    og = mg.astype(BF16)
    vec[3:4, :] = jnp.sum(og.astype(F32), 0, keepdims=True)
    feed.need()
    cg_s[...] = nt(og, wo[...])
    keep_o[...] = nn(tr_s[pl.ds(pl.multiple_of(c * half, half), half), :], og).astype(BF16)
    send_o[...] = nn(tr_s[pl.ds(pl.multiple_of((1 - c) * half, half), half), :], og).astype(BF16)
    for j in range(HEADS // 2):
        lanes = slice(128 * j, 128 * j + 128)
        low = (cg_s[:, lanes] * dinv[:, lanes]).astype(BF16)
        low_o[:, lanes] = low
        less = -(low.astype(F32) * c0[:, lanes])
        hi = less.astype(BF16)
        hi_o[:, lanes] = hi
        lo_o[:, lanes] = pltpu.roll(less - hi.astype(F32), 64, 1).astype(BF16)


def out_bwd(place, sgrad, mid, sg, cot, ctx, dinv, c0, wo):
    rows, width = mid.shape
    sd, v = jax.ShapeDtypeStruct, pltpu.VMEM
    outs = (
        sd((width // 2, width), BF16),
        sd((width // 2, width), BF16),
        sd((rows, width), BF16),
        sd((rows, width), BF16),
        sd((rows, width), BF16),
        sd((rows, width), F32),
        sd((16, width), F32),
    )
    scratch = [v((width, width), BF16), v((width, rows), BF16), v((rows, width), F32)]
    return call(out_bwd_kernel, "out_bwd", (place, sgrad, mid, sg, cot, ctx, dinv, c0, wo), outs, scratch, 12, 1, 2300000000, smem=1, far=(8,))


def value_bwd_kernel(place, seg, low, f, normed, send_o, keep_o, gv_o, normT_o, vec, col_s):
    c = place[2]
    rows, width = low.shape
    half = width // 2
    col_s[...] = label_column(seg)
    seg_row = seg[...].astype(F32)
    lane = lax.broadcasted_iota(jnp.int32, (1, 128), 1)

    def heads(i, _):
        at = pl.ds(pl.multiple_of(i * TILE, TILE), TILE)
        same = col_s[at, :1] == seg_row
        for j in range(HEADS // 2):
            lanes = slice(128 * j, 128 * j + 128)
            flanes = slice(128 * (j // 2), 128 * (j // 2) + 128)
            res = []
            for h in range(2):
                fm = lane_mask(2 * (j % 2) + h)
                wT = jnp.where(same, nt(f[1, at, flanes] * fm, f[0, :, flanes]), 0.0).astype(BF16)
                res.append(nn(wT, low[:, lanes]))
            gv_o[at, lanes] = jnp.where(lane < HD, res[0], res[1]).astype(BF16)
        return 0

    lax.fori_loop(0, rows // TILE, heads, 0)
    normT_o[...] = jnp.transpose(normed[...])
    vec[...] = jnp.zeros_like(vec)
    vec[6:7, :] = jnp.sum(gv_o[...].astype(F32), 0, keepdims=True)
    keep_o[...] = nn(normT_o[pl.ds(pl.multiple_of(c * half, half), half), :], gv_o[...]).astype(BF16)
    send_o[...] = nn(normT_o[pl.ds(pl.multiple_of((1 - c) * half, half), half), :], gv_o[...]).astype(BF16)


def value_bwd(place, seg, low, f, normed):
    rows, width = low.shape
    sd, v = jax.ShapeDtypeStruct, pltpu.VMEM
    outs = (
        sd((width // 2, width), BF16),
        sd((width // 2, width), BF16),
        sd((rows, width), BF16),
        sd((width, rows), BF16),
        sd((16, width), F32),
    )
    return call(value_bwd_kernel, "value_bwd", (place, seg, low, f, normed), outs, [v((rows, 128), F32)], 12, 0, 3680000000, smem=1)


def score_bwd_kernel(seg, low, hi, lo, vals, f, de_o, col_s):
    rows, width = low.shape
    col_s[...] = label_column(seg)
    seg_row = seg[...].astype(F32)
    ones = jnp.ones((rows, 128), BF16)
    lane = lax.broadcasted_iota(jnp.int32, (1, 128), 1)

    def heads(i, _):
        at = pl.ds(pl.multiple_of(i * TILE, TILE), TILE)
        same = col_s[at, :1] == seg_row
        for j in range(HEADS // 2):
            gr = j // 2
            lanes = slice(128 * j, 128 * j + 128)
            flanes = slice(128 * gr, 128 * gr + 128)
            v_all = jnp.concatenate([vals[:, lanes], ones], 1)
            v_at = jnp.concatenate([vals[at, lanes], ones[:TILE]], 1)
            qf_all, kf_all = f[0, :, flanes], f[1, :, flanes]
            dq, dk = None, None
            for h in range(2):
                fm = lane_mask(2 * (j % 2) + h).astype(F32)
                own = jnp.where(lane // HD == h, 1.0, 0.0).astype(BF16)
                rest = 1.0 - own

                def pair(span):
                    return jnp.concatenate([low[span, lanes] * own, hi[span, lanes] * own + lo[span, lanes] * rest], 1)

                dwT = jnp.where(same, nt(v_at, pair(slice(None))), 0.0).astype(BF16)
                gk = nn(dwT, qf_all) * fm
                dk = gk if dk is None else dk + gk
                dw = jnp.where(same, nt(pair(at), v_all), 0.0).astype(BF16)
                gq = nn(dw, kf_all) * fm
                dq = gq if dq is None else dq + gq
            if j % 2 == 0:
                de_o[0, at, flanes] = dq
                de_o[1, at, flanes] = dk
            else:
                de_o[0, at, flanes] = (de_o[0, at, flanes] + dq) * f[0, at, flanes].astype(F32)
                de_o[1, at, flanes] = (de_o[1, at, flanes] + dk) * f[1, at, flanes].astype(F32)
        return 0

    lax.fori_loop(0, rows // TILE, heads, 0)


def score_bwd(seg, low, hi, lo, vals, f):
    rows = low.shape[0]
    outs = (jax.ShapeDtypeStruct((2, rows, HEADS * FEAT), F32),)
    return call(score_bwd_kernel, "score_bwd", (seg, low, hi, lo, vals, f), outs, [pltpu.VMEM((rows, 128), F32)], 12, 0, 5520000000)[0]


def key_bwd_kernel(place, de, s, rot, proj, normT, send_o, keep_o, grads_o, vec):
    c = place[2]
    rows = s.shape[1]
    width = s.shape[2]
    half = width // 2
    p_wide, blocks = block_projection(proj)
    p_hi, p_lo = split(p_wide)

    def back(i, _):
        at = pl.ds(pl.multiple_of(i * TILE, TILE), TILE)
        cos, sin_a, sin_b = rot[at, 0:128], rot[at, 128:256], rot[at, 256:384]
        for which in range(2):
            for gr in range(width // 256):
                d_hi, d_lo = split(de[which, at, 128 * gr:128 * gr + 128])
                s_at = s[which, at, 256 * gr:256 * gr + 256]
                ds = nt(d_hi, p_hi) + nt(d_lo, p_hi) + nt(d_hi, p_lo) - s_at * (nt(d_hi, blocks) + nt(d_lo, blocks))
                for k in range(2):
                    du = turn_back(ds[:, 128 * k:128 * k + 128], cos, sin_a, sin_b)
                    lanes = slice(256 * gr + 128 * k, 256 * gr + 128 * k + 128)
                    grads_o[which, at, lanes] = du.astype(BF16)
        return 0

    lax.fori_loop(0, rows // TILE, back, 0)
    vec[...] = jnp.zeros_like(vec)
    for which in range(2):
        vec[4 + which:5 + which, :] = jnp.sum(grads_o[which].astype(F32), 0, keepdims=True)
        keep_o[which] = nn(normT[pl.ds(pl.multiple_of(c * half, half), half), :], grads_o[which]).astype(BF16)
        send_o[which] = nn(normT[pl.ds(pl.multiple_of((1 - c) * half, half), half), :], grads_o[which]).astype(BF16)


def key_bwd(place, de, s, rot, proj, normT):
    width, rows = normT.shape
    sd = jax.ShapeDtypeStruct
    outs = (
        sd((2, width // 2, width), BF16),
        sd((2, width // 2, width), BF16),
        sd((2, rows, width), BF16),
        sd((16, width), F32),
    )
    return call(key_bwd_kernel, "key_bwd", (place, de, s, rot, proj, normT), outs, [], 12, 0, 1840000000, smem=1)


def token_bwd_kernel(grads, gv, mg, fg, tok, wq_i, wk_i, wv_i, gtok_o, vec, wq, wk, wv, sems):
    feed = Feed([(wv_i, wv), (wq_i, wq), (wk_i, wk)], sems)
    hat, scale = norm_parts(tok[...].astype(F32))
    feed.need(0)
    ng = nt(gv[...], wv[...])
    feed.need()
    ng = ng + nt(grads[0], wq[...]) + nt(grads[1], wk[...])
    vec[...] = jnp.zeros_like(vec)
    vec[7:8, :] = jnp.sum(ng * hat, 0, keepdims=True)
    vec[8:9, :] = jnp.sum(ng, 0, keepdims=True)
    gtok_o[...] = (mg[...] + norm_back(ng, hat, scale, fg[...])).astype(BF16)


def token_bwd(grads, gv, mg, fg, tok, wq, wk, wv):
    rows, width = tok.shape
    sd, v = jax.ShapeDtypeStruct, pltpu.VMEM
    outs = (sd((rows, width), BF16), sd((16, width), F32))
    return call(token_bwd_kernel, "token_bwd", (grads, gv, mg, fg, tok, wq, wk, wv), outs,
                [v((width, width), BF16)] * 3, 12, 3, 1840000000, far=(5, 6, 7))


def pack_kernel(place, wu, wd, bu, out, sems):
    quarter = wu.shape[1] // 4
    x, y, c = place[0], place[1], place[2]
    feed = Feed([
        (wu.at[pl.ds(pl.multiple_of((2 * x + c) * quarter, quarter), quarter)], out.at[pl.ds(0, quarter)]),
        (wd.at[pl.ds(pl.multiple_of((2 * y + c) * quarter, quarter), quarter)], out.at[pl.ds(quarter, quarter)]),
    ], sems)
    left, parts = bu[...], []
    for _ in range(3):
        parts.append(left.astype(BF16).astype(F32))
        left = left - parts[-1]
    parts.append(jnp.zeros((13, left.shape[1]), F32))
    out[2 * quarter:2 * quarter + 16, :] = jnp.concatenate(parts, 0).astype(BF16)
    feed.need()


def pack(place, wu, wd, bu):
    width = wu.shape[1]
    outs = (jax.ShapeDtypeStruct((width // 2 + 16, width), BF16),)
    return call(pack_kernel, "pack", (place, wu, wd, bu), outs, [], 58, 2, 460000000, smem=1, far=(1, 2))[0]


def finish_kernel(woven, place, mine, got, *refs):
    n = mine.shape[0]
    outs, refs = refs[:n], refs[n:]
    held, sems = refs
    c = place[2]
    rows = mine.shape[1]
    feed = Feed([], sems)
    cut = FFN_STEP // 2
    for m in range(n):
        for side, (ref, core) in enumerate(((mine, c), (got, 1 - c))):
            held[m, side] = ref[m].astype(F32)
            if woven[m]:
                for k in range(rows // cut):
                    feed.add(held.at[m, side, pl.ds(k * cut, cut)], outs[m].at[pl.ds(pl.multiple_of(2 * k * cut + core * cut, cut), cut)])
            else:
                feed.add(held.at[m, side], outs[m].at[pl.ds(pl.multiple_of(core * rows, rows), rows)])
    feed.need()


def finish(place, mine, got, woven):
    n, rows, width = mine.shape
    outs = (jax.ShapeDtypeStruct((2 * rows, width), F32),) * n
    return call(partial(finish_kernel, woven), "finish", (place, mine, got), outs, [pltpu.VMEM((n, 2, rows, width), F32)], 20,
                sum(2 * (rows // (FFN_STEP // 2) if w else 1) for w in woven), 920000000, smem=1, far_out=range(n))


def add_low(*parts):
    total = parts[0].astype(F32)
    for part in parts[1:]:
        total = total + part.astype(F32)
    return total.astype(parts[0].dtype)


def ordered(first, then):
    return lax.optimization_barrier((first, then))[1]


class Links:
    def __init__(self):
        self.dp, self.ring = lax.axis_size("dp"), lax.axis_size("tensor")
        self.at = lax.axis_index("dp")
        self.z = lax.axis_index("tensor")
        self.bits = [1 << n for n in range(1, self.dp.bit_length() - 1)]

    def side(self, bit):
        return (self.at // bit) % 2

    def swap(self, v, bit):
        return lax.ppermute(v, "dp", [(i, i ^ bit) for i in range(self.dp)])

    def shift(self, v, by=1):
        return lax.ppermute(v, "tensor", [(i, (i + by) % self.ring) for i in range(self.ring)])

    def halve(self, v, bit):
        rows = v.shape[-2] // 2
        send = lax.dynamic_slice_in_dim(v, (1 - self.side(bit)) * rows, rows, v.ndim - 2)
        keep = lax.dynamic_slice_in_dim(v, self.side(bit) * rows, rows, v.ndim - 2)
        return add_low(keep, self.swap(send, bit))

    def join(self, v, bit):
        got = self.swap(v, bit)
        low = self.side(bit) == 0
        return jnp.concatenate([jnp.where(low, v, got), jnp.where(low, got, v)], v.ndim - 2)


def sum_halves(links, a, b, bits):
    for up, down in bits:
        a, b = links.halve(a, up), links.halve(b, down)
    return a, b


def sum_all(links, v):
    bit = 1
    while bit < links.ring:
        v = add_low(v, lax.ppermute(v, "tensor", [(i, i ^ bit) for i in range(links.ring)]))
        bit *= 2
    return v


def body(tokens, cotangent, segment, projection, first_gain, first_bias, w_query, w_key, w_value, w_out,
         b_query, b_key, b_value, b_out, second_gain, second_bias, w_up, b_up, w_down, b_down):
    links = Links()
    rows, width = tokens.shape
    pairs = list(zip(links.bits, links.bits[::-1]))
    low_bit, top_bit = links.bits[0], links.bits[-1]
    core, x, y = links.side(1), links.side(low_bit), links.side(top_bit)
    place = jnp.stack([x, y, core]).astype(jnp.int32)
    quarter = width // 4

    def line(v):
        return v.reshape(1, -1)

    share = links.shift(pack(place, w_up, w_down, line(b_up)))
    table = jnp.asarray(rotary_table(256))
    normed, s, f, vals, rot, c0, ctx, dinv, mid, second = attn_fwd(
        tokens, segment, table, projection, line(first_gain), line(first_bias), w_query, w_key, w_value, w_out,
        line(b_query), line(b_key), line(b_value), line(b_out), line(second_gain), line(second_bias))

    def swaps(share):
        return share, links.swap(share[:quarter], low_bit), links.swap(share[quarter:2 * quarter], top_bit)

    def across(parts):
        return parts + tuple(links.swap(v, 1) for v in parts)

    share = ordered(second, share)
    parts, share = swaps(share), links.shift(share)
    sums, slopes = [], []
    out, sgrad, send, keep, slope = ffn(True, False, place, second, cotangent, line(b_up), mid, line(b_down), w_up, w_down)
    sums.append((keep, links.swap(send, 1)))
    slopes.append(slope)
    for n in range(1, links.ring):
        last = n == links.ring - 1
        parts = across(ordered(out, parts))
        if not last:
            share = ordered(out, share)
            later = swaps(share)
            share = links.shift(share)
        if n == 2:
            ring = add_low(*sums[1])
            out, ring = lax.optimization_barrier((out, ring))
            ring = links.shift(ring)
        out, sgrad, send, keep, slope = ffn(False, last, place, second, cotangent, *parts, out, sgrad)
        sums.append((keep, links.swap(send, 1)))
        slopes.append(slope)
        parts = later

    def ring_step(ring, n, after):
        after, ring = lax.optimization_barrier((after, ring))
        ring = add_low(ring, *sums[n % links.ring])
        after, ring = lax.optimization_barrier((after, ring))
        return (links.shift(ring) if n < links.ring else ring), after

    ring, sgrad = ring_step(ring, 2, sgrad)
    send_o, keep_o, low, hi, lo, mg, vec_o = out_bwd(
        place, sgrad, mid, line(second_gain), cotangent, ctx, dinv, c0, w_out)
    send_v, keep_v, gv, normT, vec_v = value_bwd(place, segment, low, f, normed)
    grad_o = add_low(keep_o, links.swap(send_o, 1))
    ring, low = ring_step(ring, 3, ordered(gv, low))
    grad_v = add_low(keep_v, links.swap(send_v, 1))
    de = score_bwd(segment, ordered(grad_v, low), hi, lo, vals, f)
    for n in range(4, links.ring + 1):
        ring, de = ring_step(ring, n, de)

    some_a = links.halve(jnp.stack([ring[0], grad_v]), pairs[0][0])
    some_b = links.halve(jnp.stack([ring[1], grad_o]), pairs[0][1])
    send_k, keep_k, grads, vec_k = key_bwd(place, de, s, rot, projection, normT)
    some_a, some_b = ordered(grads, (some_a, some_b))
    qk = add_low(keep_k, links.swap(send_k, 1))
    qk_a, qk_b = links.halve(qk[0], pairs[0][0]), links.halve(qk[1], pairs[0][1])
    gtok, vec_t = token_bwd(ordered(qk, grads), gv, mg, line(first_gain), tokens, w_query, w_key, w_value)
    some_a, some_b = sum_halves(links, some_a, some_b, pairs[1:])
    ov = jnp.stack([some_a[1], some_b[1]])

    slope_all = jnp.zeros((links.ring, width), F32)
    for n, slope in enumerate(slopes):
        slope_all = lax.dynamic_update_slice_in_dim(slope_all, slope, (links.z - n) % links.ring, 0)
    vec = jnp.concatenate([vec_o + vec_v + vec_k + vec_t, slope_all])
    vec = vec + links.swap(vec, 1)
    qk_a, qk_b = ordered((vec_t, ov), (qk_a, qk_b))
    qk_a, qk_b = sum_halves(links, qk_a, qk_b, pairs[1:])
    for bit in links.bits:
        vec = vec + links.swap(vec, bit)
    ov = sum_all(links, ov)
    qk = ordered(vec, jnp.stack([qk_a, qk_b]))
    qk = sum_all(links, qk)
    vec = sum_all(links, vec)
    some_a, some_b = jnp.stack([some_a[0], ov[0]]), jnp.stack([some_b[0], ov[1]])
    qk_a, qk_b = ordered(vec, (qk[0], qk[1]))
    for up, down in pairs[::-1]:
        some_a, some_b = links.join(some_a, up), links.join(some_b, down)
        qk_a, qk_b = ordered((some_a, some_b), (qk_a, qk_b))
        qk_a, qk_b = links.join(qk_a, up), links.join(qk_b, down)
    some = jnp.concatenate([some_a, some_b])
    grad_w_up, grad_w_value, grad_w_down, grad_w_out = finish(place, some, links.swap(some, 1), (False, False, True, False))
    qk = jnp.stack([qk_a, qk_b])
    grad_w_query, grad_w_key = finish(place, qk, links.swap(qk, 1), (False, False))

    grad_b_up = lax.dynamic_index_in_dim(vec, 16 + links.z, 0, keepdims=False)
    return (
        out, gtok, vec[7], vec[8], grad_w_query, grad_w_key, grad_w_value, grad_w_out,
        vec[4], vec[5], vec[6], vec[3], vec[0], vec[1], grad_w_up, grad_b_up, grad_w_down, vec[2],
    )


def solution(mesh):
    rows = P(("dp", "tensor"), None)
    whole = P()
    return jax.shard_map(
        body,
        mesh=mesh,
        in_specs=(rows,) * 3 + (whole,) * 13 + (P(None, "tensor"), P("tensor"), P("tensor", None), whole),
        out_specs=(rows,) * 2 + (whole,) * 12 + (P(None, "tensor"), P("tensor"), P("tensor", None), whole),
        check_vma=False,
    )
```

```python
from functools import partial
import math

import jax
import jax.numpy as jnp
import ml_dtypes
import numpy as np
from jax import lax
from jax.experimental import pallas as pl
from jax.experimental.pallas import tpu as pltpu
from jax.sharding import PartitionSpec as P

HEADS = 12
HD = 64
FEAT = 32
EPS = 1e-05
F32 = jnp.float32
BF16 = jnp.bfloat16
ANY = pl.BlockSpec(memory_space=pltpu.HBM)
VM = pl.BlockSpec(memory_space=pltpu.VMEM)
SMEM = pl.BlockSpec(memory_space=pltpu.SMEM)
SCALE = HD ** -0.25


def nn(a, b):
    return lax.dot_general(a, b, (((1,), (0,)), ((), ())), preferred_element_type=F32)


def nt(a, b):
    return lax.dot_general(a, b, (((1,), (1,)), ((), ())), preferred_element_type=F32)


def split(v):
    high = v.astype(BF16)
    return high, (v - high.astype(F32)).astype(BF16)


def rotary_table(length):
    half = HD // 2
    rate = np.exp(np.arange(half) * (-2.0 * math.log(10000.0) / HD))
    angle = np.arange(length)[:, None] * rate[None, :]
    lane = np.arange(128)
    cos = np.tile(np.cos(angle), (1, 4)) * SCALE
    sin = np.tile(np.sin(angle), (1, 4)) * SCALE
    first = (lane % HD < half)[None, :]
    table = np.concatenate([cos, -sin * first, sin * ~first], 1).astype(np.float32)
    parts = []
    for _ in range(3):
        part = table.astype(ml_dtypes.bfloat16)
        parts.append(part)
        table = table - part.astype(np.float32)
    return np.stack(parts)


def lane_mask(head_in_group):
    lane = lax.broadcasted_iota(jnp.int32, (1, 128), 1)
    return jnp.where(lane // FEAT == head_in_group, 1.0, 0.0).astype(BF16)


def norm_parts(v):
    centred = v - jnp.mean(v, -1, keepdims=True)
    scale = lax.rsqrt(jnp.mean(centred * centred, -1, keepdims=True) + EPS)
    return centred * scale, scale


def norm_back(grad, hat, scale, gain):
    hat_grad = grad * gain
    return scale * (
        hat_grad
        - jnp.mean(hat_grad, -1, keepdims=True)
        - hat * jnp.mean(hat_grad * hat, -1, keepdims=True)
    )


def label_column(seg):
    rows = seg.shape[1]
    return jnp.transpose(jnp.broadcast_to(seg[...].astype(F32), (128, rows)))


def block_projection(proj):
    tall = jnp.concatenate([proj[...]] * 4, axis=0)
    wide = jnp.concatenate([tall] * 4, axis=1)
    group = lax.broadcasted_iota(jnp.int32, (256, 128), 0) // HD
    feat = lax.broadcasted_iota(jnp.int32, (256, 128), 1) // FEAT
    return jnp.where(group == feat, wide, 0.0), jnp.where(group == feat, 1.0, 0.0).astype(BF16)


def turn(u, cos, sin_a, sin_b):
    return u * cos + pltpu.roll(u, 96, 1) * sin_a + pltpu.roll(u, 32, 1) * sin_b


def turn_back(u, cos, sin_a, sin_b):
    return u * cos - pltpu.roll(u, 96, 1) * sin_a - pltpu.roll(u, 32, 1) * sin_b


class Feed:
    def __init__(self, pairs, sems):
        self.sems, self.copies, self.left = sems, [], []
        for src, dst in pairs:
            self.add(src, dst)

    def add(self, src, dst):
        copy = pltpu.make_async_copy(src, dst, self.sems.at[len(self.copies)])
        copy.start()
        self.left.append(len(self.copies))
        self.copies.append(copy)

    def need(self, *which):
        for n in which or list(self.left):
            if n in self.left:
                self.copies[n].wait()
                self.left.remove(n)


def call(kernel, name, ins, outs, scratch, limit, sems, flops, smem=0, far=(), far_out=(), alias=None):
    return pl.pallas_call(
        kernel,
        out_shape=outs,
        in_specs=[SMEM if n < smem else ANY if n in far else VM for n in range(len(ins))],
        out_specs=[ANY if n in far_out else VM for n in range(len(outs))],
        scratch_shapes=list(scratch) + ([pltpu.SemaphoreType.DMA((sems,))] if sems else []),
        input_output_aliases=alias or {},
        compiler_params=pltpu.CompilerParams(vmem_limit_bytes=limit << 20),
        cost_estimate=pl.CostEstimate(flops=flops, bytes_accessed=1000, transcendentals=0),
        name=name,
    )(*ins)


TILE = 256


def attn_fwd_kernel(seg, fg, fb, bq, bk, bv, bo, sg, sb, proj, tok_i, wv_i, wq_i, tab_i, wk_i, wo_i,
                    normed_i, s_i, f_i, v_i, rot_i, c0_o, ctx_o, dinv_o, mid_o, sec_o,
                    col_s, normed_o, s_o, f_o, v_o, rot_o, tok, wv, wq, tab, wk, wo, sems):
    feed = Feed([(tab_i, tab), (tok_i, tok), (wv_i, wv), (wq_i, wq), (wk_i, wk), (wo_i, wo)], sems)
    rows, width = tok.shape
    col_s[...] = label_column(seg)
    seg_row = seg[...].astype(F32)
    less = jnp.where(seg_row < col_s[:, :1], 1.0, 0.0)
    start = jnp.sum(less, axis=1, keepdims=True)
    place = lax.broadcasted_iota(jnp.int32, (rows, 1), 0).astype(F32) - start
    length = tab.shape[1]
    ladder = lax.broadcasted_iota(jnp.int32, (rows, length), 1).astype(F32)
    one_hot = jnp.where(ladder == place, 1.0, 0.0).astype(BF16)
    p_wide, blocks = block_projection(proj)
    p_hi, p_lo = split(p_wide)
    halves = blocks * 0.5
    feed.need(0)
    rot_o[...] = nn(one_hot, tab[0]) + nn(one_hot, tab[1]) + nn(one_hot, tab[2])
    feed.need(1, 2, 3, 4)

    def first(i, _):
        at = pl.ds(pl.multiple_of(i * TILE, TILE), TILE)
        x = tok[at, :].astype(F32)
        hat, _scale = norm_parts(x)
        normed = (hat * fg[...] + fb[...]).astype(BF16)
        normed_o[at, :] = normed
        v_o[at, :] = nn(normed, wv[...]).astype(BF16)
        cos, sin_a, sin_b = rot_o[at, 0:128], rot_o[at, 128:256], rot_o[at, 256:384]
        for which, (w, b) in enumerate(((wq, bq), (wk, bk))):
            u = nn(normed, w[...]) + b[...]
            for g in range(width // 256):
                s = jnp.concatenate([turn(u[:, k:k + 128], cos, sin_a, sin_b) for k in (256 * g, 256 * g + 128)], 1)
                s_hi, s_lo = split(s)
                s_o[which, at, 256 * g:256 * g + 256] = s_hi
                q_hi, q_lo = split(s * s)
                e = nn(s_hi, p_hi) + nn(s_lo, p_hi) + nn(s_hi, p_lo) - nn(q_hi, halves) - nn(q_lo, halves)
                f_o[which, at, 128 * g:128 * g + 128] = (jnp.exp(e) * FEAT ** -0.5).astype(BF16)
        return 0

    lax.fori_loop(0, rows // TILE, first, 0)
    feed.need()
    for held, kept in ((normed_o, normed_i), (s_o, s_i), (f_o, f_i), (v_o, v_i), (rot_o, rot_i)):
        feed.add(held, kept)

    ones = jnp.ones((rows, 128), BF16)
    even = lax.broadcasted_iota(jnp.int32, (1, 128), 1) < HD

    def second(i, _):
        at = pl.ds(pl.multiple_of(i * TILE, TILE), TILE)
        same = col_s[at, :1] == seg_row
        for j in range(HEADS // 2):
            g = j // 2
            vals = jnp.concatenate([v_o[:, 128 * j:128 * j + 128], ones], 1)
            qf = f_o[0, at, 128 * g:128 * g + 128]
            kf = f_o[1, :, 128 * g:128 * g + 128]
            res = []
            for h in range(2):
                scores = nt(qf * lane_mask(2 * (j % 2) + h), kf)
                weights = jnp.where(same, scores, 0.0).astype(BF16)
                res.append(nn(weights, vals))
            num = jnp.where(even, res[0][:, :128], res[1][:, :128])
            inv = 1.0 / jnp.where(even, res[0][:, 128:], res[1][:, 128:])
            lanes = slice(128 * j, 128 * j + 128)
            ctx = num * inv
            dinv_o[at, lanes] = inv
            c0_o[at, lanes] = ctx
            ctx_o[at, lanes] = (ctx + bv[:, lanes]).astype(BF16)
        middle = tok[at, :].astype(F32) + nn(ctx_o[at, :], wo[...]) + bo[...]
        mid_o[at, :] = middle
        hat, _scale = norm_parts(middle)
        sec_o[at, :] = (hat * sg[...] + sb[...]).astype(BF16)
        return 0

    lax.fori_loop(0, rows // TILE, second, 0)
    feed.need()


def attn_fwd(tok, seg, tab, proj, fg, fb, wq, wk, wv, wo, bq, bk, bv, bo, sg, sb):
    rows, width = tok.shape
    sd, v = jax.ShapeDtypeStruct, pltpu.VMEM
    outs = (
        sd((rows, width), BF16),
        sd((2, rows, width), BF16),
        sd((2, rows, HEADS * FEAT), BF16),
        sd((rows, width), BF16),
        sd((rows, 384), F32),
        sd((rows, width), F32),
        sd((rows, width), BF16),
        sd((rows, width), F32),
        sd((rows, width), F32),
        sd((rows, width), BF16),
    )
    near = (seg, fg, fb, bq, bk, bv, bo, sg, sb, proj)
    far = (tok, wv, wq, tab, wk, wo)
    scratch = [v((rows, 128), F32)] + [v(a.shape, a.dtype) for a in outs[:5] + far]
    return call(attn_fwd_kernel, "attn_fwd", near + far, outs, scratch, 52, len(far) + 5, 5520000000,
                far=range(len(near), len(near) + len(far)), far_out=range(5))


FFN_STEP = 256


def ffn_kernel(first, last, place, sec, cot, *refs):
    n_in = 5 if first else 8
    ins, refs = refs[:n_in], refs[n_in:]
    out_o, sg_o, send_o, keep_o, gb_o, wu, wd, secT, hidT, acc, sems = refs
    x, y, c = place[0], place[1], place[2]
    rows, width = sec.shape
    quarter, half = width // 4, width // 2

    def part(a, core):
        return pl.ds(pl.multiple_of((2 * a + core) * quarter, quarter), quarter)

    if first:
        bu, oacc, bd, wu_i, wd_i = ins
        feed = Feed([(wu_i, wu), (wd_i, wd)], sems)
        bias = bu[...]
        early = (0,)
    else:
        own, own_x, own_y, far, far_x, far_y, oacc, sacc = ins
        up, down = pl.ds(0, quarter), pl.ds(quarter, quarter)
        feed = Feed([
            (own.at[up], wu.at[part(x, c)]), (own_x, wu.at[part(1 - x, c)]),
            (far.at[up], wu.at[part(x, 1 - c)]), (far_x, wu.at[part(1 - x, 1 - c)]),
            (own.at[down], wd.at[part(y, c)]), (own_y, wd.at[part(1 - y, c)]),
            (far.at[down], wd.at[part(y, 1 - c)]), (far_y, wd.at[part(1 - y, 1 - c)]),
        ], sems)
        tail = own[2 * quarter:2 * quarter + 16, :].astype(F32)
        bias = tail[0:1, :] + tail[1:2, :] + tail[2:3, :]
        early = (0, 1, 2, 3)
    mine = pl.ds(pl.multiple_of(c * half, half), half)
    other = pl.ds(pl.multiple_of((1 - c) * half, half), half)
    secT[...] = jnp.transpose(sec[...])
    feed.need(*early)
    cut = FFN_STEP // 2
    for n, at in enumerate(range(0, width, FFN_STEP)):
        cs = slice(at, at + FFN_STEP)
        inner = nn(sec[...], wu[:, cs]) + bias[:, cs]
        cdf = 0.5 + 0.5 * lax.erf(inner * math.sqrt(0.5))
        slope = cdf + inner * (jnp.exp(-0.5 * inner * inner) * (1.0 / math.sqrt(2.0 * math.pi)))
        hidden = (inner * cdf).astype(BF16)
        feed.need()
        grad = (nt(cot[...], wd[cs, :]) * slope).astype(BF16)
        gb_o[:, cs] = jnp.sum(grad.astype(F32), 0, keepdims=True)
        more_out = nn(hidden, wd[cs, :])
        more_sg = nt(grad, wu[:, cs])
        if n == 0:
            acc[...] = oacc[...] + more_out + (bd[...] if first else 0.0)
            sg_o[...] = more_sg if first else sacc[...] + more_sg
        else:
            acc[...] += more_out
            sg_o[...] += more_sg
        hidT[...] = jnp.transpose(hidden)
        piece = slice(n * cut, n * cut + cut)
        keep_o[1, piece, :] = nn(hidT[pl.ds(pl.multiple_of(c * cut, cut), cut), :], cot[...]).astype(BF16)
        send_o[1, piece, :] = nn(hidT[pl.ds(pl.multiple_of((1 - c) * cut, cut), cut), :], cot[...]).astype(BF16)
        keep_o[0, :, cs] = nn(secT[mine, :], grad).astype(BF16)
        send_o[0, :, cs] = nn(secT[other, :], grad).astype(BF16)
    out_o[...] = acc[...].astype(out_o.dtype)


def ffn(first, last, place, sec, cot, *ins):
    rows, width = sec.shape
    sd, v = jax.ShapeDtypeStruct, pltpu.VMEM
    outs = (
        sd((rows, width), BF16 if last else F32),
        sd((rows, width), F32),
        sd((2, width // 2, width), BF16),
        sd((2, width // 2, width), BF16),
        sd((1, width), F32),
    )
    scratch = [v((width, width), BF16), v((width, width), BF16), v((width, rows), BF16), v((FFN_STEP, rows), BF16),
               v((rows, width), F32)]
    return call(partial(ffn_kernel, first, last), "ffn", (place, sec, cot) + ins, outs, scratch, 14, 8, 2760000000, smem=1,
                far=(6, 7) if first else (), alias=None if first else {10: 1})


def out_bwd_kernel(place, sgrad, mid, sg, cot, ctx, dinv, c0, wo_i,
                   send_o, keep_o, low_o, hi_o, lo_o, mg_o, vec, wo, tr_s, cg_s, sems):
    feed = Feed([(wo_i, wo)], sems)
    c = place[2]
    rows, width = mid.shape
    half = width // 2
    tr_s[...] = jnp.transpose(ctx[...])
    hat, scale = norm_parts(mid[...])
    up = sgrad[...]
    vec[...] = jnp.zeros_like(vec)
    vec[0:1, :] = jnp.sum(up * hat, 0, keepdims=True)
    vec[1:2, :] = jnp.sum(up, 0, keepdims=True)
    g = cot[...].astype(F32)
    vec[2:3, :] = jnp.sum(g, 0, keepdims=True)
    mg = g + norm_back(up, hat, scale, sg[...])
    mg_o[...] = mg
    og = mg.astype(BF16)
    vec[3:4, :] = jnp.sum(og.astype(F32), 0, keepdims=True)
    feed.need()
    cg_s[...] = nt(og, wo[...])
    keep_o[...] = nn(tr_s[pl.ds(pl.multiple_of(c * half, half), half), :], og).astype(BF16)
    send_o[...] = nn(tr_s[pl.ds(pl.multiple_of((1 - c) * half, half), half), :], og).astype(BF16)
    for j in range(HEADS // 2):
        lanes = slice(128 * j, 128 * j + 128)
        low = (cg_s[:, lanes] * dinv[:, lanes]).astype(BF16)
        low_o[:, lanes] = low
        less = -(low.astype(F32) * c0[:, lanes])
        hi = less.astype(BF16)
        hi_o[:, lanes] = hi
        lo_o[:, lanes] = pltpu.roll(less - hi.astype(F32), 64, 1).astype(BF16)


def out_bwd(place, sgrad, mid, sg, cot, ctx, dinv, c0, wo):
    rows, width = mid.shape
    sd, v = jax.ShapeDtypeStruct, pltpu.VMEM
    outs = (
        sd((width // 2, width), BF16),
        sd((width // 2, width), BF16),
        sd((rows, width), BF16),
        sd((rows, width), BF16),
        sd((rows, width), BF16),
        sd((rows, width), F32),
        sd((16, width), F32),
    )
    scratch = [v((width, width), BF16), v((width, rows), BF16), v((rows, width), F32)]
    return call(out_bwd_kernel, "out_bwd", (place, sgrad, mid, sg, cot, ctx, dinv, c0, wo), outs, scratch, 12, 1, 2300000000, smem=1, far=(8,))


def value_bwd_kernel(place, seg, low, f, normed, send_o, keep_o, gv_o, normT_o, vec, col_s):
    c = place[2]
    rows, width = low.shape
    half = width // 2
    col_s[...] = label_column(seg)
    seg_row = seg[...].astype(F32)
    lane = lax.broadcasted_iota(jnp.int32, (1, 128), 1)

    def heads(i, _):
        at = pl.ds(pl.multiple_of(i * TILE, TILE), TILE)
        same = col_s[at, :1] == seg_row
        for j in range(HEADS // 2):
            lanes = slice(128 * j, 128 * j + 128)
            flanes = slice(128 * (j // 2), 128 * (j // 2) + 128)
            res = []
            for h in range(2):
                fm = lane_mask(2 * (j % 2) + h)
                wT = jnp.where(same, nt(f[1, at, flanes] * fm, f[0, :, flanes]), 0.0).astype(BF16)
                res.append(nn(wT, low[:, lanes]))
            gv_o[at, lanes] = jnp.where(lane < HD, res[0], res[1]).astype(BF16)
        return 0

    lax.fori_loop(0, rows // TILE, heads, 0)
    normT_o[...] = jnp.transpose(normed[...])
    vec[...] = jnp.zeros_like(vec)
    vec[6:7, :] = jnp.sum(gv_o[...].astype(F32), 0, keepdims=True)
    keep_o[...] = nn(normT_o[pl.ds(pl.multiple_of(c * half, half), half), :], gv_o[...]).astype(BF16)
    send_o[...] = nn(normT_o[pl.ds(pl.multiple_of((1 - c) * half, half), half), :], gv_o[...]).astype(BF16)


def value_bwd(place, seg, low, f, normed):
    rows, width = low.shape
    sd, v = jax.ShapeDtypeStruct, pltpu.VMEM
    outs = (
        sd((width // 2, width), BF16),
        sd((width // 2, width), BF16),
        sd((rows, width), BF16),
        sd((width, rows), BF16),
        sd((16, width), F32),
    )
    return call(value_bwd_kernel, "value_bwd", (place, seg, low, f, normed), outs, [v((rows, 128), F32)], 12, 0, 3680000000, smem=1)


def score_bwd_kernel(seg, low, hi, lo, vals, f, de_o, col_s):
    rows, width = low.shape
    col_s[...] = label_column(seg)
    seg_row = seg[...].astype(F32)
    ones = jnp.ones((rows, 128), BF16)
    lane = lax.broadcasted_iota(jnp.int32, (1, 128), 1)

    def heads(i, _):
        at = pl.ds(pl.multiple_of(i * TILE, TILE), TILE)
        same = col_s[at, :1] == seg_row
        for j in range(HEADS // 2):
            gr = j // 2
            lanes = slice(128 * j, 128 * j + 128)
            flanes = slice(128 * gr, 128 * gr + 128)
            v_all = jnp.concatenate([vals[:, lanes], ones], 1)
            v_at = jnp.concatenate([vals[at, lanes], ones[:TILE]], 1)
            qf_all, kf_all = f[0, :, flanes], f[1, :, flanes]
            dq, dk = None, None
            for h in range(2):
                fm = lane_mask(2 * (j % 2) + h).astype(F32)
                own = jnp.where(lane // HD == h, 1.0, 0.0).astype(BF16)
                rest = 1.0 - own

                def pair(span):
                    return jnp.concatenate([low[span, lanes] * own, hi[span, lanes] * own + lo[span, lanes] * rest], 1)

                dwT = jnp.where(same, nt(v_at, pair(slice(None))), 0.0).astype(BF16)
                gk = nn(dwT, qf_all) * fm
                dk = gk if dk is None else dk + gk
                dw = jnp.where(same, nt(pair(at), v_all), 0.0).astype(BF16)
                gq = nn(dw, kf_all) * fm
                dq = gq if dq is None else dq + gq
            if j % 2 == 0:
                de_o[0, at, flanes] = dq
                de_o[1, at, flanes] = dk
            else:
                de_o[0, at, flanes] = (de_o[0, at, flanes] + dq) * f[0, at, flanes].astype(F32)
                de_o[1, at, flanes] = (de_o[1, at, flanes] + dk) * f[1, at, flanes].astype(F32)
        return 0

    lax.fori_loop(0, rows // TILE, heads, 0)


def score_bwd(seg, low, hi, lo, vals, f):
    rows = low.shape[0]
    outs = (jax.ShapeDtypeStruct((2, rows, HEADS * FEAT), F32),)
    return call(score_bwd_kernel, "score_bwd", (seg, low, hi, lo, vals, f), outs, [pltpu.VMEM((rows, 128), F32)], 12, 0, 5520000000)[0]


def key_bwd_kernel(place, de, s, rot, proj, normT, send_o, keep_o, grads_o, vec):
    c = place[2]
    rows = s.shape[1]
    width = s.shape[2]
    half = width // 2
    p_wide, blocks = block_projection(proj)
    p_hi, p_lo = split(p_wide)

    def back(i, _):
        at = pl.ds(pl.multiple_of(i * TILE, TILE), TILE)
        cos, sin_a, sin_b = rot[at, 0:128], rot[at, 128:256], rot[at, 256:384]
        for which in range(2):
            for gr in range(width // 256):
                d_hi, d_lo = split(de[which, at, 128 * gr:128 * gr + 128])
                s_at = s[which, at, 256 * gr:256 * gr + 256].astype(F32)
                ds = nt(d_hi, p_hi) + nt(d_lo, p_hi) + nt(d_hi, p_lo) - s_at * (nt(d_hi, blocks) + nt(d_lo, blocks))
                for k in range(2):
                    du = turn_back(ds[:, 128 * k:128 * k + 128], cos, sin_a, sin_b)
                    lanes = slice(256 * gr + 128 * k, 256 * gr + 128 * k + 128)
                    grads_o[which, at, lanes] = du.astype(BF16)
        return 0

    lax.fori_loop(0, rows // TILE, back, 0)
    vec[...] = jnp.zeros_like(vec)
    for which in range(2):
        vec[4 + which:5 + which, :] = jnp.sum(grads_o[which].astype(F32), 0, keepdims=True)
        keep_o[which] = nn(normT[pl.ds(pl.multiple_of(c * half, half), half), :], grads_o[which]).astype(BF16)
        send_o[which] = nn(normT[pl.ds(pl.multiple_of((1 - c) * half, half), half), :], grads_o[which]).astype(BF16)


def key_bwd(place, de, s, rot, proj, normT):
    width, rows = normT.shape
    sd = jax.ShapeDtypeStruct
    outs = (
        sd((2, width // 2, width), BF16),
        sd((2, width // 2, width), BF16),
        sd((2, rows, width), BF16),
        sd((16, width), F32),
    )
    return call(key_bwd_kernel, "key_bwd", (place, de, s, rot, proj, normT), outs, [], 12, 0, 1840000000, smem=1)


def token_bwd_kernel(grads, gv, mg, fg, tok, wq_i, wk_i, wv_i, gtok_o, vec, wq, wk, wv, sems):
    feed = Feed([(wv_i, wv), (wq_i, wq), (wk_i, wk)], sems)
    hat, scale = norm_parts(tok[...].astype(F32))
    feed.need(0)
    ng = nt(gv[...], wv[...])
    feed.need()
    ng = ng + nt(grads[0], wq[...]) + nt(grads[1], wk[...])
    vec[...] = jnp.zeros_like(vec)
    vec[7:8, :] = jnp.sum(ng * hat, 0, keepdims=True)
    vec[8:9, :] = jnp.sum(ng, 0, keepdims=True)
    gtok_o[...] = (mg[...] + norm_back(ng, hat, scale, fg[...])).astype(BF16)


def token_bwd(grads, gv, mg, fg, tok, wq, wk, wv):
    rows, width = tok.shape
    sd, v = jax.ShapeDtypeStruct, pltpu.VMEM
    outs = (sd((rows, width), BF16), sd((16, width), F32))
    return call(token_bwd_kernel, "token_bwd", (grads, gv, mg, fg, tok, wq, wk, wv), outs,
                [v((width, width), BF16)] * 3, 12, 3, 1840000000, far=(5, 6, 7))


def pack_kernel(place, wu, wd, bu, out, sems):
    quarter = wu.shape[1] // 4
    x, y, c = place[0], place[1], place[2]
    feed = Feed([
        (wu.at[pl.ds(pl.multiple_of((2 * x + c) * quarter, quarter), quarter)], out.at[pl.ds(0, quarter)]),
        (wd.at[pl.ds(pl.multiple_of((2 * y + c) * quarter, quarter), quarter)], out.at[pl.ds(quarter, quarter)]),
    ], sems)
    left, parts = bu[...], []
    for _ in range(3):
        parts.append(left.astype(BF16).astype(F32))
        left = left - parts[-1]
    parts.append(jnp.zeros((13, left.shape[1]), F32))
    out[2 * quarter:2 * quarter + 16, :] = jnp.concatenate(parts, 0).astype(BF16)
    feed.need()


def pack(place, wu, wd, bu):
    width = wu.shape[1]
    outs = (jax.ShapeDtypeStruct((width // 2 + 16, width), BF16),)
    return call(pack_kernel, "pack", (place, wu, wd, bu), outs, [], 58, 2, 460000000, smem=1, far=(1, 2))[0]


def finish_kernel(woven, place, mine, got, *refs):
    n = mine.shape[0]
    outs, refs = refs[:n], refs[n:]
    held, sems = refs
    c = place[2]
    rows = mine.shape[1]
    feed = Feed([], sems)
    cut = FFN_STEP // 2
    for m in range(n):
        for side, (ref, core) in enumerate(((mine, c), (got, 1 - c))):
            held[m, side] = ref[m].astype(F32)
            if woven[m]:
                for k in range(rows // cut):
                    feed.add(held.at[m, side, pl.ds(k * cut, cut)], outs[m].at[pl.ds(pl.multiple_of(2 * k * cut + core * cut, cut), cut)])
            else:
                feed.add(held.at[m, side], outs[m].at[pl.ds(pl.multiple_of(core * rows, rows), rows)])
    feed.need()


def finish(place, mine, got, woven):
    n, rows, width = mine.shape
    outs = (jax.ShapeDtypeStruct((2 * rows, width), F32),) * n
    return call(partial(finish_kernel, woven), "finish", (place, mine, got), outs, [pltpu.VMEM((n, 2, rows, width), F32)], 20,
                sum(2 * (rows // (FFN_STEP // 2) if w else 1) for w in woven), 920000000, smem=1, far_out=range(n))


def add_low(*parts):
    total = parts[0].astype(F32)
    for part in parts[1:]:
        total = total + part.astype(F32)
    return total.astype(parts[0].dtype)


def ordered(first, then):
    return lax.optimization_barrier((first, then))[1]


class Links:
    def __init__(self):
        self.dp, self.ring = lax.axis_size("dp"), lax.axis_size("tensor")
        self.at = lax.axis_index("dp")
        self.z = lax.axis_index("tensor")
        self.bits = [1 << n for n in range(1, self.dp.bit_length() - 1)]

    def side(self, bit):
        return (self.at // bit) % 2

    def swap(self, v, bit):
        return lax.ppermute(v, "dp", [(i, i ^ bit) for i in range(self.dp)])

    def shift(self, v, by=1):
        return lax.ppermute(v, "tensor", [(i, (i + by) % self.ring) for i in range(self.ring)])

    def near(self, v, bit):
        return lax.ppermute(v, "tensor", [(i, i ^ bit) for i in range(self.ring)])

    def cut(self, v, bit):
        rows = v.shape[-2] // 2
        return (lax.dynamic_slice_in_dim(v, (1 - self.side(bit)) * rows, rows, v.ndim - 2),
                lax.dynamic_slice_in_dim(v, self.side(bit) * rows, rows, v.ndim - 2))

    def join(self, v, got, bit):
        low = self.side(bit) == 0
        return jnp.concatenate([jnp.where(low, v, got), jnp.where(low, got, v)], v.ndim - 2)


def fence(*values):
    return lax.optimization_barrier(values)


class Halves:
    def __init__(self, links, a, b):
        self.links, self.vals, self.level = links, [a, b], 0
        self.levels = len(links.bits)

    def bits(self):
        return self.links.bits[self.level], self.links.bits[::-1][self.level]

    def send(self):
        cuts = [self.links.cut(v, bit) for v, bit in zip(self.vals, self.bits())]
        self.own = [c[1] for c in cuts]
        return [self.links.swap(c[0], bit) for c, bit in zip(cuts, self.bits())]

    def take(self, got):
        self.vals = [add_low(v, g) for v, g in zip(self.own, got)]
        self.level += 1
        return self.vals

    def rest(self):
        while self.level < self.levels:
            self.take(self.send())
        return self.vals


class Joins:
    def __init__(self, links, a, b):
        self.links, self.vals, self.level = links, [a, b], len(links.bits)

    def bits(self):
        return self.links.bits[self.level], self.links.bits[::-1][self.level]

    def send(self):
        self.level -= 1
        return [self.links.swap(v, bit) for v, bit in zip(self.vals, self.bits())]

    def take(self, got):
        self.vals = [self.links.join(v, g, bit) for v, g, bit in zip(self.vals, got, self.bits())]
        return self.vals

    def rest(self, left):
        while self.level > left:
            self.take(self.send())
        return self.vals


def body(tokens, cotangent, segment, projection, first_gain, first_bias, w_query, w_key, w_value, w_out,
         b_query, b_key, b_value, b_out, second_gain, second_bias, w_up, b_up, w_down, b_down):
    links = Links()
    rows, width = tokens.shape
    pairs = list(zip(links.bits, links.bits[::-1]))
    low_bit, top_bit = links.bits[0], links.bits[-1]
    core, x, y = links.side(1), links.side(low_bit), links.side(top_bit)
    place = jnp.stack([x, y, core]).astype(jnp.int32)
    quarter = width // 4

    def line(v):
        return v.reshape(1, -1)

    share = links.shift(pack(place, w_up, w_down, line(b_up)))
    table = jnp.asarray(rotary_table(256))
    normed, s, f, vals, rot, c0, ctx, dinv, mid, second = attn_fwd(
        tokens, segment, table, projection, line(first_gain), line(first_bias), w_query, w_key, w_value, w_out,
        line(b_query), line(b_key), line(b_value), line(b_out), line(second_gain), line(second_bias))

    def beside(share):
        return links.swap(share[:quarter], low_bit), links.swap(share[quarter:2 * quarter], top_bit)

    def own_ffn(first, last, parts, acc):
        ins = (line(b_up), mid, line(b_down), w_up, w_down) if first else parts + acc
        return ffn(first, last, place, second, cotangent, *ins)

    share, second = fence(share, second)
    swapped, coming = beside(share), links.shift(share)
    out, sgrad, send, keep, slope = own_ffn(True, False, (), ())
    swapped, out, send = fence(swapped, out, send)
    slopes, keeps, sends = [slope], [keep], [send]
    across = tuple(links.swap(v, 1) for v in (share,) + swapped)
    for n in range(1, links.ring):
        last = n == links.ring - 1
        parts = (share,) + swapped + across
        if not last:
            parts, share, out = fence(parts, coming, out)
            swapped = beside(share)
            coming = links.shift(share) if n < links.ring - 2 else share
        if n == 2:
            ring, out = fence(add_low(keeps[1], sends[1]), out)
            ring = links.shift(ring)
        sends[-1] = links.swap(sends[-1], 1)
        out, sgrad, send, keep, slope = own_ffn(False, last, parts, (out, sgrad))
        slopes.append(slope)
        keeps.append(keep)
        sends.append(send)
        if not last:
            swapped, coming, out = fence(swapped, coming, out)
            across = tuple(links.swap(v, 1) for v in (share,) + swapped)
            across, sends[-1] = fence(across, sends[-1])
            if n == 1:
                sends[-1] = links.swap(sends[-1], 1)

    sends[-1] = links.swap(sends[-1], 1)
    ring, sgrad, extra = fence(ring, sgrad, sends[2 % links.ring])
    ring = links.shift(add_low(ring, keeps[2 % links.ring], extra)) if links.ring > 2 else ring
    send_o, keep_o, low, hi, lo, mg, vec_o = out_bwd(
        place, sgrad, mid, line(second_gain), cotangent, ctx, dinv, c0, w_out)
    far_o = links.swap(send_o, 1)
    send_v, keep_v, gv, normT, vec_v = value_bwd(place, segment, low, f, normed)
    far_v = links.swap(send_v, 1)
    ring, far_o, far_v, gv = fence(ring, far_o, far_v, gv)
    if links.ring > 3:
        ring = add_low(ring, keeps[3], sends[3])
    ov = Halves(links, add_low(keep_v, far_v), add_low(keep_o, far_o))
    ring, vals_in, low, gv = fence(ring, ov.vals, low, gv)
    ov.vals = list(vals_in)
    if links.ring > 3:
        ring = links.shift(ring)
    got = ov.send()
    de = score_bwd(segment, low, hi, lo, vals, f)
    got, ring, de = fence(got, ring, de)
    ov.take(got)
    for n in range(4, links.ring):
        ring = links.shift(add_low(ring, keeps[n], sends[n]))
    ring = add_low(ring, keeps[0], sends[0])
    vals_in, ring, de = fence(ov.vals, ring, de)
    ov.vals = list(vals_in)
    ff = Halves(links, ring[0], ring[1])
    deep = len(links.bits) > 1
    got_ov, got_ff = (ov.send() if deep else None), ff.send()
    send_k, keep_k, grads, vec_k = key_bwd(place, de, s, rot, projection, normT)
    got_ff, send_k, grads = fence(got_ff, send_k, grads)
    far_k = links.swap(send_k, 1)
    got_ov, far_k, grads = fence(got_ov, far_k, grads)
    if deep:
        ov.take(got_ov)
    ff.take(got_ff)
    qk_sum = add_low(keep_k, far_k)
    qk_sum, ff_in, ov_in, grads = fence(qk_sum, ff.vals, ov.rest(), grads)
    ff.vals = list(ff_in)
    qk = Halves(links, qk_sum[0], qk_sum[1])
    got_qk = qk.send()
    ov = jnp.stack(ov_in)
    got_ov = links.near(ov, 1)
    got_ff = ff.send() if deep else None
    gtok, vec_t = token_bwd(grads, gv, mg, line(first_gain), tokens, w_query, w_key, w_value)

    slope_all = jnp.zeros((links.ring, width), F32)
    for n, slope in enumerate(slopes):
        slope_all = lax.dynamic_update_slice_in_dim(slope_all, slope, (links.z - n) % links.ring, 0)
    got_qk, got_ov, got_ff, vec_t = fence(got_qk, got_ov, got_ff, vec_t)
    vec = jnp.concatenate([vec_o + vec_v + vec_k + vec_t, slope_all])
    qk.take(got_qk)
    ov = add_low(ov, got_ov)
    if deep:
        ff.take(got_ff)
    qk_in, ff_in, ov, vec = fence(qk.vals, ff.rest(), ov, vec)
    qk.vals = list(qk_in)
    got_qk = qk.send() if deep else None
    got_ov = links.near(ov, 2)
    ff = Joins(links, *ff_in)
    got_ff = ff.send()
    got_vec = links.swap(vec, 1)

    got_qk, got_ff, got_vec = fence(got_qk, got_ff, got_vec)
    if deep:
        qk.take(got_qk)
    ff.take(got_ff)
    qk_in, ff_in, vec = fence(qk.rest(), ff.vals, vec + got_vec)
    ff.vals = list(ff_in)
    qk = jnp.stack(qk_in)
    got_qk = links.near(qk, 1)
    got_ff = ff.send() if deep else None
    got_vec = links.swap(vec, low_bit)

    got_qk, got_ff, got_ov, got_vec = fence(got_qk, got_ff, got_ov, got_vec)
    qk = add_low(qk, got_qk)
    if deep:
        ff.take(got_ff)
    qk, ff_in, ov, vec = fence(qk, jnp.stack(ff.rest(0)), add_low(ov, got_ov), vec + got_vec)
    got_qk = links.near(qk, 2)
    got_ff = links.swap(ff_in, 1)
    ov = Joins(links, ov[0], ov[1])
    got_ov = ov.send()
    got_vec = links.swap(vec, top_bit) if deep else jnp.zeros_like(vec)

    got_ff, got_ov, got_vec = fence(got_ff, got_ov, got_vec)
    grad_w_up, grad_w_down = finish(place, ff_in, got_ff, (False, True))
    ov.take(got_ov)
    ov_in, vec = fence(ov.vals, vec + got_vec)
    ov.vals = list(ov_in)
    got_ov = ov.send() if deep else None
    for bit in links.bits[1:-1]:
        vec = vec + links.swap(vec, bit)
    got_vec = links.near(vec, 1)

    got_qk, got_ov, got_vec = fence(got_qk, got_ov, got_vec)
    qk = add_low(qk, got_qk)
    if deep:
        ov.take(got_ov)
    qk, ov_in, vec = fence(qk, jnp.stack(ov.rest(0)), vec + got_vec)
    qk = Joins(links, qk[0], qk[1])
    got_qk = qk.send()
    got_ov = links.swap(ov_in, 1)
    got_vec = links.near(vec, 2)

    got_qk, got_ov, got_vec = fence(got_qk, got_ov, got_vec)
    vec = vec + got_vec
    qk.take(got_qk)
    qk.vals = list(fence(*qk.vals))
    got_qk = qk.send() if deep else None
    grad_w_value, grad_w_out = finish(place, ov_in, got_ov, (False, False))
    got_qk, grad_w_value, grad_w_out, vec = fence(got_qk, grad_w_value, grad_w_out, vec)
    if deep:
        qk.take(got_qk)
    qk = jnp.stack(qk.rest(0))
    grad_w_query, grad_w_key = finish(place, qk, links.swap(qk, 1), (False, False))

    grad_b_up = lax.dynamic_index_in_dim(vec, 16 + links.z, 0, keepdims=False)
    return (
        out, gtok, vec[7], vec[8], grad_w_query, grad_w_key, grad_w_value, grad_w_out,
        vec[4], vec[5], vec[6], vec[3], vec[0], vec[1], grad_w_up, grad_b_up, grad_w_down, vec[2],
    )


def solution(mesh):
    rows = P(("dp", "tensor"), None)
    whole = P()
    return jax.shard_map(
        body,
        mesh=mesh,
        in_specs=(rows,) * 3 + (whole,) * 13 + (P(None, "tensor"), P("tensor"), P("tensor", None), whole),
        out_specs=(rows,) * 2 + (whole,) * 12 + (P(None, "tensor"), P("tensor"), P("tensor", None), whole),
        check_vma=False,
    )
```

```python
from functools import partial
import math

import jax
import jax.numpy as jnp
import ml_dtypes
import numpy as np
from jax import lax
from jax.experimental import pallas as pl
from jax.experimental.pallas import tpu as pltpu
from jax.sharding import PartitionSpec as P

HEADS = 12
HD = 64
FEAT = 32
EPS = 1e-05
F32 = jnp.float32
BF16 = jnp.bfloat16
ANY = pl.BlockSpec(memory_space=pltpu.HBM)
VM = pl.BlockSpec(memory_space=pltpu.VMEM)
SMEM = pl.BlockSpec(memory_space=pltpu.SMEM)
SCALE = HD ** -0.25


def nn(a, b):
    return lax.dot_general(a, b, (((1,), (0,)), ((), ())), preferred_element_type=F32)


def nt(a, b):
    return lax.dot_general(a, b, (((1,), (1,)), ((), ())), preferred_element_type=F32)


def split(v):
    high = v.astype(BF16)
    return high, (v - high.astype(F32)).astype(BF16)


def rotary_table(length):
    half = HD // 2
    rate = np.exp(np.arange(half) * (-2.0 * math.log(10000.0) / HD))
    angle = np.arange(length)[:, None] * rate[None, :]
    lane = np.arange(128)
    cos = np.tile(np.cos(angle), (1, 4)) * SCALE
    sin = np.tile(np.sin(angle), (1, 4)) * SCALE
    first = (lane % HD < half)[None, :]
    table = np.concatenate([cos, -sin * first, sin * ~first], 1).astype(np.float32)
    parts = []
    for _ in range(3):
        part = table.astype(ml_dtypes.bfloat16)
        parts.append(part)
        table = table - part.astype(np.float32)
    return np.stack(parts)


def lane_mask(head_in_group):
    lane = lax.broadcasted_iota(jnp.int32, (1, 128), 1)
    return jnp.where(lane // FEAT == head_in_group, 1.0, 0.0).astype(BF16)


def norm_parts(v):
    centred = v - jnp.mean(v, -1, keepdims=True)
    scale = lax.rsqrt(jnp.mean(centred * centred, -1, keepdims=True) + EPS)
    return centred * scale, scale


def norm_back(grad, hat, scale, gain):
    hat_grad = grad * gain
    return scale * (
        hat_grad
        - jnp.mean(hat_grad, -1, keepdims=True)
        - hat * jnp.mean(hat_grad * hat, -1, keepdims=True)
    )


def label_column(seg):
    rows = seg.shape[1]
    return jnp.transpose(jnp.broadcast_to(seg[...].astype(F32), (128, rows)))


def block_projection(proj):
    tall = jnp.concatenate([proj[...]] * 4, axis=0)
    wide = jnp.concatenate([tall] * 4, axis=1)
    group = lax.broadcasted_iota(jnp.int32, (256, 128), 0) // HD
    feat = lax.broadcasted_iota(jnp.int32, (256, 128), 1) // FEAT
    return jnp.where(group == feat, wide, 0.0), jnp.where(group == feat, 1.0, 0.0).astype(BF16)


def turn(u, cos, sin_a, sin_b):
    return u * cos + pltpu.roll(u, 96, 1) * sin_a + pltpu.roll(u, 32, 1) * sin_b


def turn_back(u, cos, sin_a, sin_b):
    return u * cos - pltpu.roll(u, 96, 1) * sin_a - pltpu.roll(u, 32, 1) * sin_b


class Feed:
    def __init__(self, pairs, sems):
        self.sems, self.copies, self.left = sems, [], []
        for src, dst in pairs:
            self.add(src, dst)

    def add(self, src, dst):
        copy = pltpu.make_async_copy(src, dst, self.sems.at[len(self.copies)])
        copy.start()
        self.left.append(len(self.copies))
        self.copies.append(copy)

    def need(self, *which):
        for n in which or list(self.left):
            if n in self.left:
                self.copies[n].wait()
                self.left.remove(n)


def call(kernel, name, ins, outs, scratch, limit, sems, flops, smem=0, far=(), far_out=(), alias=None):
    return pl.pallas_call(
        kernel,
        out_shape=outs,
        in_specs=[SMEM if n < smem else ANY if n in far else VM for n in range(len(ins))],
        out_specs=[ANY if n in far_out else VM for n in range(len(outs))],
        scratch_shapes=list(scratch) + ([pltpu.SemaphoreType.DMA((sems,))] if sems else []),
        input_output_aliases=alias or {},
        compiler_params=pltpu.CompilerParams(vmem_limit_bytes=limit << 20),
        cost_estimate=pl.CostEstimate(flops=flops, bytes_accessed=1000, transcendentals=0),
        name=name,
    )(*ins)


TILE = 256
TOKEN_LIMIT = 44


def attn_fwd_kernel(seg, fg, fb, bq, bk, bv, bo, sg, sb, proj, tok_i, wv_i, wq_i, tab_i, wk_i, wo_i,
                    normed_i, s_i, f_i, v_i, rot_i, c0_o, ctx_o, dinv_o, mid_o, sec_o,
                    col_s, normed_o, s_o, f_o, v_o, rot_o, tok, wv, wq, tab, wk, wo, sems):
    feed = Feed([(tab_i, tab), (tok_i, tok), (wv_i, wv), (wq_i, wq), (wk_i, wk), (wo_i, wo)], sems)
    rows, width = tok.shape
    col_s[...] = label_column(seg)
    seg_row = seg[...].astype(F32)
    less = jnp.where(seg_row < col_s[:, :1], 1.0, 0.0)
    start = jnp.sum(less, axis=1, keepdims=True)
    place = lax.broadcasted_iota(jnp.int32, (rows, 1), 0).astype(F32) - start
    length = tab.shape[1]
    ladder = lax.broadcasted_iota(jnp.int32, (rows, length), 1).astype(F32)
    one_hot = jnp.where(ladder == place, 1.0, 0.0).astype(BF16)
    p_wide, blocks = block_projection(proj)
    p_hi, p_lo = split(p_wide)
    halves = blocks * 0.5
    feed.need(0)
    rot_o[...] = nn(one_hot, tab[0]) + nn(one_hot, tab[1]) + nn(one_hot, tab[2])
    feed.need(1, 2)

    def first(i, _):
        at = pl.ds(pl.multiple_of(i * TILE, TILE), TILE)
        x = tok[at, :].astype(F32)
        hat, _scale = norm_parts(x)
        normed = (hat * fg[...] + fb[...]).astype(BF16)
        normed_o[at, :] = normed
        v_o[at, :] = nn(normed, wv[...]).astype(BF16)
        return 0

    lax.fori_loop(0, rows // TILE, first, 0)

    def rotated(i, which, w, b):
        at = pl.ds(pl.multiple_of(i * TILE, TILE), TILE)
        cos, sin_a, sin_b = rot_o[at, 0:128], rot_o[at, 128:256], rot_o[at, 256:384]
        u = nn(normed_o[at, :], w[...]) + b[...]
        for g in range(width // 256):
            s = jnp.concatenate([turn(u[:, k:k + 128], cos, sin_a, sin_b) for k in (256 * g, 256 * g + 128)], 1)
            s_hi, s_lo = split(s)
            s_o[which, at, 256 * g:256 * g + 256] = s_hi
            q_hi, q_lo = split(s * s)
            e = nn(s_hi, p_hi) + nn(s_lo, p_hi) + nn(s_hi, p_lo) - nn(q_hi, halves) - nn(q_lo, halves)
            f_o[which, at, 128 * g:128 * g + 128] = (jnp.exp(e) * FEAT ** -0.5).astype(BF16)
        return 0

    feed.need(3)
    lax.fori_loop(0, rows // TILE, lambda i, _: rotated(i, 0, wq, bq), 0)
    feed.need(4)
    lax.fori_loop(0, rows // TILE, lambda i, _: rotated(i, 1, wk, bk), 0)
    feed.need()
    for held, kept in ((normed_o, normed_i), (s_o, s_i), (f_o, f_i), (v_o, v_i), (rot_o, rot_i)):
        feed.add(held, kept)

    ones = jnp.ones((rows, 128), BF16)
    even = lax.broadcasted_iota(jnp.int32, (1, 128), 1) < HD

    def second(i, _):
        at = pl.ds(pl.multiple_of(i * TILE, TILE), TILE)
        same = col_s[at, :1] == seg_row
        for j in range(HEADS // 2):
            g = j // 2
            vals = jnp.concatenate([v_o[:, 128 * j:128 * j + 128], ones], 1)
            qf = f_o[0, at, 128 * g:128 * g + 128]
            kf = f_o[1, :, 128 * g:128 * g + 128]
            res = []
            for h in range(2):
                scores = nt(qf * lane_mask(2 * (j % 2) + h), kf)
                weights = jnp.where(same, scores, 0.0).astype(BF16)
                res.append(nn(weights, vals))
            num = jnp.where(even, res[0][:, :128], res[1][:, :128])
            inv = 1.0 / jnp.where(even, res[0][:, 128:], res[1][:, 128:])
            lanes = slice(128 * j, 128 * j + 128)
            ctx = num * inv
            dinv_o[at, lanes] = inv
            c0_o[at, lanes] = ctx
            ctx_o[at, lanes] = (ctx + bv[:, lanes]).astype(BF16)
        middle = tok[at, :].astype(F32) + nn(ctx_o[at, :], wo[...]) + bo[...]
        mid_o[at, :] = middle
        hat, _scale = norm_parts(middle)
        sec_o[at, :] = (hat * sg[...] + sb[...]).astype(BF16)
        return 0

    lax.fori_loop(0, rows // TILE, second, 0)
    feed.need()


def attn_fwd(tok, seg, tab, proj, fg, fb, wq, wk, wv, wo, bq, bk, bv, bo, sg, sb):
    rows, width = tok.shape
    sd, v = jax.ShapeDtypeStruct, pltpu.VMEM
    outs = (
        sd((rows, width), BF16),
        sd((2, rows, width), BF16),
        sd((2, rows, HEADS * FEAT), BF16),
        sd((rows, width), BF16),
        sd((rows, 384), F32),
        sd((rows, width), F32),
        sd((rows, width), BF16),
        sd((rows, width), F32),
        sd((rows, width), F32),
        sd((rows, width), BF16),
    )
    near = (seg, fg, fb, bq, bk, bv, bo, sg, sb, proj)
    far = (tok, wv, wq, tab, wk, wo)
    scratch = [v((rows, 128), F32)] + [v(a.shape, a.dtype) for a in outs[:5] + far]
    return call(attn_fwd_kernel, "attn_fwd", near + far, outs, scratch, 52, len(far) + 5, 5520000000,
                far=range(len(near), len(near) + len(far)), far_out=range(5))


FFN_STEP = 256


def ffn_kernel(first, last, place, sec, cot, *refs):
    n_in = 5 if first else 8
    ins, refs = refs[:n_in], refs[n_in:]
    out_o, sg_o, send_o, keep_o, gb_o, wu, wd, secT, hidT, acc, sems = refs
    x, y, c = place[0], place[1], place[2]
    rows, width = sec.shape
    quarter, half = width // 4, width // 2

    def part(a, core):
        return pl.ds(pl.multiple_of((2 * a + core) * quarter, quarter), quarter)

    if first:
        bu, oacc, bd, wu_i, wd_i = ins
        feed = Feed([(wu_i, wu), (wd_i, wd)], sems)
        bias = bu[...]
        early = (0,)
    else:
        own, own_x, own_y, far, far_x, far_y, oacc, sacc = ins
        up, down = pl.ds(0, quarter), pl.ds(quarter, quarter)
        feed = Feed([
            (own.at[up], wu.at[part(x, c)]), (own_x, wu.at[part(1 - x, c)]),
            (far.at[up], wu.at[part(x, 1 - c)]), (far_x, wu.at[part(1 - x, 1 - c)]),
            (own.at[down], wd.at[part(y, c)]), (own_y, wd.at[part(1 - y, c)]),
            (far.at[down], wd.at[part(y, 1 - c)]), (far_y, wd.at[part(1 - y, 1 - c)]),
        ], sems)
        tail = own[2 * quarter:2 * quarter + 16, :].astype(F32)
        bias = tail[0:1, :] + tail[1:2, :] + tail[2:3, :]
        early = (0, 1, 2, 3)
    mine = pl.ds(pl.multiple_of(c * half, half), half)
    other = pl.ds(pl.multiple_of((1 - c) * half, half), half)
    secT[...] = jnp.transpose(sec[...])
    feed.need(*early)
    cut = FFN_STEP // 2
    for n, at in enumerate(range(0, width, FFN_STEP)):
        cs = slice(at, at + FFN_STEP)
        inner = nn(sec[...], wu[:, cs]) + bias[:, cs]
        cdf = 0.5 + 0.5 * lax.erf(inner * math.sqrt(0.5))
        slope = cdf + inner * (jnp.exp(-0.5 * inner * inner) * (1.0 / math.sqrt(2.0 * math.pi)))
        hidden = (inner * cdf).astype(BF16)
        feed.need()
        grad = (nt(cot[...], wd[cs, :]) * slope).astype(BF16)
        gb_o[:, cs] = jnp.sum(grad.astype(F32), 0, keepdims=True)
        more_out = nn(hidden, wd[cs, :])
        more_sg = nt(grad, wu[:, cs])
        if n == 0:
            acc[...] = oacc[...] + more_out + (bd[...] if first else 0.0)
            sg_o[...] = more_sg if first else sacc[...] + more_sg
        else:
            acc[...] += more_out
            sg_o[...] += more_sg
        hidT[...] = jnp.transpose(hidden)
        piece = slice(n * cut, n * cut + cut)
        keep_o[1, piece, :] = nn(hidT[pl.ds(pl.multiple_of(c * cut, cut), cut), :], cot[...]).astype(BF16)
        send_o[1, piece, :] = nn(hidT[pl.ds(pl.multiple_of((1 - c) * cut, cut), cut), :], cot[...]).astype(BF16)
        keep_o[0, :, cs] = nn(secT[mine, :], grad).astype(BF16)
        send_o[0, :, cs] = nn(secT[other, :], grad).astype(BF16)
    out_o[...] = acc[...].astype(out_o.dtype)


def ffn(first, last, place, sec, cot, *ins):
    rows, width = sec.shape
    sd, v = jax.ShapeDtypeStruct, pltpu.VMEM
    outs = (
        sd((rows, width), BF16 if last else F32),
        sd((rows, width), F32),
        sd((2, width // 2, width), BF16),
        sd((2, width // 2, width), BF16),
        sd((1, width), F32),
    )
    scratch = [v((width, width), BF16), v((width, width), BF16), v((width, rows), BF16), v((FFN_STEP, rows), BF16),
               v((rows, width), F32)]
    return call(partial(ffn_kernel, first, last), "ffn", (place, sec, cot) + ins, outs, scratch, 14, 8, 690000000, smem=1,
                far=(6, 7) if first else (), alias=None if first else {10: 1})


def out_bwd_kernel(place, sgrad, mid, sg, cot, ctx, dinv, c0, wo_i,
                   send_o, keep_o, low_o, hi_o, lo_o, mg_o, vec, wo, tr_s, cg_s, sems):
    feed = Feed([(wo_i, wo)], sems)
    c = place[2]
    rows, width = mid.shape
    half = width // 2
    tr_s[...] = jnp.transpose(ctx[...])
    hat, scale = norm_parts(mid[...])
    up = sgrad[...]
    vec[...] = jnp.zeros_like(vec)
    vec[0:1, :] = jnp.sum(up * hat, 0, keepdims=True)
    vec[1:2, :] = jnp.sum(up, 0, keepdims=True)
    g = cot[...].astype(F32)
    vec[2:3, :] = jnp.sum(g, 0, keepdims=True)
    mg = g + norm_back(up, hat, scale, sg[...])
    mg_o[...] = mg
    og = mg.astype(BF16)
    vec[3:4, :] = jnp.sum(og.astype(F32), 0, keepdims=True)
    feed.need()
    cg_s[...] = nt(og, wo[...])
    keep_o[...] = nn(tr_s[pl.ds(pl.multiple_of(c * half, half), half), :], og).astype(BF16)
    send_o[...] = nn(tr_s[pl.ds(pl.multiple_of((1 - c) * half, half), half), :], og).astype(BF16)
    for j in range(HEADS // 2):
        lanes = slice(128 * j, 128 * j + 128)
        low = (cg_s[:, lanes] * dinv[:, lanes]).astype(BF16)
        low_o[:, lanes] = low
        less = -(low.astype(F32) * c0[:, lanes])
        hi = less.astype(BF16)
        hi_o[:, lanes] = hi
        lo_o[:, lanes] = pltpu.roll(less - hi.astype(F32), 64, 1).astype(BF16)


def out_bwd(place, sgrad, mid, sg, cot, ctx, dinv, c0, wo):
    rows, width = mid.shape
    sd, v = jax.ShapeDtypeStruct, pltpu.VMEM
    outs = (
        sd((width // 2, width), BF16),
        sd((width // 2, width), BF16),
        sd((rows, width), BF16),
        sd((rows, width), BF16),
        sd((rows, width), BF16),
        sd((rows, width), F32),
        sd((16, width), F32),
    )
    scratch = [v((width, width), BF16), v((width, rows), BF16), v((rows, width), F32)]
    return call(out_bwd_kernel, "out_bwd", (place, sgrad, mid, sg, cot, ctx, dinv, c0, wo), outs, scratch, 12, 1, 575000000, smem=1, far=(8,))


def value_bwd_kernel(place, seg, low, f, normed, send_o, keep_o, gv_o, normT_o, vec, col_s):
    c = place[2]
    rows, width = low.shape
    half = width // 2
    col_s[...] = label_column(seg)
    seg_row = seg[...].astype(F32)
    lane = lax.broadcasted_iota(jnp.int32, (1, 128), 1)

    def heads(i, _):
        at = pl.ds(pl.multiple_of(i * TILE, TILE), TILE)
        same = col_s[at, :1] == seg_row
        for j in range(HEADS // 2):
            lanes = slice(128 * j, 128 * j + 128)
            flanes = slice(128 * (j // 2), 128 * (j // 2) + 128)
            res = []
            for h in range(2):
                fm = lane_mask(2 * (j % 2) + h)
                wT = jnp.where(same, nt(f[1, at, flanes] * fm, f[0, :, flanes]), 0.0).astype(BF16)
                res.append(nn(wT, low[:, lanes]))
            gv_o[at, lanes] = jnp.where(lane < HD, res[0], res[1]).astype(BF16)
        return 0

    lax.fori_loop(0, rows // TILE, heads, 0)
    normT_o[...] = jnp.transpose(normed[...])
    vec[...] = jnp.zeros_like(vec)
    vec[6:7, :] = jnp.sum(gv_o[...].astype(F32), 0, keepdims=True)
    keep_o[...] = nn(normT_o[pl.ds(pl.multiple_of(c * half, half), half), :], gv_o[...]).astype(BF16)
    send_o[...] = nn(normT_o[pl.ds(pl.multiple_of((1 - c) * half, half), half), :], gv_o[...]).astype(BF16)


def value_bwd(place, seg, low, f, normed):
    rows, width = low.shape
    sd, v = jax.ShapeDtypeStruct, pltpu.VMEM
    outs = (
        sd((width // 2, width), BF16),
        sd((width // 2, width), BF16),
        sd((rows, width), BF16),
        sd((width, rows), BF16),
        sd((16, width), F32),
    )
    return call(value_bwd_kernel, "value_bwd", (place, seg, low, f, normed), outs, [v((rows, 128), F32)], 12, 0, 920000000, smem=1)


def score_bwd_kernel(seg, low, hi, lo, vals, f, de_o, col_s):
    rows, width = low.shape
    col_s[...] = label_column(seg)
    seg_row = seg[...].astype(F32)
    ones = jnp.ones((rows, 128), BF16)
    lane = lax.broadcasted_iota(jnp.int32, (1, 128), 1)

    def heads(i, _):
        at = pl.ds(pl.multiple_of(i * TILE, TILE), TILE)
        same = col_s[at, :1] == seg_row
        for j in range(HEADS // 2):
            gr = j // 2
            lanes = slice(128 * j, 128 * j + 128)
            flanes = slice(128 * gr, 128 * gr + 128)
            v_all = jnp.concatenate([vals[:, lanes], ones], 1)
            v_at = jnp.concatenate([vals[at, lanes], ones[:TILE]], 1)
            qf_all, kf_all = f[0, :, flanes], f[1, :, flanes]
            dq, dk = None, None
            for h in range(2):
                fm = lane_mask(2 * (j % 2) + h).astype(F32)
                own = jnp.where(lane // HD == h, 1.0, 0.0).astype(BF16)
                rest = 1.0 - own

                def pair(span):
                    return jnp.concatenate([low[span, lanes] * own, hi[span, lanes] * own + lo[span, lanes] * rest], 1)

                dwT = jnp.where(same, nt(v_at, pair(slice(None))), 0.0).astype(BF16)
                gk = nn(dwT, qf_all) * fm
                dk = gk if dk is None else dk + gk
                dw = jnp.where(same, nt(pair(at), v_all), 0.0).astype(BF16)
                gq = nn(dw, kf_all) * fm
                dq = gq if dq is None else dq + gq
            if j % 2 == 0:
                de_o[0, at, flanes] = dq
                de_o[1, at, flanes] = dk
            else:
                de_o[0, at, flanes] = (de_o[0, at, flanes] + dq) * f[0, at, flanes].astype(F32)
                de_o[1, at, flanes] = (de_o[1, at, flanes] + dk) * f[1, at, flanes].astype(F32)
        return 0

    lax.fori_loop(0, rows // TILE, heads, 0)


def score_bwd(seg, low, hi, lo, vals, f):
    rows = low.shape[0]
    outs = (jax.ShapeDtypeStruct((2, rows, HEADS * FEAT), F32),)
    return call(score_bwd_kernel, "score_bwd", (seg, low, hi, lo, vals, f), outs, [pltpu.VMEM((rows, 128), F32)], 12, 0, 1380000000)[0]


def key_bwd_kernel(place, de, s, rot, proj, normT, send_o, keep_o, grads_o, vec):
    c = place[2]
    rows = s.shape[1]
    width = s.shape[2]
    half = width // 2
    p_wide, blocks = block_projection(proj)
    p_hi, p_lo = split(p_wide)

    def back(i, _):
        at = pl.ds(pl.multiple_of(i * TILE, TILE), TILE)
        cos, sin_a, sin_b = rot[at, 0:128], rot[at, 128:256], rot[at, 256:384]
        for which in range(2):
            for gr in range(width // 256):
                d_hi, d_lo = split(de[which, at, 128 * gr:128 * gr + 128])
                s_at = s[which, at, 256 * gr:256 * gr + 256].astype(F32)
                ds = nt(d_hi, p_hi) + nt(d_lo, p_hi) + nt(d_hi, p_lo) - s_at * (nt(d_hi, blocks) + nt(d_lo, blocks))
                for k in range(2):
                    du = turn_back(ds[:, 128 * k:128 * k + 128], cos, sin_a, sin_b)
                    lanes = slice(256 * gr + 128 * k, 256 * gr + 128 * k + 128)
                    grads_o[which, at, lanes] = du.astype(BF16)
        return 0

    lax.fori_loop(0, rows // TILE, back, 0)
    vec[...] = jnp.zeros_like(vec)
    for which in range(2):
        vec[4 + which:5 + which, :] = jnp.sum(grads_o[which].astype(F32), 0, keepdims=True)
        keep_o[which] = nn(normT[pl.ds(pl.multiple_of(c * half, half), half), :], grads_o[which]).astype(BF16)
        send_o[which] = nn(normT[pl.ds(pl.multiple_of((1 - c) * half, half), half), :], grads_o[which]).astype(BF16)


def key_bwd(place, de, s, rot, proj, normT):
    width, rows = normT.shape
    sd = jax.ShapeDtypeStruct
    outs = (
        sd((2, width // 2, width), BF16),
        sd((2, width // 2, width), BF16),
        sd((2, rows, width), BF16),
        sd((16, width), F32),
    )
    return call(key_bwd_kernel, "key_bwd", (place, de, s, rot, proj, normT), outs, [], 12, 0, 460000000, smem=1)


def token_bwd_kernel(slopes, which, grads, gv, mg, fg, *refs):
    vecs, slope, refs = refs[:3], refs[3:3 + slopes], refs[3 + slopes:]
    tok_i, wq_i, wk_i, wv_i, gtok_o, vec, tok, wq, wk, wv, sems = refs
    feed = Feed([(tok_i, tok), (wv_i, wv), (wq_i, wq), (wk_i, wk)], sems)
    feed.need(0)
    hat, scale = norm_parts(tok[...].astype(F32))
    feed.need(1)
    ng = nt(gv[...], wv[...])
    feed.need()
    ng = ng + nt(grads[0], wq[...]) + nt(grads[1], wk[...])
    vec[...] = jnp.zeros_like(vec)
    vec[0:16, :] = vecs[0][...] + vecs[1][...] + vecs[2][...]
    vec[7:8, :] = jnp.sum(ng * hat, 0, keepdims=True)
    vec[8:9, :] = jnp.sum(ng, 0, keepdims=True)
    for n in range(slopes):
        vec[pl.ds(16 + which[n], 1), :] = slope[n][...]
    gtok_o[...] = (mg[...] + norm_back(ng, hat, scale, fg[...])).astype(BF16)


def token_bwd(which, grads, gv, mg, fg, vecs, slopes, tok, wq, wk, wv):
    rows, width = tok.shape
    n = len(slopes)
    sd, v = jax.ShapeDtypeStruct, pltpu.VMEM
    outs = (sd((rows, width), BF16), sd((16 + -(-n // 8) * 8, width), F32))
    ins = (which, grads, gv, mg, fg) + tuple(vecs) + tuple(slopes) + (tok, wq, wk, wv)
    return call(partial(token_bwd_kernel, n), "token_bwd", ins, outs,
                [v((rows, width), BF16)] + [v((width, width), BF16)] * 3, TOKEN_LIMIT, 4, 460_000_000, smem=1, far=range(len(ins) - 4, len(ins)))


def pack_kernel(place, wu, wd, bu, out, sems):
    quarter = wu.shape[1] // 4
    x, y, c = place[0], place[1], place[2]
    feed = Feed([
        (wu.at[pl.ds(pl.multiple_of((2 * x + c) * quarter, quarter), quarter)], out.at[pl.ds(0, quarter)]),
        (wd.at[pl.ds(pl.multiple_of((2 * y + c) * quarter, quarter), quarter)], out.at[pl.ds(quarter, quarter)]),
    ], sems)
    left, parts = bu[...], []
    for _ in range(3):
        parts.append(left.astype(BF16).astype(F32))
        left = left - parts[-1]
    parts.append(jnp.zeros((13, left.shape[1]), F32))
    out[2 * quarter:2 * quarter + 16, :] = jnp.concatenate(parts, 0).astype(BF16)
    feed.need()


def pack(place, wu, wd, bu):
    width = wu.shape[1]
    outs = (jax.ShapeDtypeStruct((width // 2 + 16, width), BF16),)
    return call(pack_kernel, "pack", (place, wu, wd, bu), outs, [], 58, 2, 115000000, smem=1, far=(1, 2))[0]


def split_kernel(items, place, *refs):
    send, own = refs[-2:]
    step = send.shape[1]
    for n, (side, terms) in enumerate(items):
        here = place[side]
        for out, at in ((send, 1 - here), (own, here)):
            rows = pl.ds(pl.multiple_of(at * step, step), step)
            total = None
            for m, e in terms:
                term = (refs[m][rows, :] if e is None else refs[m][e, rows, :]).astype(F32)
                total = term if total is None else total + term
            out[n] = total.astype(BF16)


def split_sums(place, *sums):
    arrays, items = [], []
    for side, *terms in sums:
        at = []
        for v, e in terms:
            m = next((n for n, u in enumerate(arrays) if u is v), len(arrays))
            if m == len(arrays):
                arrays.append(v)
            at.append((m, e))
        items.append((side, tuple(at)))
    rows, width = arrays[0].shape[-2:]
    outs = (jax.ShapeDtypeStruct((len(sums), rows // 2, width), BF16),) * 2
    return call(partial(split_kernel, tuple(items)), "split_sums", (place,) + tuple(arrays), outs, [], 8, 0, 100_000_000, smem=1)


def finish_kernel(woven, place, mine, got, *refs):
    n = mine.shape[0]
    outs, refs = refs[:n], refs[n:]
    held, sems = refs
    c = place[2]
    rows = mine.shape[1]
    feed = Feed([], sems)
    cut = FFN_STEP // 2
    for m in range(n):
        for side, (ref, core) in enumerate(((mine, c), (got, 1 - c))):
            held[m, side] = ref[m].astype(F32)
            if woven[m]:
                for k in range(rows // cut):
                    feed.add(held.at[m, side, pl.ds(k * cut, cut)], outs[m].at[pl.ds(pl.multiple_of(2 * k * cut + core * cut, cut), cut)])
            else:
                feed.add(held.at[m, side], outs[m].at[pl.ds(pl.multiple_of(core * rows, rows), rows)])
    feed.need()


def finish(place, mine, got, woven):
    n, rows, width = mine.shape
    outs = (jax.ShapeDtypeStruct((2 * rows, width), F32),) * n
    return call(partial(finish_kernel, woven), "finish", (place, mine, got), outs, [pltpu.VMEM((n, 2, rows, width), F32)], 20,
                sum(2 * (rows // (FFN_STEP // 2) if w else 1) for w in woven), 230000000, smem=1, far_out=range(n))


def add_low(*parts):
    total = parts[0].astype(F32)
    for part in parts[1:]:
        total = total + part.astype(F32)
    return total.astype(parts[0].dtype)


def ordered(first, then):
    return lax.optimization_barrier((first, then))[1]


class Links:
    def __init__(self, first):
        self.dp, self.ring = lax.axis_size("dp"), lax.axis_size("tensor")
        at, z = lax.axis_index("dp"), lax.axis_index("tensor")
        self.bits = [1 << n for n in range(1, self.dp.bit_length() - 1)]
        order = [1] + self.bits
        sides = [(at // bit) % 2 for bit in order]
        place = jnp.stack([sides[1], sides[-1], sides[0]]).astype(jnp.int32)
        steps = jnp.arange(self.ring, dtype=jnp.int32)
        which = (z - steps) % self.ring
        low, self.place, self.which, self.mine, self.first = lax.optimization_barrier(
            ([side == 0 for side in sides], place, which, (steps == z).astype(F32)[:, None], first))
        self.low = dict(zip(order, low))

    def swap(self, v, bit):
        return lax.ppermute(v, "dp", [(i, i ^ bit) for i in range(self.dp)])

    def shift(self, v, by=1):
        return lax.ppermute(v, "tensor", [(i, (i + by) % self.ring) for i in range(self.ring)])

    def near(self, v, bit):
        return lax.ppermute(v, "tensor", [(i, i ^ bit) for i in range(self.ring)])

    def join(self, v, got, bit):
        low = self.low[bit]
        return jnp.concatenate([jnp.where(low, v, got), jnp.where(low, got, v)], v.ndim - 2)


def fence(*values):
    return lax.optimization_barrier(values)


class Joins:
    def __init__(self, links, a, b):
        self.links, self.vals, self.level = links, [a, b], len(links.bits)

    def bits(self):
        return self.links.bits[self.level], self.links.bits[::-1][self.level]

    def send(self):
        self.level -= 1
        return [self.links.swap(v, bit) for v, bit in zip(self.vals, self.bits())]

    def take(self, got):
        self.vals = [self.links.join(v, g, bit) for v, g, bit in zip(self.vals, got, self.bits())]
        return self.vals

    def rest(self, left):
        while self.level > left:
            self.take(self.send())
        return self.vals


def halve(links, v, bit):
    rows = v.shape[-2] // 2
    first, second = v[..., :rows, :], v[..., rows:, :]
    low = links.low[bit]
    return add_low(jnp.where(low, first, second), links.swap(jnp.where(low, second, first), bit))


def body(tokens, cotangent, segment, projection, first_gain, first_bias, w_query, w_key, w_value, w_out,
         b_query, b_key, b_value, b_out, second_gain, second_bias, w_up, b_up, w_down, b_down):
    links = Links(tokens)
    tokens, place = links.first, links.place
    rows, width = tokens.shape
    low_bit, top_bit = links.bits[0], links.bits[-1]
    order = [low_bit, top_bit] + links.bits[1:-1]
    core_low = links.low[1]
    quarter = width // 4

    def line(v):
        return v.reshape(1, -1)

    share = links.shift(pack(place, w_up, w_down, line(b_up)))
    table = jnp.asarray(rotary_table(256))
    normed, s, f, vals, rot, c0, ctx, dinv, mid, second = attn_fwd(
        tokens, segment, table, projection, line(first_gain), line(first_bias), w_query, w_key, w_value, w_out,
        line(b_query), line(b_key), line(b_value), line(b_out), line(second_gain), line(second_bias))

    def beside(share):
        return links.swap(share[:quarter], low_bit), links.swap(share[quarter:2 * quarter], top_bit)

    def own_ffn(first, last, parts, acc):
        ins = (line(b_up), mid, line(b_down), w_up, w_down) if first else parts + acc
        return ffn(first, last, place, second, cotangent, *ins)

    share, second = fence(share, second)
    swapped, coming = beside(share), links.shift(share)
    out, sgrad, send, keep, slope = own_ffn(True, False, (), ())
    swapped, out, send = fence(swapped, out, send)
    slopes, keeps, sends = [slope], [keep], [send]
    across = tuple(links.swap(v, 1) for v in (share,) + swapped)
    for n in range(1, links.ring):
        last = n == links.ring - 1
        parts = (share,) + swapped + across
        if not last:
            parts, share, out = fence(parts, coming, out)
            swapped = beside(share)
            coming = links.shift(share) if n < links.ring - 2 else share
        sends[-1] = links.swap(sends[-1], 1)
        if last:
            up_send, up_own = split_sums(place, *[(0, (keeps[k], 0), (sends[k], 0)) for k in range(2)])
            up_send, up_own, down, out = fence(up_send, up_own, add_low(keeps[1][1], sends[1][1]), out)
            up_got, down = links.swap(up_send, low_bit), links.shift(down)
        out, sgrad, send, keep, slope = own_ffn(False, last, parts, (out, sgrad))
        slopes.append(slope)
        keeps.append(keep)
        sends.append(send)
        if not last:
            swapped, coming, out = fence(swapped, coming, out)
            across = tuple(links.swap(v, 1) for v in (share,) + swapped)
            across, sends[-1] = fence(across, sends[-1])

    sgrad, up_got, down, send = fence(sgrad, up_got, down, sends[-1])
    sends[-1] = links.swap(send, 1)
    send_o, keep_o, low, hi, lo, mg, vec_o = out_bwd(
        place, sgrad, mid, line(second_gain), cotangent, ctx, dinv, c0, w_out)
    low, sends = fence(low, sends)
    up_send, up_more = split_sums(place, *[(0, (keeps[k], 0), (sends[k], 0)) for k in range(2, links.ring)])
    low, up_send, up_more, down = fence(low, up_send, up_more, add_low(down, keeps[2][1], sends[2][1]))
    down, up_last = links.shift(down), links.swap(up_send, low_bit)
    far_o = links.swap(send_o, 1)
    send_v, keep_v, gv, normT, vec_v = value_bwd(place, segment, low, f, normed)
    gv, low, down, up_last, send_v = fence(gv, low, down, up_last, send_v)
    far_v = links.swap(send_v, 1)
    up_send, up_own = split_sums(
        place, *[(1, (up_own, n), (up_got, n)) for n in range(2)], *[(1, (up_more, n), (up_last, n)) for n in range(links.ring - 2)])
    far_o, far_v, up_send, up_own, down, low = fence(far_o, far_v, up_send, up_own, add_low(down, keeps[3][1], sends[3][1]), low)
    ov_send, ov_own = split_sums(place, (0, (keep_v, None), (far_v, None)), (0, (keep_o, None), (far_o, None)))
    ov_send, ov_own, low = fence(ov_send, ov_own, low)
    down, up_got, ov_got = links.shift(down), links.swap(up_send, order[1]), links.swap(ov_send, low_bit)
    de = score_bwd(segment, low, hi, lo, vals, f)
    de, down, up_got, ov_got = fence(de, down, up_got, ov_got)
    for n in range(4, links.ring):
        down = links.shift(add_low(down, keeps[n][1], sends[n][1]))
    ov_send, ov_own = split_sums(place, *[(1, (ov_own, n), (ov_got, n)) for n in range(2)])
    down_send, down_own = split_sums(place, (0, (down, None), (keeps[0], 1), (sends[0], 1)))
    up = add_low(up_own, up_got)
    for bit in order[2:]:
        up = halve(links, up, bit)
    ov_send, ov_own, down_send, down_own, up, de = fence(ov_send, ov_own, down_send, down_own, up, de)
    ov_got, up_way, down_got = links.swap(ov_send, order[1]), links.shift(up[1]), links.swap(down_send, low_bit)
    send_k, keep_k, grads, vec_k = key_bwd(place, de, s, rot, projection, normT)
    ov_got, up_way, down_got, send_k, grads = fence(ov_got, up_way, down_got, send_k, grads)

    far_k = links.swap(send_k, 1)
    ov = add_low(ov_own, ov_got)
    for bit in order[2:]:
        ov = halve(links, ov, bit)
    ov_got = links.near(ov, 1)
    down_send, down_own = split_sums(place, (1, (down_own, 0), (down_got, 0)))
    far_k, down_send, down_own, up_way, grads = fence(far_k, down_send, down_own, add_low(up_way, up[2]), grads)
    qk_send, qk_own = split_sums(place, *[(n, (keep_k, n), (far_k, n)) for n in range(2)])
    qk_send, qk_own, grads = fence(qk_send, qk_own, grads)
    way_a, way_b = [low_bit, top_bit], [top_bit, low_bit]

    def both_ways(v, level):
        return links.swap(v[0], way_a[level]), links.swap(v[1], way_b[level])

    got_qk = both_ways(qk_send, 0)
    down_got, up_way = links.swap(down_send, order[1]), links.shift(up_way)
    ov_got, grads = fence(ov_got, grads)
    ov, grads = fence(add_low(ov, ov_got), grads)
    ov_got = links.near(ov, 2)
    gtok, vec = token_bwd(links.which, grads, gv, mg, line(first_gain), (vec_o, vec_v, vec_k), slopes, tokens, w_query, w_key, w_value)
    got_qk, up_way, down_got, vec = fence(got_qk, up_way, down_got, vec)

    qk_send, qk_own = split_sums(place, *[(1 - n, (qk_own, n), (got_qk[n], None)) for n in range(2)])
    down = add_low(down_own, down_got)
    for bit in order[2:]:
        down = halve(links, down, bit)
    qk_send, qk_own, up_way, down = fence(qk_send, qk_own, add_low(up_way, up[3]), down[0])
    got_qk = both_ways(qk_send, 1)
    up_way = links.shift(up_way)
    got_vec = links.swap(vec, 1)
    got_qk, up_way, got_vec, ov_got = fence(got_qk, up_way, got_vec, ov_got)

    qk = jnp.stack([add_low(qk_own[n], got_qk[n]) for n in range(2)])
    for bit in order[2:]:
        qk = halve(links, qk, bit)
    for n in range(4, links.ring):
        up_way = links.shift(add_low(up_way, up[n]))
    qk, vec, ff, ov = fence(qk, vec + got_vec, jnp.stack([add_low(up_way, up[0]), down]), add_low(ov, ov_got))
    got_qk = links.near(qk, 1)
    some = jnp.concatenate([ff, ov])
    for bit in order[:1:-1]:
        some = links.join(some, links.swap(some, bit), bit)
    some_got = links.swap(some, order[1])
    got_vec = links.swap(vec, low_bit)
    got_qk, some_got, got_vec = fence(got_qk, some_got, got_vec)

    qk, vec, some = fence(add_low(qk, got_qk), vec + got_vec, links.join(some, some_got, order[1]))
    got_qk = links.near(qk, 2)
    some_got = links.swap(some, low_bit)
    got_vec = links.swap(vec, order[1])
    got_qk, got_vec = fence(got_qk, got_vec)

    qk = add_low(qk, got_qk)
    for bit in order[:1:-1]:
        qk = links.join(qk, links.swap(qk, bit), bit)
    qk, vec = fence(qk, vec + got_vec)
    got_qk = both_ways(qk, 1)
    for bit in order[2:]:
        vec = vec + links.swap(vec, bit)
    got_vec = links.near(vec, 1)
    got_qk, some_got, got_vec = fence(got_qk, some_got, got_vec)

    qk = [links.join(qk[n], got_qk[n], (way_a, way_b)[n][1]) for n in range(2)]
    qk, vec, some = fence(qk, vec + got_vec, links.join(some, some_got, low_bit))
    got_qk = both_ways(qk, 0)
    got_vec = links.near(vec, 2)
    some_got = links.swap(some, 1)
    some, some_got = fence(some, some_got)
    grad_w_up, grad_w_down, grad_w_value, grad_w_out = finish(place, some, some_got, (False, True, False, False))
    got_qk, got_vec, grad_w_up, grad_w_down, grad_w_value, grad_w_out = fence(
        got_qk, got_vec, grad_w_up, grad_w_down, grad_w_value, grad_w_out)

    vec = vec + got_vec
    qk = jnp.stack([links.join(qk[n], got_qk[n], (way_a, way_b)[n][0]) for n in range(2)])
    grad_w_query, grad_w_key = finish(place, qk, links.swap(qk, 1), (False, False))

    grad_b_up = jnp.sum(vec[16:16 + links.ring] * links.mine, 0)
    return (
        out, gtok, vec[7], vec[8], grad_w_query, grad_w_key, grad_w_value, grad_w_out,
        vec[4], vec[5], vec[6], vec[3], vec[0], vec[1], grad_w_up, grad_b_up, grad_w_down, vec[2],
    )


def solution(mesh):
    rows = P(("dp", "tensor"), None)
    whole = P()
    return jax.shard_map(
        body,
        mesh=mesh,
        in_specs=(rows,) * 3 + (whole,) * 13 + (P(None, "tensor"), P("tensor"), P("tensor", None), whole),
        out_specs=(rows,) * 2 + (whole,) * 12 + (P(None, "tensor"), P("tensor"), P("tensor", None), whole),
        check_vma=False,
    )
```

```python
from functools import partial
import math

import jax
import jax.numpy as jnp
import ml_dtypes
import numpy as np
from jax import lax
from jax.experimental import pallas as pl
from jax.experimental.pallas import tpu as pltpu
from jax.sharding import PartitionSpec as P

HEADS = 12
HD = 64
FEAT = 32
EPS = 1e-05
F32 = jnp.float32
BF16 = jnp.bfloat16
ANY = pl.BlockSpec(memory_space=pltpu.HBM)
VM = pl.BlockSpec(memory_space=pltpu.VMEM)
SMEM = pl.BlockSpec(memory_space=pltpu.SMEM)
SCALE = HD ** -0.25


def nn(a, b):
    return lax.dot_general(a, b, (((1,), (0,)), ((), ())), preferred_element_type=F32)


def nt(a, b):
    return lax.dot_general(a, b, (((1,), (1,)), ((), ())), preferred_element_type=F32)


def split(v):
    high = v.astype(BF16)
    return high, (v - high.astype(F32)).astype(BF16)


def rotary_table(length):
    half = HD // 2
    rate = np.exp(np.arange(half) * (-2.0 * math.log(10000.0) / HD))
    angle = np.arange(length)[:, None] * rate[None, :]
    lane = np.arange(128)
    cos = np.tile(np.cos(angle), (1, 4)) * SCALE
    sin = np.tile(np.sin(angle), (1, 4)) * SCALE
    first = (lane % HD < half)[None, :]
    table = np.concatenate([cos, -sin * first, sin * ~first], 1).astype(np.float32)
    parts = []
    for _ in range(3):
        part = table.astype(ml_dtypes.bfloat16)
        parts.append(part)
        table = table - part.astype(np.float32)
    return np.stack(parts)


def lane_mask(head_in_group):
    lane = lax.broadcasted_iota(jnp.int32, (1, 128), 1)
    return jnp.where(lane // FEAT == head_in_group, 1.0, 0.0).astype(BF16)


def norm_parts(v):
    centred = v - jnp.mean(v, -1, keepdims=True)
    scale = lax.rsqrt(jnp.mean(centred * centred, -1, keepdims=True) + EPS)
    return centred * scale, scale


def norm_back(grad, hat, scale, gain):
    hat_grad = grad * gain
    return scale * (
        hat_grad
        - jnp.mean(hat_grad, -1, keepdims=True)
        - hat * jnp.mean(hat_grad * hat, -1, keepdims=True)
    )


def label_column(seg):
    rows = seg.shape[1]
    return jnp.transpose(jnp.broadcast_to(seg[...].astype(F32), (128, rows)))


def block_projection(proj):
    tall = jnp.concatenate([proj[...]] * 4, axis=0)
    wide = jnp.concatenate([tall] * 4, axis=1)
    group = lax.broadcasted_iota(jnp.int32, (256, 128), 0) // HD
    feat = lax.broadcasted_iota(jnp.int32, (256, 128), 1) // FEAT
    return jnp.where(group == feat, wide, 0.0), jnp.where(group == feat, 1.0, 0.0).astype(BF16)


def turn(u, cos, sin_a, sin_b):
    return u * cos + pltpu.roll(u, 96, 1) * sin_a + pltpu.roll(u, 32, 1) * sin_b


def turn_back(u, cos, sin_a, sin_b):
    return u * cos - pltpu.roll(u, 96, 1) * sin_a - pltpu.roll(u, 32, 1) * sin_b


class Feed:
    def __init__(self, pairs, sems):
        self.sems, self.copies, self.left = sems, [], []
        for src, dst in pairs:
            self.add(src, dst)

    def add(self, src, dst):
        copy = pltpu.make_async_copy(src, dst, self.sems.at[len(self.copies)])
        copy.start()
        self.left.append(len(self.copies))
        self.copies.append(copy)

    def need(self, *which):
        for n in which or list(self.left):
            if n in self.left:
                self.copies[n].wait()
                self.left.remove(n)


def call(kernel, name, ins, outs, scratch, limit, sems, flops, smem=0, far=(), far_out=(), alias=None):
    return pl.pallas_call(
        kernel,
        out_shape=outs,
        in_specs=[SMEM if n < smem else ANY if n in far else VM for n in range(len(ins))],
        out_specs=[ANY if n in far_out else VM for n in range(len(outs))],
        scratch_shapes=list(scratch) + ([pltpu.SemaphoreType.DMA((sems,))] if sems else []),
        input_output_aliases=alias or {},
        compiler_params=pltpu.CompilerParams(vmem_limit_bytes=limit << 20),
        cost_estimate=pl.CostEstimate(flops=flops, bytes_accessed=1000, transcendentals=0),
        name=name,
    )(*ins)


TILE = 256
TOKEN_LIMIT = 44


def attn_fwd_kernel(seg, fg, fb, bq, bk, bv, bo, sg, sb, proj, tok_i, wv_i, wq_i, tab_i, wk_i, wo_i,
                    normed_i, s_i, f_i, v_i, rot_i, c0_o, ctx_o, dinv_o, mid_o, sec_o,
                    col_s, normed_o, s_o, f_o, v_o, rot_o, tok, wv, wq, tab, wk, wo, sems):
    feed = Feed([(tab_i, tab), (tok_i, tok), (wv_i, wv), (wq_i, wq), (wk_i, wk), (wo_i, wo)], sems)
    rows, width = tok.shape
    col_s[...] = label_column(seg)
    seg_row = seg[...].astype(F32)
    less = jnp.where(seg_row < col_s[:, :1], 1.0, 0.0)
    start = jnp.sum(less, axis=1, keepdims=True)
    place = lax.broadcasted_iota(jnp.int32, (rows, 1), 0).astype(F32) - start
    length = tab.shape[1]
    ladder = lax.broadcasted_iota(jnp.int32, (rows, length), 1).astype(F32)
    one_hot = jnp.where(ladder == place, 1.0, 0.0).astype(BF16)
    p_wide, blocks = block_projection(proj)
    p_hi, p_lo = split(p_wide)
    halves = blocks * 0.5
    feed.need(0)
    rot_o[...] = nn(one_hot, tab[0]) + nn(one_hot, tab[1]) + nn(one_hot, tab[2])
    feed.need(1, 2)

    def first(i, _):
        at = pl.ds(pl.multiple_of(i * TILE, TILE), TILE)
        x = tok[at, :].astype(F32)
        hat, _scale = norm_parts(x)
        normed = (hat * fg[...] + fb[...]).astype(BF16)
        normed_o[at, :] = normed
        v_o[at, :] = nn(normed, wv[...]).astype(BF16)
        return 0

    lax.fori_loop(0, rows // TILE, first, 0)

    def rotated(i, which, w, b):
        at = pl.ds(pl.multiple_of(i * TILE, TILE), TILE)
        cos, sin_a, sin_b = rot_o[at, 0:128], rot_o[at, 128:256], rot_o[at, 256:384]
        u = nn(normed_o[at, :], w[...]) + b[...]
        for g in range(width // 256):
            s = jnp.concatenate([turn(u[:, k:k + 128], cos, sin_a, sin_b) for k in (256 * g, 256 * g + 128)], 1)
            s_hi, s_lo = split(s)
            s_o[which, at, 256 * g:256 * g + 256] = s_hi
            q_hi, q_lo = split(s * s)
            e = nn(s_hi, p_hi) + nn(s_lo, p_hi) + nn(s_hi, p_lo) - nn(q_hi, halves) - nn(q_lo, halves)
            f_o[which, at, 128 * g:128 * g + 128] = (jnp.exp(e) * FEAT ** -0.5).astype(BF16)
        return 0

    feed.need(3)
    lax.fori_loop(0, rows // TILE, lambda i, _: rotated(i, 0, wq, bq), 0)
    feed.need(4)
    lax.fori_loop(0, rows // TILE, lambda i, _: rotated(i, 1, wk, bk), 0)
    feed.need()
    for held, kept in ((normed_o, normed_i), (s_o, s_i), (f_o, f_i), (v_o, v_i), (rot_o, rot_i)):
        feed.add(held, kept)

    ones = jnp.ones((rows, 128), BF16)
    even = lax.broadcasted_iota(jnp.int32, (1, 128), 1) < HD

    def second(i, _):
        at = pl.ds(pl.multiple_of(i * TILE, TILE), TILE)
        same = col_s[at, :1] == seg_row
        for j in range(HEADS // 2):
            g = j // 2
            vals = jnp.concatenate([v_o[:, 128 * j:128 * j + 128], ones], 1)
            qf = f_o[0, at, 128 * g:128 * g + 128]
            kf = f_o[1, :, 128 * g:128 * g + 128]
            res = []
            for h in range(2):
                scores = nt(qf * lane_mask(2 * (j % 2) + h), kf)
                weights = jnp.where(same, scores, 0.0).astype(BF16)
                res.append(nn(weights, vals))
            num = jnp.where(even, res[0][:, :128], res[1][:, :128])
            inv = 1.0 / jnp.where(even, res[0][:, 128:], res[1][:, 128:])
            lanes = slice(128 * j, 128 * j + 128)
            ctx = num * inv
            dinv_o[at, lanes] = inv
            c0_o[at, lanes] = ctx
            ctx_o[at, lanes] = (ctx + bv[:, lanes]).astype(BF16)
        middle = tok[at, :].astype(F32) + nn(ctx_o[at, :], wo[...]) + bo[...]
        mid_o[at, :] = middle
        hat, _scale = norm_parts(middle)
        sec_o[at, :] = (hat * sg[...] + sb[...]).astype(BF16)
        return 0

    lax.fori_loop(0, rows // TILE, second, 0)
    feed.need()


def attn_fwd(tok, seg, tab, proj, fg, fb, wq, wk, wv, wo, bq, bk, bv, bo, sg, sb):
    rows, width = tok.shape
    sd, v = jax.ShapeDtypeStruct, pltpu.VMEM
    outs = (
        sd((rows, width), BF16),
        sd((2, rows, width), BF16),
        sd((2, rows, HEADS * FEAT), BF16),
        sd((rows, width), BF16),
        sd((rows, 384), F32),
        sd((rows, width), F32),
        sd((rows, width), BF16),
        sd((rows, width), F32),
        sd((rows, width), F32),
        sd((rows, width), BF16),
    )
    near = (seg, fg, fb, bq, bk, bv, bo, sg, sb, proj)
    far = (tok, wv, wq, tab, wk, wo)
    scratch = [v((rows, 128), F32)] + [v(a.shape, a.dtype) for a in outs[:5] + far]
    return call(attn_fwd_kernel, "attn_fwd", near + far, outs, scratch, 52, len(far) + 5, 5520000000,
                far=range(len(near), len(near) + len(far)), far_out=range(5))


FFN_STEP = 256


def ffn_kernel(first, last, place, sec, cot, *refs):
    n_in = 5 if first else 8
    ins, refs = refs[:n_in], refs[n_in:]
    out_o, sg_o, send_o, keep_o, gb_o, wu, wd, secT, hidT, acc, sems = refs
    x, y, c = place[0], place[1], place[2]
    rows, width = sec.shape
    quarter, half = width // 4, width // 2

    def part(a, core):
        return pl.ds(pl.multiple_of((2 * a + core) * quarter, quarter), quarter)

    if first:
        bu, oacc, bd, wu_i, wd_i = ins
        feed = Feed([(wu_i, wu), (wd_i, wd)], sems)
        bias = bu[...]
        early = (0,)
    else:
        own, own_x, own_y, far, far_x, far_y, oacc, sacc = ins
        up, down = pl.ds(0, quarter), pl.ds(quarter, quarter)
        feed = Feed([
            (own.at[up], wu.at[part(x, c)]), (own_x, wu.at[part(1 - x, c)]),
            (far.at[up], wu.at[part(x, 1 - c)]), (far_x, wu.at[part(1 - x, 1 - c)]),
            (own.at[down], wd.at[part(y, c)]), (own_y, wd.at[part(1 - y, c)]),
            (far.at[down], wd.at[part(y, 1 - c)]), (far_y, wd.at[part(1 - y, 1 - c)]),
        ], sems)
        tail = own[2 * quarter:2 * quarter + 16, :].astype(F32)
        bias = tail[0:1, :] + tail[1:2, :] + tail[2:3, :]
        early = (0, 1, 2, 3)
    mine = pl.ds(pl.multiple_of(c * half, half), half)
    other = pl.ds(pl.multiple_of((1 - c) * half, half), half)
    secT[...] = jnp.transpose(sec[...])
    feed.need(*early)
    cut = FFN_STEP // 2
    for n, at in enumerate(range(0, width, FFN_STEP)):
        cs = slice(at, at + FFN_STEP)
        inner = nn(sec[...], wu[:, cs]) + bias[:, cs]
        cdf = 0.5 + 0.5 * lax.erf(inner * math.sqrt(0.5))
        slope = cdf + inner * (jnp.exp(-0.5 * inner * inner) * (1.0 / math.sqrt(2.0 * math.pi)))
        hidden = (inner * cdf).astype(BF16)
        feed.need()
        grad = (nt(cot[...], wd[cs, :]) * slope).astype(BF16)
        gb_o[:, cs] = jnp.sum(grad.astype(F32), 0, keepdims=True)
        more_out = nn(hidden, wd[cs, :])
        more_sg = nt(grad, wu[:, cs])
        if n == 0:
            acc[...] = oacc[...] + more_out + (bd[...] if first else 0.0)
            sg_o[...] = more_sg if first else sacc[...] + more_sg
        else:
            acc[...] += more_out
            sg_o[...] += more_sg
        hidT[...] = jnp.transpose(hidden)
        piece = slice(n * cut, n * cut + cut)
        keep_o[1, piece, :] = nn(hidT[pl.ds(pl.multiple_of(c * cut, cut), cut), :], cot[...]).astype(BF16)
        send_o[1, piece, :] = nn(hidT[pl.ds(pl.multiple_of((1 - c) * cut, cut), cut), :], cot[...]).astype(BF16)
        keep_o[0, :, cs] = nn(secT[mine, :], grad).astype(BF16)
        send_o[0, :, cs] = nn(secT[other, :], grad).astype(BF16)
    out_o[...] = acc[...].astype(out_o.dtype)


def ffn(first, last, place, sec, cot, *ins):
    rows, width = sec.shape
    sd, v = jax.ShapeDtypeStruct, pltpu.VMEM
    outs = (
        sd((rows, width), BF16 if last else F32),
        sd((rows, width), F32),
        sd((2, width // 2, width), BF16),
        sd((2, width // 2, width), BF16),
        sd((1, width), F32),
    )
    scratch = [v((width, width), BF16), v((width, width), BF16), v((width, rows), BF16), v((FFN_STEP, rows), BF16),
               v((rows, width), F32)]
    return call(partial(ffn_kernel, first, last), "ffn", (place, sec, cot) + ins, outs, scratch, 14, 8, 690000000, smem=1,
                far=(6, 7) if first else (), alias=None if first else {10: 1})


def out_bwd_kernel(place, sgrad, mid, sg, cot, ctx, dinv, c0, wo_i,
                   send_o, keep_o, low_o, hi_o, lo_o, mg_o, vec, wo, tr_s, cg_s, sems):
    feed = Feed([(wo_i, wo)], sems)
    c = place[2]
    rows, width = mid.shape
    half = width // 2
    tr_s[...] = jnp.transpose(ctx[...])
    hat, scale = norm_parts(mid[...])
    up = sgrad[...]
    vec[...] = jnp.zeros_like(vec)
    vec[0:1, :] = jnp.sum(up * hat, 0, keepdims=True)
    vec[1:2, :] = jnp.sum(up, 0, keepdims=True)
    g = cot[...].astype(F32)
    vec[2:3, :] = jnp.sum(g, 0, keepdims=True)
    mg = g + norm_back(up, hat, scale, sg[...])
    mg_o[...] = mg
    og = mg.astype(BF16)
    vec[3:4, :] = jnp.sum(og.astype(F32), 0, keepdims=True)
    feed.need()
    cg_s[...] = nt(og, wo[...])
    keep_o[...] = nn(tr_s[pl.ds(pl.multiple_of(c * half, half), half), :], og).astype(BF16)
    send_o[...] = nn(tr_s[pl.ds(pl.multiple_of((1 - c) * half, half), half), :], og).astype(BF16)
    for j in range(HEADS // 2):
        lanes = slice(128 * j, 128 * j + 128)
        low = (cg_s[:, lanes] * dinv[:, lanes]).astype(BF16)
        low_o[:, lanes] = low
        less = -(low.astype(F32) * c0[:, lanes])
        hi = less.astype(BF16)
        hi_o[:, lanes] = hi
        lo_o[:, lanes] = pltpu.roll(less - hi.astype(F32), 64, 1).astype(BF16)


def out_bwd(place, sgrad, mid, sg, cot, ctx, dinv, c0, wo):
    rows, width = mid.shape
    sd, v = jax.ShapeDtypeStruct, pltpu.VMEM
    outs = (
        sd((width // 2, width), BF16),
        sd((width // 2, width), BF16),
        sd((rows, width), BF16),
        sd((rows, width), BF16),
        sd((rows, width), BF16),
        sd((rows, width), F32),
        sd((16, width), F32),
    )
    scratch = [v((width, width), BF16), v((width, rows), BF16), v((rows, width), F32)]
    return call(out_bwd_kernel, "out_bwd", (place, sgrad, mid, sg, cot, ctx, dinv, c0, wo), outs, scratch, 12, 1, 575000000, smem=1, far=(8,))


def value_bwd_kernel(place, seg, low, f, normed, send_o, keep_o, gv_o, normT_o, vec, col_s):
    c = place[2]
    rows, width = low.shape
    half = width // 2
    col_s[...] = label_column(seg)
    seg_row = seg[...].astype(F32)
    lane = lax.broadcasted_iota(jnp.int32, (1, 128), 1)

    def heads(i, _):
        at = pl.ds(pl.multiple_of(i * TILE, TILE), TILE)
        same = col_s[at, :1] == seg_row
        for j in range(HEADS // 2):
            lanes = slice(128 * j, 128 * j + 128)
            flanes = slice(128 * (j // 2), 128 * (j // 2) + 128)
            res = []
            for h in range(2):
                fm = lane_mask(2 * (j % 2) + h)
                wT = jnp.where(same, nt(f[1, at, flanes] * fm, f[0, :, flanes]), 0.0).astype(BF16)
                res.append(nn(wT, low[:, lanes]))
            gv_o[at, lanes] = jnp.where(lane < HD, res[0], res[1]).astype(BF16)
        return 0

    lax.fori_loop(0, rows // TILE, heads, 0)
    normT_o[...] = jnp.transpose(normed[...])
    vec[...] = jnp.zeros_like(vec)
    vec[6:7, :] = jnp.sum(gv_o[...].astype(F32), 0, keepdims=True)
    keep_o[...] = nn(normT_o[pl.ds(pl.multiple_of(c * half, half), half), :], gv_o[...]).astype(BF16)
    send_o[...] = nn(normT_o[pl.ds(pl.multiple_of((1 - c) * half, half), half), :], gv_o[...]).astype(BF16)


def value_bwd(place, seg, low, f, normed):
    rows, width = low.shape
    sd, v = jax.ShapeDtypeStruct, pltpu.VMEM
    outs = (
        sd((width // 2, width), BF16),
        sd((width // 2, width), BF16),
        sd((rows, width), BF16),
        sd((width, rows), BF16),
        sd((16, width), F32),
    )
    return call(value_bwd_kernel, "value_bwd", (place, seg, low, f, normed), outs, [v((rows, 128), F32)], 12, 0, 920000000, smem=1)


def score_bwd_kernel(seg, low, hi, lo, vals, f, de_o, col_s):
    rows, width = low.shape
    col_s[...] = label_column(seg)
    seg_row = seg[...].astype(F32)
    ones = jnp.ones((rows, 128), BF16)
    lane = lax.broadcasted_iota(jnp.int32, (1, 128), 1)

    def heads(i, _):
        at = pl.ds(pl.multiple_of(i * TILE, TILE), TILE)
        same = col_s[at, :1] == seg_row
        for j in range(HEADS // 2):
            gr = j // 2
            lanes = slice(128 * j, 128 * j + 128)
            flanes = slice(128 * gr, 128 * gr + 128)
            v_all = jnp.concatenate([vals[:, lanes], ones], 1)
            v_at = jnp.concatenate([vals[at, lanes], ones[:TILE]], 1)
            qf_all, kf_all = f[0, :, flanes], f[1, :, flanes]
            dq, dk = None, None
            for h in range(2):
                fm = lane_mask(2 * (j % 2) + h).astype(F32)
                own = jnp.where(lane // HD == h, 1.0, 0.0).astype(BF16)
                rest = 1.0 - own

                def pair(span):
                    return jnp.concatenate([low[span, lanes] * own, hi[span, lanes] * own + lo[span, lanes] * rest], 1)

                dwT = jnp.where(same, nt(v_at, pair(slice(None))), 0.0).astype(BF16)
                gk = nn(dwT, qf_all) * fm
                dk = gk if dk is None else dk + gk
                dw = jnp.where(same, nt(pair(at), v_all), 0.0).astype(BF16)
                gq = nn(dw, kf_all) * fm
                dq = gq if dq is None else dq + gq
            if j % 2 == 0:
                de_o[0, at, flanes] = dq
                de_o[1, at, flanes] = dk
            else:
                de_o[0, at, flanes] = (de_o[0, at, flanes] + dq) * f[0, at, flanes].astype(F32)
                de_o[1, at, flanes] = (de_o[1, at, flanes] + dk) * f[1, at, flanes].astype(F32)
        return 0

    lax.fori_loop(0, rows // TILE, heads, 0)


def score_bwd(seg, low, hi, lo, vals, f):
    rows = low.shape[0]
    outs = (jax.ShapeDtypeStruct((2, rows, HEADS * FEAT), F32),)
    return call(score_bwd_kernel, "score_bwd", (seg, low, hi, lo, vals, f), outs, [pltpu.VMEM((rows, 128), F32)], 12, 0, 1380000000)[0]


def key_bwd_kernel(place, de, s, rot, proj, normT, send_o, keep_o, grads_o, vec):
    c = place[2]
    rows = s.shape[1]
    width = s.shape[2]
    half = width // 2
    p_wide, blocks = block_projection(proj)
    p_hi, p_lo = split(p_wide)

    def back(i, _):
        at = pl.ds(pl.multiple_of(i * TILE, TILE), TILE)
        cos, sin_a, sin_b = rot[at, 0:128], rot[at, 128:256], rot[at, 256:384]
        for which in range(2):
            for gr in range(width // 256):
                d_hi, d_lo = split(de[which, at, 128 * gr:128 * gr + 128])
                s_at = s[which, at, 256 * gr:256 * gr + 256].astype(F32)
                ds = nt(d_hi, p_hi) + nt(d_lo, p_hi) + nt(d_hi, p_lo) - s_at * (nt(d_hi, blocks) + nt(d_lo, blocks))
                for k in range(2):
                    du = turn_back(ds[:, 128 * k:128 * k + 128], cos, sin_a, sin_b)
                    lanes = slice(256 * gr + 128 * k, 256 * gr + 128 * k + 128)
                    grads_o[which, at, lanes] = du.astype(BF16)
        return 0

    lax.fori_loop(0, rows // TILE, back, 0)
    vec[...] = jnp.zeros_like(vec)
    for which in range(2):
        vec[4 + which:5 + which, :] = jnp.sum(grads_o[which].astype(F32), 0, keepdims=True)
        keep_o[which] = nn(normT[pl.ds(pl.multiple_of(c * half, half), half), :], grads_o[which]).astype(BF16)
        send_o[which] = nn(normT[pl.ds(pl.multiple_of((1 - c) * half, half), half), :], grads_o[which]).astype(BF16)


def key_bwd(place, de, s, rot, proj, normT):
    width, rows = normT.shape
    sd = jax.ShapeDtypeStruct
    outs = (
        sd((2, width // 2, width), BF16),
        sd((2, width // 2, width), BF16),
        sd((2, rows, width), BF16),
        sd((16, width), F32),
    )
    return call(key_bwd_kernel, "key_bwd", (place, de, s, rot, proj, normT), outs, [], 12, 0, 460000000, smem=1)


def token_bwd_kernel(slopes, which, grads, gv, mg, fg, *refs):
    vecs, slope, refs = refs[:3], refs[3:3 + slopes], refs[3 + slopes:]
    tok_i, wq_i, wk_i, wv_i, gtok_o, vec, tok, wq, wk, wv, sems = refs
    feed = Feed([(tok_i, tok), (wv_i, wv), (wq_i, wq), (wk_i, wk)], sems)
    feed.need(0)
    hat, scale = norm_parts(tok[...].astype(F32))
    feed.need(1)
    ng = nt(gv[...], wv[...])
    feed.need()
    ng = ng + nt(grads[0], wq[...]) + nt(grads[1], wk[...])
    vec[...] = jnp.zeros_like(vec)
    vec[0:16, :] = vecs[0][...] + vecs[1][...] + vecs[2][...]
    vec[7:8, :] = jnp.sum(ng * hat, 0, keepdims=True)
    vec[8:9, :] = jnp.sum(ng, 0, keepdims=True)
    for n in range(slopes):
        vec[pl.ds(16 + which[n], 1), :] = slope[n][...]
    gtok_o[...] = (mg[...] + norm_back(ng, hat, scale, fg[...])).astype(BF16)


def token_bwd(which, grads, gv, mg, fg, vecs, slopes, tok, wq, wk, wv):
    rows, width = tok.shape
    n = len(slopes)
    sd, v = jax.ShapeDtypeStruct, pltpu.VMEM
    outs = (sd((rows, width), BF16), sd((16 + -(-n // 8) * 8, width), F32))
    ins = (which, grads, gv, mg, fg) + tuple(vecs) + tuple(slopes) + (tok, wq, wk, wv)
    return call(partial(token_bwd_kernel, n), "token_bwd", ins, outs,
                [v((rows, width), BF16)] + [v((width, width), BF16)] * 3, TOKEN_LIMIT, 4, 460_000_000, smem=1, far=range(len(ins) - 4, len(ins)))


def pack_kernel(place, wu, wd, bu, out, sems):
    quarter = wu.shape[1] // 4
    x, y, c = place[0], place[1], place[2]
    feed = Feed([
        (wu.at[pl.ds(pl.multiple_of((2 * x + c) * quarter, quarter), quarter)], out.at[pl.ds(0, quarter)]),
        (wd.at[pl.ds(pl.multiple_of((2 * y + c) * quarter, quarter), quarter)], out.at[pl.ds(quarter, quarter)]),
    ], sems)
    left, parts = bu[...], []
    for _ in range(3):
        parts.append(left.astype(BF16).astype(F32))
        left = left - parts[-1]
    parts.append(jnp.zeros((13, left.shape[1]), F32))
    out[2 * quarter:2 * quarter + 16, :] = jnp.concatenate(parts, 0).astype(BF16)
    feed.need()


def pack(place, wu, wd, bu):
    width = wu.shape[1]
    outs = (jax.ShapeDtypeStruct((width // 2 + 16, width), BF16),)
    return call(pack_kernel, "pack", (place, wu, wd, bu), outs, [], 58, 2, 115000000, smem=1, far=(1, 2))[0]


def split_kernel(items, place, *refs):
    send, own = refs[-2:]
    step = send.shape[1]
    for n, (side, terms) in enumerate(items):
        here = place[side]
        for out, at in ((send, 1 - here), (own, here)):
            rows = pl.ds(pl.multiple_of(at * step, step), step)
            total = None
            for m, e in terms:
                term = (refs[m][rows, :] if e is None else refs[m][e, rows, :]).astype(F32)
                total = term if total is None else total + term
            out[n] = total.astype(BF16)


def split_sums(place, *sums):
    arrays, items = [], []
    for side, *terms in sums:
        at = []
        for v, e in terms:
            m = next((n for n, u in enumerate(arrays) if u is v), len(arrays))
            if m == len(arrays):
                arrays.append(v)
            at.append((m, e))
        items.append((side, tuple(at)))
    rows, width = arrays[0].shape[-2:]
    outs = (jax.ShapeDtypeStruct((len(sums), rows // 2, width), BF16),) * 2
    return call(partial(split_kernel, tuple(items)), "split_sums", (place,) + tuple(arrays), outs, [], 8, 0, 100_000_000, smem=1)


def finish_kernel(woven, place, *refs):
    n = len(woven)
    parts, outs, (held, sems) = refs[:2 * n], refs[2 * n:3 * n], refs[3 * n:]
    c = place[2]
    rows = held.shape[2]
    feed = Feed([], sems)
    cut = FFN_STEP // 2
    for m in range(n):
        for side, core in ((0, c), (1, 1 - c)):
            held[m, side] = parts[side * n + m][...].astype(F32)
            if woven[m]:
                for k in range(rows // cut):
                    feed.add(held.at[m, side, pl.ds(k * cut, cut)], outs[m].at[pl.ds(pl.multiple_of(2 * k * cut + core * cut, cut), cut)])
            else:
                feed.add(held.at[m, side], outs[m].at[pl.ds(pl.multiple_of(core * rows, rows), rows)])
    feed.need()


def finish(place, mine, got, woven):
    n = len(woven)
    rows, width = mine[0].shape
    outs = (jax.ShapeDtypeStruct((2 * rows, width), F32),) * n
    return call(partial(finish_kernel, woven), "finish", (place,) + tuple(mine) + tuple(got), outs,
                [pltpu.VMEM((n, 2, rows, width), F32)], 20,
                sum(2 * (rows // (FFN_STEP // 2) if w else 1) for w in woven), 230_000_000, smem=1, far_out=range(n))


def add_low(*parts):
    total = parts[0].astype(F32)
    for part in parts[1:]:
        total = total + part.astype(F32)
    return total.astype(parts[0].dtype)


def ordered(first, then):
    return lax.optimization_barrier((first, then))[1]


class Links:
    def __init__(self, first):
        self.dp, self.ring = lax.axis_size("dp"), lax.axis_size("tensor")
        at, z = lax.axis_index("dp"), lax.axis_index("tensor")
        self.bits = [1 << n for n in range(1, self.dp.bit_length() - 1)]
        order = [1] + self.bits
        sides = [(at // bit) % 2 for bit in order]
        place = jnp.stack([sides[1], sides[-1], sides[0]]).astype(jnp.int32)
        steps = jnp.arange(self.ring, dtype=jnp.int32)
        which = (z - steps) % self.ring
        low, self.place, self.which, self.mine, self.first = lax.optimization_barrier(
            ([side == 0 for side in sides], place, which, (steps == z).astype(F32)[:, None], first))
        self.low = dict(zip(order, low))

    def swap(self, v, bit):
        return lax.ppermute(v, "dp", [(i, i ^ bit) for i in range(self.dp)])

    def shift(self, v, by=1):
        return lax.ppermute(v, "tensor", [(i, (i + by) % self.ring) for i in range(self.ring)])

    def near(self, v, bit):
        return lax.ppermute(v, "tensor", [(i, i ^ bit) for i in range(self.ring)])

    def join(self, v, got, bit, axis=None):
        low = self.low[bit]
        axis = v.ndim - 2 if axis is None else axis
        if axis < v.ndim - 2 and v.shape[axis] > 1:
            v, got = jnp.expand_dims(v, axis), jnp.expand_dims(got, axis)
        return jnp.concatenate([jnp.where(low, v, got), jnp.where(low, got, v)], axis)


def fence(*values):
    return lax.optimization_barrier(values)


def halve(links, v, bit):
    rows = v.shape[-2] // 2
    first, second = v[..., :rows, :], v[..., rows:, :]
    low = links.low[bit]
    return add_low(jnp.where(low, first, second), links.swap(jnp.where(low, second, first), bit))


def body(tokens, cotangent, segment, projection, first_gain, first_bias, w_query, w_key, w_value, w_out,
         b_query, b_key, b_value, b_out, second_gain, second_bias, w_up, b_up, w_down, b_down):
    links = Links(tokens)
    tokens, place = links.first, links.place
    rows, width = tokens.shape
    low_bit, top_bit = links.bits[0], links.bits[-1]
    order = [low_bit, top_bit] + links.bits[1:-1]
    core_low = links.low[1]
    quarter = width // 4

    def line(v):
        return v.reshape(1, -1)

    share = links.shift(pack(place, w_up, w_down, line(b_up)))
    table = jnp.asarray(rotary_table(256))
    normed, s, f, vals, rot, c0, ctx, dinv, mid, second = attn_fwd(
        tokens, segment, table, projection, line(first_gain), line(first_bias), w_query, w_key, w_value, w_out,
        line(b_query), line(b_key), line(b_value), line(b_out), line(second_gain), line(second_bias))

    def beside(share):
        return links.swap(share[:quarter], low_bit), links.swap(share[quarter:2 * quarter], top_bit)

    def own_ffn(first, last, parts, acc):
        ins = (line(b_up), mid, line(b_down), w_up, w_down) if first else parts + acc
        return ffn(first, last, place, second, cotangent, *ins)

    share, second = fence(share, second)
    swapped, coming = beside(share), links.shift(share)
    out, sgrad, send, keep, slope = own_ffn(True, False, (), ())
    swapped, out, send = fence(swapped, out, send)
    slopes, keeps, sends = [slope], [keep], [send]
    across = tuple(links.swap(v, 1) for v in (share,) + swapped)
    for n in range(1, links.ring):
        last = n == links.ring - 1
        parts = (share,) + swapped + across
        if not last:
            parts, share, out = fence(parts, coming, out)
            swapped = beside(share)
            coming = links.shift(share) if n < links.ring - 2 else share
        sends[-1] = links.swap(sends[-1], 1)
        if last:
            up_send, up_own = split_sums(place, *[(0, (keeps[k], 0), (sends[k], 0)) for k in range(2)])
            up_send, up_own, down, out = fence(up_send, up_own, add_low(keeps[1][1], sends[1][1]), out)
            up_got, down = links.swap(up_send, low_bit), links.shift(down)
        out, sgrad, send, keep, slope = own_ffn(False, last, parts, (out, sgrad))
        slopes.append(slope)
        keeps.append(keep)
        sends.append(send)
        if not last:
            swapped, coming, out = fence(swapped, coming, out)
            across = tuple(links.swap(v, 1) for v in (share,) + swapped)
            across, sends[-1] = fence(across, sends[-1])

    sgrad, up_got, down, send = fence(sgrad, up_got, down, sends[-1])
    sends[-1] = links.swap(send, 1)
    send_o, keep_o, low, hi, lo, mg, vec_o = out_bwd(
        place, sgrad, mid, line(second_gain), cotangent, ctx, dinv, c0, w_out)
    low, sends = fence(low, sends)
    up_send, up_more = split_sums(place, *[(0, (keeps[k], 0), (sends[k], 0)) for k in range(2, links.ring)])
    low, up_send, up_more, down = fence(low, up_send, up_more, add_low(down, keeps[2][1], sends[2][1]))
    down, up_last = links.shift(down), links.swap(up_send, low_bit)
    far_o = links.swap(send_o, 1)
    send_v, keep_v, gv, normT, vec_v = value_bwd(place, segment, low, f, normed)
    gv, low, down, up_last, send_v = fence(gv, low, down, up_last, send_v)
    far_v = links.swap(send_v, 1)
    up_send, up_own = split_sums(
        place, *[(1, (up_own, n), (up_got, n)) for n in range(2)], *[(1, (up_more, n), (up_last, n)) for n in range(links.ring - 2)])
    far_o, far_v, up_send, up_own, down, low = fence(far_o, far_v, up_send, up_own, add_low(down, keeps[3][1], sends[3][1]), low)
    ov_send, ov_own = split_sums(place, (0, (keep_v, None), (far_v, None)), (0, (keep_o, None), (far_o, None)))
    ov_send, ov_own, low = fence(ov_send, ov_own, low)
    down, up_got, ov_got = links.shift(down), links.swap(up_send, order[1]), links.swap(ov_send, low_bit)
    de = score_bwd(segment, low, hi, lo, vals, f)
    de, down, up_got, ov_got = fence(de, down, up_got, ov_got)
    for n in range(4, links.ring):
        down = links.shift(add_low(down, keeps[n][1], sends[n][1]))
    ov_send, ov_own = split_sums(place, *[(1, (ov_own, n), (ov_got, n)) for n in range(2)])
    down_send, down_own = split_sums(place, (0, (down, None), (keeps[0], 1), (sends[0], 1)))
    up = add_low(up_own, up_got)
    for bit in order[2:]:
        up = halve(links, up, bit)
    ov_send, ov_own, down_send, down_own, up, de = fence(ov_send, ov_own, down_send, down_own, up, de)
    ov_got, up_way, down_got = links.swap(ov_send, order[1]), links.shift(up[1]), links.swap(down_send, low_bit)
    send_k, keep_k, grads, vec_k = key_bwd(place, de, s, rot, projection, normT)
    ov_got, up_way, down_got, send_k, grads = fence(ov_got, up_way, down_got, send_k, grads)

    far_k = links.swap(send_k, 1)
    ov = add_low(ov_own, ov_got)
    for bit in order[2:]:
        ov = halve(links, ov, bit)
    ov_got = links.near(ov, 1)
    down_send, down_own = split_sums(place, (1, (down_own, 0), (down_got, 0)))
    far_k, down_send, down_own, up_way, grads = fence(far_k, down_send, down_own, add_low(up_way, up[2]), grads)
    qk_send, qk_own = split_sums(place, *[(n, (keep_k, n), (far_k, n)) for n in range(2)])
    qk_send, qk_own, grads = fence(qk_send, qk_own, grads)
    way_a, way_b = [low_bit, top_bit], [top_bit, low_bit]

    def both_ways(v, level):
        return links.swap(v[0], way_a[level]), links.swap(v[1], way_b[level])

    got_qk = both_ways(qk_send, 0)
    down_got, up_way = links.swap(down_send, order[1]), links.shift(up_way)
    gtok, vec = token_bwd(links.which, grads, gv, mg, line(first_gain), (vec_o, vec_v, vec_k), slopes, tokens, w_query, w_key, w_value)
    got_qk, up_way, down_got, vec, ov_got = fence(got_qk, up_way, down_got, vec, ov_got)

    qk_send, qk_own = split_sums(place, *[(1 - n, (qk_own, n), (got_qk[n], None)) for n in range(2)])
    down = add_low(down_own, down_got)
    for bit in order[2:]:
        down = halve(links, down, bit)
    qk_send, qk_own, up_way, down, ov = fence(qk_send, qk_own, add_low(up_way, up[3]), down[0], add_low(ov, ov_got))
    got_qk = both_ways(qk_send, 1)
    up_way = links.shift(up_way)
    ov_got = links.near(ov, 2)
    got_vec = links.swap(vec, 1)
    got_qk, up_way, got_vec = fence(got_qk, up_way, got_vec)

    qk = jnp.stack([add_low(qk_own[n], got_qk[n]) for n in range(2)])
    for bit in order[2:]:
        qk = halve(links, qk, bit)
    for n in range(4, links.ring):
        up_way = links.shift(add_low(up_way, up[n]))
    def back_first(pair):
        for bit in order[:1:-1]:
            pair = [links.join(v, links.swap(v, bit), bit) for v in pair]
        return pair

    def one(pair):
        return links.swap(pair[0], order[1]), links.swap(pair[1], low_bit)

    def one_in(pair, got):
        return links.join(pair[0], got[0], order[1]), links.join(pair[1][None], got[1][None], low_bit, 0)

    def two(pair):
        return links.swap(pair[0], low_bit), links.swap(pair[1], order[1])

    def two_in(pair, got):
        return links.join(pair[0], got[0], low_bit), links.join(pair[1], got[1], order[1]).reshape(-1, width)

    def last(pair):
        return [links.swap(v, 1) for v in pair]

    def qk_in(pair, got, level):
        return [links.join(v, g, way[level]) for v, g, way in zip(pair, got, (way_a, way_b))]

    qk, vec, ff, ov = fence(qk, vec + got_vec, [add_low(up_way, up[0]), down], ov)
    got_qk = links.near(qk, 1)
    ff = back_first(ff)
    ff_got = one(ff)
    got_vec = links.swap(vec, low_bit)
    got_qk, ff_got, got_vec, ov_got = fence(got_qk, ff_got, got_vec, ov_got)

    qk, vec, ff, ov = fence(add_low(qk, got_qk), vec + got_vec, one_in(ff, ff_got), [add_low(ov[n], ov_got[n]) for n in range(2)])
    got_qk = links.near(qk, 2)
    ff_got = two(ff)
    ov = back_first(ov)
    ov_got = one(ov)
    got_vec = links.swap(vec, order[1])
    got_qk, ov_got, got_vec, ff_got = fence(got_qk, ov_got, got_vec, ff_got)

    qk = back_first([add_low(qk[n], got_qk[n]) for n in range(2)])
    qk, ov, vec, ff = fence(qk, one_in(ov, ov_got), vec + got_vec, two_in(ff, ff_got))
    got_qk = one(qk)
    ov_got = two(ov)
    ff_got = last(ff)
    for bit in order[2:]:
        vec = vec + links.swap(vec, bit)
    got_vec = links.near(vec, 1)
    got_qk, ff_got, got_vec = fence(got_qk, ff_got, got_vec)

    qk, vec = fence(qk_in(qk, got_qk, 1), vec + got_vec)
    got_qk = two(qk)
    got_vec = links.near(vec, 2)
    grad_w_up, grad_w_down = finish(place, ff, ff_got, (False, True))
    got_qk, ov_got, got_vec, grad_w_up, grad_w_down = fence(got_qk, ov_got, got_vec, grad_w_up, grad_w_down)

    qk, ov, vec = fence(qk_in(qk, got_qk, 0), two_in(ov, ov_got), vec + got_vec)
    got_qk, ov_got = last(qk), last(ov)
    got_qk, ov_got = fence(got_qk, ov_got)
    grad_w_query, grad_w_key, grad_w_value, grad_w_out = finish(place, [*qk, *ov], [*got_qk, *ov_got], (False,) * 4)

    grad_b_up = jnp.sum(vec[16:16 + links.ring] * links.mine, 0)
    return (
        out, gtok, vec[7], vec[8], grad_w_query, grad_w_key, grad_w_value, grad_w_out,
        vec[4], vec[5], vec[6], vec[3], vec[0], vec[1], grad_w_up, grad_b_up, grad_w_down, vec[2],
    )


def solution(mesh):
    rows = P(("dp", "tensor"), None)
    whole = P()
    return jax.shard_map(
        body,
        mesh=mesh,
        in_specs=(rows,) * 3 + (whole,) * 13 + (P(None, "tensor"), P("tensor"), P("tensor", None), whole),
        out_specs=(rows,) * 2 + (whole,) * 12 + (P(None, "tensor"), P("tensor"), P("tensor", None), whole),
        check_vma=False,
    )
```

```python
from functools import partial
import math

import jax
import jax.numpy as jnp
import ml_dtypes
import numpy as np
from jax import lax
from jax.experimental import pallas as pl
from jax.experimental.pallas import tpu as pltpu
from jax.sharding import PartitionSpec as P

HEADS = 12
HD = 64
FEAT = 32
EPS = 1e-05
F32 = jnp.float32
BF16 = jnp.bfloat16
ANY = pl.BlockSpec(memory_space=pltpu.HBM)
VM = pl.BlockSpec(memory_space=pltpu.VMEM)
SMEM = pl.BlockSpec(memory_space=pltpu.SMEM)
SCALE = HD ** -0.25


def nn(a, b):
    return lax.dot_general(a, b, (((1,), (0,)), ((), ())), preferred_element_type=F32)


def nt(a, b):
    return lax.dot_general(a, b, (((1,), (1,)), ((), ())), preferred_element_type=F32)


def split(v):
    high = v.astype(BF16)
    return high, (v - high.astype(F32)).astype(BF16)


def rotary_table(length):
    half = HD // 2
    rate = np.exp(np.arange(half) * (-2.0 * math.log(10000.0) / HD))
    angle = np.arange(length)[:, None] * rate[None, :]
    lane = np.arange(128)
    cos = np.tile(np.cos(angle), (1, 4)) * SCALE
    sin = np.tile(np.sin(angle), (1, 4)) * SCALE
    first = (lane % HD < half)[None, :]
    table = np.concatenate([cos, -sin * first, sin * ~first], 1).astype(np.float32)
    parts = []
    for _ in range(3):
        part = table.astype(ml_dtypes.bfloat16)
        parts.append(part)
        table = table - part.astype(np.float32)
    return np.stack(parts)


def lane_mask(head_in_group):
    lane = lax.broadcasted_iota(jnp.int32, (1, 128), 1)
    return jnp.where(lane // FEAT == head_in_group, 1.0, 0.0).astype(BF16)


def norm_parts(v):
    centred = v - jnp.mean(v, -1, keepdims=True)
    scale = lax.rsqrt(jnp.mean(centred * centred, -1, keepdims=True) + EPS)
    return centred * scale, scale


def norm_back(grad, hat, scale, gain):
    hat_grad = grad * gain
    return scale * (
        hat_grad
        - jnp.mean(hat_grad, -1, keepdims=True)
        - hat * jnp.mean(hat_grad * hat, -1, keepdims=True)
    )


def label_column(seg):
    rows = seg.shape[1]
    return jnp.transpose(jnp.broadcast_to(seg[...].astype(F32), (128, rows)))


def block_projection(proj):
    tall = jnp.concatenate([proj[...]] * 4, axis=0)
    wide = jnp.concatenate([tall] * 4, axis=1)
    group = lax.broadcasted_iota(jnp.int32, (256, 128), 0) // HD
    feat = lax.broadcasted_iota(jnp.int32, (256, 128), 1) // FEAT
    return jnp.where(group == feat, wide, 0.0), jnp.where(group == feat, 1.0, 0.0).astype(BF16)


def turn(u, cos, sin_a, sin_b):
    return u * cos + pltpu.roll(u, 96, 1) * sin_a + pltpu.roll(u, 32, 1) * sin_b


def turn_back(u, cos, sin_a, sin_b):
    return u * cos - pltpu.roll(u, 96, 1) * sin_a - pltpu.roll(u, 32, 1) * sin_b


class Feed:
    def __init__(self, pairs, sems):
        self.sems, self.copies, self.left = sems, [], []
        for src, dst in pairs:
            self.add(src, dst)

    def add(self, src, dst):
        copy = pltpu.make_async_copy(src, dst, self.sems.at[len(self.copies)])
        copy.start()
        self.left.append(len(self.copies))
        self.copies.append(copy)

    def need(self, *which):
        for n in which or list(self.left):
            if n in self.left:
                self.copies[n].wait()
                self.left.remove(n)


def call(kernel, name, ins, outs, scratch, limit, sems, flops, smem=0, far=(), far_out=(), alias=None):
    return pl.pallas_call(
        kernel,
        out_shape=outs,
        in_specs=[SMEM if n < smem else ANY if n in far else VM for n in range(len(ins))],
        out_specs=[ANY if n in far_out else VM for n in range(len(outs))],
        scratch_shapes=list(scratch) + ([pltpu.SemaphoreType.DMA((sems,))] if sems else []),
        input_output_aliases=alias or {},
        compiler_params=pltpu.CompilerParams(vmem_limit_bytes=limit << 20),
        cost_estimate=pl.CostEstimate(flops=flops, bytes_accessed=1000, transcendentals=0),
        name=name,
    )(*ins)


TILE = 256
TOKEN_LIMIT = 44


def attn_fwd_kernel(seg, fg, fb, bq, bk, bv, bo, sg, sb, proj, tok_i, wv_i, wq_i, tab_i, wk_i, wo_i,
                    normed_i, s_i, f_i, v_i, rot_i, c0_o, ctx_o, dinv_o, mid_o, sec_o,
                    col_s, normed_o, s_o, f_o, v_o, rot_o, tok, wv, wq, tab, wk, wo, sems):
    feed = Feed([(tab_i, tab), (tok_i, tok), (wv_i, wv), (wq_i, wq), (wk_i, wk), (wo_i, wo)], sems)
    rows, width = tok.shape
    col_s[...] = label_column(seg)
    seg_row = seg[...].astype(F32)
    less = jnp.where(seg_row < col_s[:, :1], 1.0, 0.0)
    start = jnp.sum(less, axis=1, keepdims=True)
    place = lax.broadcasted_iota(jnp.int32, (rows, 1), 0).astype(F32) - start
    length = tab.shape[1]
    ladder = lax.broadcasted_iota(jnp.int32, (rows, length), 1).astype(F32)
    one_hot = jnp.where(ladder == place, 1.0, 0.0).astype(BF16)
    p_wide, blocks = block_projection(proj)
    p_hi, p_lo = split(p_wide)
    halves = blocks * 0.5
    feed.need(0)
    rot_o[...] = nn(one_hot, tab[0]) + nn(one_hot, tab[1]) + nn(one_hot, tab[2])
    feed.need(1, 2)

    def first(i, _):
        at = pl.ds(pl.multiple_of(i * TILE, TILE), TILE)
        x = tok[at, :].astype(F32)
        hat, _scale = norm_parts(x)
        normed = (hat * fg[...] + fb[...]).astype(BF16)
        normed_o[at, :] = normed
        v_o[at, :] = nn(normed, wv[...]).astype(BF16)
        return 0

    lax.fori_loop(0, rows // TILE, first, 0)

    def rotated(i, which, w, b):
        at = pl.ds(pl.multiple_of(i * TILE, TILE), TILE)
        cos, sin_a, sin_b = rot_o[at, 0:128], rot_o[at, 128:256], rot_o[at, 256:384]
        u = nn(normed_o[at, :], w[...]) + b[...]
        for g in range(width // 256):
            s = jnp.concatenate([turn(u[:, k:k + 128], cos, sin_a, sin_b) for k in (256 * g, 256 * g + 128)], 1)
            s_hi, s_lo = split(s)
            s_o[which, at, 256 * g:256 * g + 256] = s_hi
            q_hi, q_lo = split(s * s)
            e = nn(s_hi, p_hi) + nn(s_lo, p_hi) + nn(s_hi, p_lo) - nn(q_hi, halves) - nn(q_lo, halves)
            f_o[which, at, 128 * g:128 * g + 128] = (jnp.exp(e) * FEAT ** -0.5).astype(BF16)
        return 0

    feed.need(3)
    lax.fori_loop(0, rows // TILE, lambda i, _: rotated(i, 0, wq, bq), 0)
    feed.need(4)
    lax.fori_loop(0, rows // TILE, lambda i, _: rotated(i, 1, wk, bk), 0)
    feed.need()
    for held, kept in ((normed_o, normed_i), (s_o, s_i), (f_o, f_i), (v_o, v_i), (rot_o, rot_i)):
        feed.add(held, kept)

    ones = jnp.ones((rows, 128), BF16)
    even = lax.broadcasted_iota(jnp.int32, (1, 128), 1) < HD

    def second(i, _):
        at = pl.ds(pl.multiple_of(i * TILE, TILE), TILE)
        same = col_s[at, :1] == seg_row
        for j in range(HEADS // 2):
            g = j // 2
            vals = jnp.concatenate([v_o[:, 128 * j:128 * j + 128], ones], 1)
            qf = f_o[0, at, 128 * g:128 * g + 128]
            kf = f_o[1, :, 128 * g:128 * g + 128]
            res = []
            for h in range(2):
                scores = nt(qf * lane_mask(2 * (j % 2) + h), kf)
                weights = jnp.where(same, scores, 0.0).astype(BF16)
                res.append(nn(weights, vals))
            num = jnp.where(even, res[0][:, :128], res[1][:, :128])
            inv = 1.0 / jnp.where(even, res[0][:, 128:], res[1][:, 128:])
            lanes = slice(128 * j, 128 * j + 128)
            ctx = num * inv
            dinv_o[at, lanes] = inv
            c0_o[at, lanes] = ctx
            ctx_o[at, lanes] = (ctx + bv[:, lanes]).astype(BF16)
        middle = tok[at, :].astype(F32) + nn(ctx_o[at, :], wo[...]) + bo[...]
        mid_o[at, :] = middle
        hat, _scale = norm_parts(middle)
        sec_o[at, :] = (hat * sg[...] + sb[...]).astype(BF16)
        return 0

    lax.fori_loop(0, rows // TILE, second, 0)
    feed.need()


def attn_fwd(tok, seg, tab, proj, fg, fb, wq, wk, wv, wo, bq, bk, bv, bo, sg, sb):
    rows, width = tok.shape
    sd, v = jax.ShapeDtypeStruct, pltpu.VMEM
    outs = (
        sd((rows, width), BF16),
        sd((2, rows, width), BF16),
        sd((2, rows, HEADS * FEAT), BF16),
        sd((rows, width), BF16),
        sd((rows, 384), F32),
        sd((rows, width), F32),
        sd((rows, width), BF16),
        sd((rows, width), F32),
        sd((rows, width), F32),
        sd((rows, width), BF16),
    )
    near = (seg, fg, fb, bq, bk, bv, bo, sg, sb, proj)
    far = (tok, wv, wq, tab, wk, wo)
    scratch = [v((rows, 128), F32)] + [v(a.shape, a.dtype) for a in outs[:5] + far]
    return call(attn_fwd_kernel, "attn_fwd", near + far, outs, scratch, 52, len(far) + 5, 5520000000,
                far=range(len(near), len(near) + len(far)), far_out=range(5))


FFN_STEP = 256


def ffn_kernel(first, last, place, sec, cot, *refs):
    n_in = 5 if first else 8
    ins, refs = refs[:n_in], refs[n_in:]
    out_o, sg_o, send_o, keep_o, gb_o, wu, wd, secT, hidT, acc, sems = refs
    x, y, c = place[0], place[1], place[2]
    rows, width = sec.shape
    quarter, half = width // 4, width // 2

    def part(a, core):
        return pl.ds(pl.multiple_of((2 * a + core) * quarter, quarter), quarter)

    if first:
        bu, oacc, bd, wu_i, wd_i = ins
        feed = Feed([(wu_i, wu), (wd_i, wd)], sems)
        bias = bu[...]
        early = (0,)
    else:
        own, own_x, own_y, far, far_x, far_y, oacc, sacc = ins
        up, down = pl.ds(0, quarter), pl.ds(quarter, quarter)
        feed = Feed([
            (own.at[up], wu.at[part(x, c)]), (own_x, wu.at[part(1 - x, c)]),
            (far.at[up], wu.at[part(x, 1 - c)]), (far_x, wu.at[part(1 - x, 1 - c)]),
            (own.at[down], wd.at[part(y, c)]), (own_y, wd.at[part(1 - y, c)]),
            (far.at[down], wd.at[part(y, 1 - c)]), (far_y, wd.at[part(1 - y, 1 - c)]),
        ], sems)
        tail = own[2 * quarter:2 * quarter + 16, :].astype(F32)
        bias = tail[0:1, :] + tail[1:2, :] + tail[2:3, :]
        early = (0, 1, 2, 3)
    mine = pl.ds(pl.multiple_of(c * half, half), half)
    other = pl.ds(pl.multiple_of((1 - c) * half, half), half)
    secT[...] = jnp.transpose(sec[...])
    feed.need(*early)
    cut = FFN_STEP // 2
    for n, at in enumerate(range(0, width, FFN_STEP)):
        cs = slice(at, at + FFN_STEP)
        inner = nn(sec[...], wu[:, cs]) + bias[:, cs]
        cdf = 0.5 + 0.5 * lax.erf(inner * math.sqrt(0.5))
        slope = cdf + inner * (jnp.exp(-0.5 * inner * inner) * (1.0 / math.sqrt(2.0 * math.pi)))
        hidden = (inner * cdf).astype(BF16)
        feed.need()
        grad = (nt(cot[...], wd[cs, :]) * slope).astype(BF16)
        gb_o[:, cs] = jnp.sum(grad.astype(F32), 0, keepdims=True)
        more_out = nn(hidden, wd[cs, :])
        more_sg = nt(grad, wu[:, cs])
        if n == 0:
            acc[...] = oacc[...] + more_out + (bd[...] if first else 0.0)
            sg_o[...] = more_sg if first else sacc[...] + more_sg
        else:
            acc[...] += more_out
            sg_o[...] += more_sg
        hidT[...] = jnp.transpose(hidden)
        piece = slice(n * cut, n * cut + cut)
        keep_o[1, piece, :] = nn(hidT[pl.ds(pl.multiple_of(c * cut, cut), cut), :], cot[...]).astype(BF16)
        send_o[1, piece, :] = nn(hidT[pl.ds(pl.multiple_of((1 - c) * cut, cut), cut), :], cot[...]).astype(BF16)
        keep_o[0, :, cs] = nn(secT[mine, :], grad).astype(BF16)
        send_o[0, :, cs] = nn(secT[other, :], grad).astype(BF16)
    out_o[...] = acc[...].astype(out_o.dtype)


def ffn(first, last, place, sec, cot, *ins):
    rows, width = sec.shape
    sd, v = jax.ShapeDtypeStruct, pltpu.VMEM
    outs = (
        sd((rows, width), BF16 if last else F32),
        sd((rows, width), F32),
        sd((2, width // 2, width), BF16),
        sd((2, width // 2, width), BF16),
        sd((1, width), F32),
    )
    scratch = [v((width, width), BF16), v((width, width), BF16), v((width, rows), BF16), v((FFN_STEP, rows), BF16),
               v((rows, width), F32)]
    return call(partial(ffn_kernel, first, last), "ffn", (place, sec, cot) + ins, outs, scratch, 14, 8, 690000000, smem=1,
                far=(6, 7) if first else (), alias=None if first else {10: 1})


def out_bwd_kernel(place, sgrad, mid, sg, cot, ctx, dinv, c0, wo_i,
                   send_o, keep_o, low_o, hi_o, lo_o, mg_o, vec, wo, tr_s, cg_s, sems):
    feed = Feed([(wo_i, wo)], sems)
    c = place[2]
    rows, width = mid.shape
    half = width // 2
    tr_s[...] = jnp.transpose(ctx[...])
    hat, scale = norm_parts(mid[...])
    up = sgrad[...]
    vec[...] = jnp.zeros_like(vec)
    vec[0:1, :] = jnp.sum(up * hat, 0, keepdims=True)
    vec[1:2, :] = jnp.sum(up, 0, keepdims=True)
    g = cot[...].astype(F32)
    vec[2:3, :] = jnp.sum(g, 0, keepdims=True)
    mg = g + norm_back(up, hat, scale, sg[...])
    mg_o[...] = mg
    og = mg.astype(BF16)
    vec[3:4, :] = jnp.sum(og.astype(F32), 0, keepdims=True)
    feed.need()
    cg_s[...] = nt(og, wo[...])
    keep_o[...] = nn(tr_s[pl.ds(pl.multiple_of(c * half, half), half), :], og).astype(BF16)
    send_o[...] = nn(tr_s[pl.ds(pl.multiple_of((1 - c) * half, half), half), :], og).astype(BF16)
    for j in range(HEADS // 2):
        lanes = slice(128 * j, 128 * j + 128)
        low = (cg_s[:, lanes] * dinv[:, lanes]).astype(BF16)
        low_o[:, lanes] = low
        less = -(low.astype(F32) * c0[:, lanes])
        hi = less.astype(BF16)
        hi_o[:, lanes] = hi
        lo_o[:, lanes] = pltpu.roll(less - hi.astype(F32), 64, 1).astype(BF16)


def out_bwd(place, sgrad, mid, sg, cot, ctx, dinv, c0, wo):
    rows, width = mid.shape
    sd, v = jax.ShapeDtypeStruct, pltpu.VMEM
    outs = (
        sd((width // 2, width), BF16),
        sd((width // 2, width), BF16),
        sd((rows, width), BF16),
        sd((rows, width), BF16),
        sd((rows, width), BF16),
        sd((rows, width), F32),
        sd((16, width), F32),
    )
    scratch = [v((width, width), BF16), v((width, rows), BF16), v((rows, width), F32)]
    return call(out_bwd_kernel, "out_bwd", (place, sgrad, mid, sg, cot, ctx, dinv, c0, wo), outs, scratch, 12, 1, 575000000, smem=1, far=(8,))


def value_bwd_kernel(place, seg, low, f, normed, send_o, keep_o, gv_o, normT_o, vec, col_s):
    c = place[2]
    rows, width = low.shape
    half = width // 2
    col_s[...] = label_column(seg)
    seg_row = seg[...].astype(F32)
    lane = lax.broadcasted_iota(jnp.int32, (1, 128), 1)

    def heads(i, _):
        at = pl.ds(pl.multiple_of(i * TILE, TILE), TILE)
        same = col_s[at, :1] == seg_row
        for j in range(HEADS // 2):
            lanes = slice(128 * j, 128 * j + 128)
            flanes = slice(128 * (j // 2), 128 * (j // 2) + 128)
            res = []
            for h in range(2):
                fm = lane_mask(2 * (j % 2) + h)
                wT = jnp.where(same, nt(f[1, at, flanes] * fm, f[0, :, flanes]), 0.0).astype(BF16)
                res.append(nn(wT, low[:, lanes]))
            gv_o[at, lanes] = jnp.where(lane < HD, res[0], res[1]).astype(BF16)
        return 0

    lax.fori_loop(0, rows // TILE, heads, 0)
    normT_o[...] = jnp.transpose(normed[...])
    vec[...] = jnp.zeros_like(vec)
    vec[6:7, :] = jnp.sum(gv_o[...].astype(F32), 0, keepdims=True)
    keep_o[...] = nn(normT_o[pl.ds(pl.multiple_of(c * half, half), half), :], gv_o[...]).astype(BF16)
    send_o[...] = nn(normT_o[pl.ds(pl.multiple_of((1 - c) * half, half), half), :], gv_o[...]).astype(BF16)


def value_bwd(place, seg, low, f, normed):
    rows, width = low.shape
    sd, v = jax.ShapeDtypeStruct, pltpu.VMEM
    outs = (
        sd((width // 2, width), BF16),
        sd((width // 2, width), BF16),
        sd((rows, width), BF16),
        sd((width, rows), BF16),
        sd((16, width), F32),
    )
    return call(value_bwd_kernel, "value_bwd", (place, seg, low, f, normed), outs, [v((rows, 128), F32)], 12, 0, 920000000, smem=1)


def score_bwd_kernel(seg, low, hi, lo, vals, f, de_o, col_s):
    rows, width = low.shape
    col_s[...] = label_column(seg)
    seg_row = seg[...].astype(F32)
    ones = jnp.ones((rows, 128), BF16)
    lane = lax.broadcasted_iota(jnp.int32, (1, 128), 1)

    def heads(i, _):
        at = pl.ds(pl.multiple_of(i * TILE, TILE), TILE)
        same = col_s[at, :1] == seg_row
        for j in range(HEADS // 2):
            gr = j // 2
            lanes = slice(128 * j, 128 * j + 128)
            flanes = slice(128 * gr, 128 * gr + 128)
            v_all = jnp.concatenate([vals[:, lanes], ones], 1)
            v_at = jnp.concatenate([vals[at, lanes], ones[:TILE]], 1)
            qf_all, kf_all = f[0, :, flanes], f[1, :, flanes]
            dq, dk = None, None
            for h in range(2):
                fm = lane_mask(2 * (j % 2) + h).astype(F32)
                own = jnp.where(lane // HD == h, 1.0, 0.0).astype(BF16)
                rest = 1.0 - own

                def pair(span):
                    return jnp.concatenate([low[span, lanes] * own, hi[span, lanes] * own + lo[span, lanes] * rest], 1)

                dwT = jnp.where(same, nt(v_at, pair(slice(None))), 0.0).astype(BF16)
                gk = nn(dwT, qf_all) * fm
                dk = gk if dk is None else dk + gk
                dw = jnp.where(same, nt(pair(at), v_all), 0.0).astype(BF16)
                gq = nn(dw, kf_all) * fm
                dq = gq if dq is None else dq + gq
            if j % 2 == 0:
                de_o[0, at, flanes] = dq
                de_o[1, at, flanes] = dk
            else:
                de_o[0, at, flanes] = (de_o[0, at, flanes] + dq) * f[0, at, flanes].astype(F32)
                de_o[1, at, flanes] = (de_o[1, at, flanes] + dk) * f[1, at, flanes].astype(F32)
        return 0

    lax.fori_loop(0, rows // TILE, heads, 0)


def score_bwd(seg, low, hi, lo, vals, f):
    rows = low.shape[0]
    outs = (jax.ShapeDtypeStruct((2, rows, HEADS * FEAT), F32),)
    return call(score_bwd_kernel, "score_bwd", (seg, low, hi, lo, vals, f), outs, [pltpu.VMEM((rows, 128), F32)], 12, 0, 1380000000)[0]


def key_bwd_kernel(place, de, s, rot, proj, normT, send_o, keep_o, grads_o, vec):
    c = place[2]
    rows = s.shape[1]
    width = s.shape[2]
    half = width // 2
    p_wide, blocks = block_projection(proj)
    p_hi, p_lo = split(p_wide)

    def back(i, _):
        at = pl.ds(pl.multiple_of(i * TILE, TILE), TILE)
        cos, sin_a, sin_b = rot[at, 0:128], rot[at, 128:256], rot[at, 256:384]
        for which in range(2):
            for gr in range(width // 256):
                d_hi, d_lo = split(de[which, at, 128 * gr:128 * gr + 128])
                s_at = s[which, at, 256 * gr:256 * gr + 256].astype(F32)
                ds = nt(d_hi, p_hi) + nt(d_lo, p_hi) + nt(d_hi, p_lo) - s_at * (nt(d_hi, blocks) + nt(d_lo, blocks))
                for k in range(2):
                    du = turn_back(ds[:, 128 * k:128 * k + 128], cos, sin_a, sin_b)
                    lanes = slice(256 * gr + 128 * k, 256 * gr + 128 * k + 128)
                    grads_o[which, at, lanes] = du.astype(BF16)
        return 0

    lax.fori_loop(0, rows // TILE, back, 0)
    vec[...] = jnp.zeros_like(vec)
    for which in range(2):
        vec[4 + which:5 + which, :] = jnp.sum(grads_o[which].astype(F32), 0, keepdims=True)
        keep_o[which] = nn(normT[pl.ds(pl.multiple_of(c * half, half), half), :], grads_o[which]).astype(BF16)
        send_o[which] = nn(normT[pl.ds(pl.multiple_of((1 - c) * half, half), half), :], grads_o[which]).astype(BF16)


def key_bwd(place, de, s, rot, proj, normT):
    width, rows = normT.shape
    sd = jax.ShapeDtypeStruct
    outs = (
        sd((2, width // 2, width), BF16),
        sd((2, width // 2, width), BF16),
        sd((2, rows, width), BF16),
        sd((16, width), F32),
    )
    return call(key_bwd_kernel, "key_bwd", (place, de, s, rot, proj, normT), outs, [], 12, 0, 460000000, smem=1)


def token_bwd_kernel(slopes, which, grads, gv, mg, fg, *refs):
    vecs, slope, refs = refs[:3], refs[3:3 + slopes], refs[3 + slopes:]
    tok_i, wq_i, wk_i, wv_i, gtok_o, vec, tok, wq, wk, wv, sems = refs
    feed = Feed([(tok_i, tok), (wv_i, wv), (wq_i, wq), (wk_i, wk)], sems)
    feed.need(0)
    hat, scale = norm_parts(tok[...].astype(F32))
    feed.need(1)
    ng = nt(gv[...], wv[...])
    feed.need()
    ng = ng + nt(grads[0], wq[...]) + nt(grads[1], wk[...])
    vec[...] = jnp.zeros_like(vec)
    vec[0:16, :] = vecs[0][...] + vecs[1][...] + vecs[2][...]
    vec[7:8, :] = jnp.sum(ng * hat, 0, keepdims=True)
    vec[8:9, :] = jnp.sum(ng, 0, keepdims=True)
    for n in range(slopes):
        vec[pl.ds(16 + which[n], 1), :] = slope[n][...]
    gtok_o[...] = (mg[...] + norm_back(ng, hat, scale, fg[...])).astype(BF16)


def token_bwd(which, grads, gv, mg, fg, vecs, slopes, tok, wq, wk, wv):
    rows, width = tok.shape
    n = len(slopes)
    sd, v = jax.ShapeDtypeStruct, pltpu.VMEM
    outs = (sd((rows, width), BF16), sd((16 + -(-n // 8) * 8, width), F32))
    ins = (which, grads, gv, mg, fg) + tuple(vecs) + tuple(slopes) + (tok, wq, wk, wv)
    return call(partial(token_bwd_kernel, n), "token_bwd", ins, outs,
                [v((rows, width), BF16)] + [v((width, width), BF16)] * 3, TOKEN_LIMIT, 4, 460_000_000, smem=1, far=range(len(ins) - 4, len(ins)))


def pack_kernel(place, wu, wd, bu, out, sems):
    quarter = wu.shape[1] // 4
    x, y, c = place[0], place[1], place[2]
    feed = Feed([
        (wu.at[pl.ds(pl.multiple_of((2 * x + c) * quarter, quarter), quarter)], out.at[pl.ds(0, quarter)]),
        (wd.at[pl.ds(pl.multiple_of((2 * y + c) * quarter, quarter), quarter)], out.at[pl.ds(quarter, quarter)]),
    ], sems)
    left, parts = bu[...], []
    for _ in range(3):
        parts.append(left.astype(BF16).astype(F32))
        left = left - parts[-1]
    parts.append(jnp.zeros((13, left.shape[1]), F32))
    out[2 * quarter:2 * quarter + 16, :] = jnp.concatenate(parts, 0).astype(BF16)
    feed.need()


def pack(place, wu, wd, bu):
    width = wu.shape[1]
    outs = (jax.ShapeDtypeStruct((width // 2 + 16, width), BF16),)
    return call(pack_kernel, "pack", (place, wu, wd, bu), outs, [], 58, 2, 115000000, smem=1, far=(1, 2))[0]


def split_kernel(items, place, *refs):
    send, own = refs[-2:]
    step = send.shape[1]
    for n, (side, terms) in enumerate(items):
        here = place[side]
        for out, at in ((send, 1 - here), (own, here)):
            rows = pl.ds(pl.multiple_of(at * step, step), step)
            total = None
            for m, e in terms:
                term = (refs[m][rows, :] if e is None else refs[m][e, rows, :]).astype(F32)
                total = term if total is None else total + term
            out[n] = total.astype(BF16)


def split_sums(place, *sums):
    arrays, items = [], []
    for side, *terms in sums:
        at = []
        for v, e in terms:
            m = next((n for n, u in enumerate(arrays) if u is v), len(arrays))
            if m == len(arrays):
                arrays.append(v)
            at.append((m, e))
        items.append((side, tuple(at)))
    rows, width = arrays[0].shape[-2:]
    outs = (jax.ShapeDtypeStruct((len(sums), rows // 2, width), BF16),) * 2
    return call(partial(split_kernel, tuple(items)), "split_sums", (place,) + tuple(arrays), outs, [], 8, 0, 100_000_000, smem=1)


def finish_kernel(woven, place, *refs):
    mats = len(woven)
    parts, outs, (held, sems) = refs[:-mats - 2], refs[-mats - 2:-2], refs[-2:]
    c = place[2]
    rows = held.shape[2]
    feed = Feed([], sems)
    cut = FFN_STEP // 2
    per = len(parts) // 2
    for m in range(mats):
        for side, core in ((0, c), (1, 1 - c)):
            ref, entry = parts[side * per + m * per // mats], m % (mats // per)
            held[m, side] = ref[entry].astype(F32)
            if woven[m]:
                for k in range(rows // cut):
                    feed.add(held.at[m, side, pl.ds(k * cut, cut)], outs[m].at[pl.ds(pl.multiple_of(2 * k * cut + core * cut, cut), cut)])
            else:
                feed.add(held.at[m, side], outs[m].at[pl.ds(pl.multiple_of(core * rows, rows), rows)])
    feed.need()


def finish(place, mine, got, woven):
    n = len(woven)
    rows, width = mine[0].shape[1:]
    outs = (jax.ShapeDtypeStruct((2 * rows, width), F32),) * n
    return call(partial(finish_kernel, woven), "finish", (place,) + tuple(mine) + tuple(got), outs,
                [pltpu.VMEM((n, 2, rows, width), F32)], 20,
                sum(2 * (rows // (FFN_STEP // 2) if w else 1) for w in woven), 230_000_000, smem=1, far_out=range(n))


def add_low(*parts):
    total = parts[0].astype(F32)
    for part in parts[1:]:
        total = total + part.astype(F32)
    return total.astype(parts[0].dtype)


def ordered(first, then):
    return lax.optimization_barrier((first, then))[1]


class Links:
    def __init__(self, first):
        self.dp, self.ring = lax.axis_size("dp"), lax.axis_size("tensor")
        at, z = lax.axis_index("dp"), lax.axis_index("tensor")
        self.bits = [1 << n for n in range(1, self.dp.bit_length() - 1)]
        order = [1] + self.bits
        sides = [(at // bit) % 2 for bit in order]
        place = jnp.stack([sides[1], sides[-1], sides[0]]).astype(jnp.int32)
        steps = jnp.arange(self.ring, dtype=jnp.int32)
        which = (z - steps) % self.ring
        low, self.place, self.which, self.mine, self.first = lax.optimization_barrier(
            ([side == 0 for side in sides], place, which, (steps == z).astype(F32)[:, None], first))
        self.low = dict(zip(order, low))

    def swap(self, v, bit):
        return lax.ppermute(v, "dp", [(i, i ^ bit) for i in range(self.dp)])

    def shift(self, v, by=1):
        return lax.ppermute(v, "tensor", [(i, (i + by) % self.ring) for i in range(self.ring)])

    def near(self, v, bit):
        return lax.ppermute(v, "tensor", [(i, i ^ bit) for i in range(self.ring)])

    def join(self, v, got, bit, axis=None):
        low = self.low[bit]
        axis = v.ndim - 2 if axis is None else axis
        if axis < v.ndim - 2 and v.shape[axis] > 1:
            v, got = jnp.expand_dims(v, axis), jnp.expand_dims(got, axis)
        return jnp.concatenate([jnp.where(low, v, got), jnp.where(low, got, v)], axis)


def fence(*values):
    return lax.optimization_barrier(values)


def halve(links, v, bit):
    rows = v.shape[-2] // 2
    first, second = v[..., :rows, :], v[..., rows:, :]
    low = links.low[bit]
    return add_low(jnp.where(low, first, second), links.swap(jnp.where(low, second, first), bit))


def body(tokens, cotangent, segment, projection, first_gain, first_bias, w_query, w_key, w_value, w_out,
         b_query, b_key, b_value, b_out, second_gain, second_bias, w_up, b_up, w_down, b_down):
    links = Links(tokens)
    tokens, place = links.first, links.place
    rows, width = tokens.shape
    low_bit, top_bit = links.bits[0], links.bits[-1]
    order = [low_bit, top_bit] + links.bits[1:-1]
    core_low = links.low[1]
    quarter = width // 4

    def line(v):
        return v.reshape(1, -1)

    share = links.shift(pack(place, w_up, w_down, line(b_up)))
    table = jnp.asarray(rotary_table(256))
    normed, s, f, vals, rot, c0, ctx, dinv, mid, second = attn_fwd(
        tokens, segment, table, projection, line(first_gain), line(first_bias), w_query, w_key, w_value, w_out,
        line(b_query), line(b_key), line(b_value), line(b_out), line(second_gain), line(second_bias))

    def beside(share):
        return links.swap(share[:quarter], low_bit), links.swap(share[quarter:2 * quarter], top_bit)

    def own_ffn(first, last, parts, acc):
        ins = (line(b_up), mid, line(b_down), w_up, w_down) if first else parts + acc
        return ffn(first, last, place, second, cotangent, *ins)

    share, second = fence(share, second)
    swapped, coming = beside(share), links.shift(share)
    out, sgrad, send, keep, slope = own_ffn(True, False, (), ())
    swapped, out, send = fence(swapped, out, send)
    slopes, keeps, sends = [slope], [keep], [send]
    across = tuple(links.swap(v, 1) for v in (share,) + swapped)
    for n in range(1, links.ring):
        last = n == links.ring - 1
        parts = (share,) + swapped + across
        if not last:
            parts, share, out = fence(parts, coming, out)
            swapped = beside(share)
            coming = links.shift(share) if n < links.ring - 2 else share
        sends[-1] = links.swap(sends[-1], 1)
        if last:
            up_send, up_own = split_sums(place, *[(0, (keeps[k], 0), (sends[k], 0)) for k in range(2)])
            up_send, up_own, down, out = fence(up_send, up_own, add_low(keeps[1][1], sends[1][1]), out)
            up_got, down = links.swap(up_send, low_bit), links.shift(down)
        out, sgrad, send, keep, slope = own_ffn(False, last, parts, (out, sgrad))
        slopes.append(slope)
        keeps.append(keep)
        sends.append(send)
        if not last:
            swapped, coming, out = fence(swapped, coming, out)
            across = tuple(links.swap(v, 1) for v in (share,) + swapped)
            across, sends[-1] = fence(across, sends[-1])

    sgrad, up_got, down, send = fence(sgrad, up_got, down, sends[-1])
    sends[-1] = links.swap(send, 1)
    send_o, keep_o, low, hi, lo, mg, vec_o = out_bwd(
        place, sgrad, mid, line(second_gain), cotangent, ctx, dinv, c0, w_out)
    low, sends = fence(low, sends)
    up_send, up_more = split_sums(place, *[(0, (keeps[k], 0), (sends[k], 0)) for k in range(2, links.ring)])
    low, up_send, up_more, down = fence(low, up_send, up_more, add_low(down, keeps[2][1], sends[2][1]))
    down, up_last = links.shift(down), links.swap(up_send, low_bit)
    far_o = links.swap(send_o, 1)
    send_v, keep_v, gv, normT, vec_v = value_bwd(place, segment, low, f, normed)
    gv, low, down, up_last, send_v = fence(gv, low, down, up_last, send_v)
    far_v = links.swap(send_v, 1)
    up_send, up_own = split_sums(
        place, *[(1, (up_own, n), (up_got, n)) for n in range(2)], *[(1, (up_more, n), (up_last, n)) for n in range(links.ring - 2)])
    far_o, far_v, up_send, up_own, down, low = fence(far_o, far_v, up_send, up_own, add_low(down, keeps[3][1], sends[3][1]), low)
    ov_send, ov_own = split_sums(place, (0, (keep_v, None), (far_v, None)), (0, (keep_o, None), (far_o, None)))
    ov_send, ov_own, low = fence(ov_send, ov_own, low)
    down, up_got, ov_got = links.shift(down), links.swap(up_send, order[1]), links.swap(ov_send, low_bit)
    de = score_bwd(segment, low, hi, lo, vals, f)
    de, down, up_got, ov_got = fence(de, down, up_got, ov_got)
    for n in range(4, links.ring):
        down = links.shift(add_low(down, keeps[n][1], sends[n][1]))
    ov_send, ov_own = split_sums(place, *[(1, (ov_own, n), (ov_got, n)) for n in range(2)])
    down_send, down_own = split_sums(place, (0, (down, None), (keeps[0], 1), (sends[0], 1)))
    up = add_low(up_own, up_got)
    for bit in order[2:]:
        up = halve(links, up, bit)
    ov_send, ov_own, down_send, down_own, up, de = fence(ov_send, ov_own, down_send, down_own, up, de)
    ov_got, up_way, down_got = links.swap(ov_send, order[1]), links.shift(up[1]), links.swap(down_send, low_bit)
    send_k, keep_k, grads, vec_k = key_bwd(place, de, s, rot, projection, normT)
    ov_got, up_way, down_got, send_k, grads = fence(ov_got, up_way, down_got, send_k, grads)

    far_k = links.swap(send_k, 1)
    ov = add_low(ov_own, ov_got)
    for bit in order[2:]:
        ov = halve(links, ov, bit)
    ov_got = links.near(ov, 1)
    down_send, down_own = split_sums(place, (1, (down_own, 0), (down_got, 0)))
    far_k, down_send, down_own, up_way, grads = fence(far_k, down_send, down_own, add_low(up_way, up[2]), grads)
    qk_send, qk_own = split_sums(place, *[(n, (keep_k, n), (far_k, n)) for n in range(2)])
    qk_send, qk_own, grads = fence(qk_send, qk_own, grads)
    way_a, way_b = [low_bit, top_bit], [top_bit, low_bit]

    def both_ways(v, level):
        return links.swap(v[0], way_a[level]), links.swap(v[1], way_b[level])

    got_qk = both_ways(qk_send, 0)
    down_got, up_way = links.swap(down_send, order[1]), links.shift(up_way)
    ov, = fence(add_low(ov, ov_got))
    ov_got = links.near(ov, 2)
    got_qk, up_way, down_got, grads = fence(got_qk, up_way, down_got, grads)

    qk_send, qk_own = split_sums(place, *[(1 - n, (qk_own, n), (got_qk[n], None)) for n in range(2)])
    down = add_low(down_own, down_got)
    for bit in order[2:]:
        down = halve(links, down, bit)
    qk_send, qk_own, up_way, down, grads = fence(qk_send, qk_own, add_low(up_way, up[3]), down[0], grads)
    got_qk = both_ways(qk_send, 1)
    up_way = links.shift(up_way)
    gtok, vec = token_bwd(links.which, grads, gv, mg, line(first_gain), (vec_o, vec_v, vec_k), slopes, tokens, w_query, w_key, w_value)
    got_qk, up_way, vec, ov_got = fence(got_qk, up_way, vec, ov_got)

    def back_first(v):
        for bit in order[:1:-1]:
            v = links.join(v, links.swap(v, bit), bit)
        return v

    qk = jnp.stack([add_low(qk_own[n], got_qk[n]) for n in range(2)])
    for bit in order[2:]:
        qk = halve(links, qk, bit)
    for n in range(4, links.ring):
        up_way = links.shift(add_low(up_way, up[n]))
    ov = add_low(ov, ov_got)
    qk, vec, one, two = fence(
        qk, vec, back_first(jnp.stack([add_low(up_way, up[0]), ov[0]])), back_first(jnp.stack([down, ov[1]])))
    got_qk = links.near(qk, 1)
    one_got, two_got = links.swap(one, order[1]), links.swap(two, low_bit)
    vec = vec + links.swap(vec, 1)
    got_vec = links.swap(vec, low_bit)
    got_qk, one_got, two_got, got_vec = fence(got_qk, one_got, two_got, got_vec)

    qk, vec, one, two = fence(
        add_low(qk, got_qk), vec + got_vec, links.join(one, one_got, order[1]), links.join(two[:, None], two_got[:, None], low_bit, 1))
    got_qk = links.near(qk, 2)
    one_got, two_got = links.swap(one, low_bit), links.swap(two, order[1])
    got_vec = links.swap(vec, order[1])
    got_qk, one_got, two_got, got_vec = fence(got_qk, one_got, two_got, got_vec)

    qk = add_low(qk, got_qk)
    qk = [back_first(qk[n]) for n in range(2)]
    qk, vec, one, two = fence(
        qk, vec + got_vec, links.join(one, one_got, low_bit), links.join(two, two_got, order[1]).reshape(one.shape[0], -1, width))
    got_qk = both_ways(qk, 1)
    one_got, two_got = links.swap(one, 1), links.swap(two, 1)
    for bit in order[2:]:
        vec = vec + links.swap(vec, bit)
    got_vec = links.near(vec, 1)
    got_qk, one_got, two_got, got_vec = fence(got_qk, one_got, two_got, got_vec)

    def qk_in(pair, got, level):
        return [links.join(v, g, way[level]) for v, g, way in zip(pair, got, (way_a, way_b))]

    qk, vec = fence(qk_in(qk, got_qk, 1), vec + got_vec)
    got_qk = both_ways(qk, 0)
    got_vec = links.near(vec, 2)
    grad_w_up, grad_w_value, grad_w_down, grad_w_out = finish(place, [one, two], [one_got, two_got], (False, False, True, False))
    got_qk, got_vec, grad_w_up, grad_w_down, grad_w_value, grad_w_out = fence(
        got_qk, got_vec, grad_w_up, grad_w_down, grad_w_value, grad_w_out)

    qk, vec = fence([v[None] for v in qk_in(qk, got_qk, 0)], vec + got_vec)
    grad_w_query, grad_w_key = finish(place, qk, [links.swap(v, 1) for v in qk], (False, False))

    grad_b_up = jnp.sum(vec[16:16 + links.ring] * links.mine, 0)
    return (
        out, gtok, vec[7], vec[8], grad_w_query, grad_w_key, grad_w_value, grad_w_out,
        vec[4], vec[5], vec[6], vec[3], vec[0], vec[1], grad_w_up, grad_b_up, grad_w_down, vec[2],
    )


def solution(mesh):
    rows = P(("dp", "tensor"), None)
    whole = P()
    return jax.shard_map(
        body,
        mesh=mesh,
        in_specs=(rows,) * 3 + (whole,) * 13 + (P(None, "tensor"), P("tensor"), P("tensor", None), whole),
        out_specs=(rows,) * 2 + (whole,) * 12 + (P(None, "tensor"), P("tensor"), P("tensor", None), whole),
        check_vma=False,
    )
```

```python
from functools import partial
import math

import jax
import jax.numpy as jnp
import numpy as np
from jax import lax
from jax.experimental import pallas as pl
from jax.experimental.pallas import tpu as pltpu
from jax.sharding import PartitionSpec as P

HEADS = 12
HD = 64
FEAT = 32
EPS = 1e-05
F32 = jnp.float32
BF16 = jnp.bfloat16
ANY = pl.BlockSpec(memory_space=pltpu.HBM)
VM = pl.BlockSpec(memory_space=pltpu.VMEM)
SMEM = pl.BlockSpec(memory_space=pltpu.SMEM)
SCALE = HD ** -0.25


def nn(a, b):
    return lax.dot_general(a, b, (((1,), (0,)), ((), ())), preferred_element_type=F32)


def nt(a, b):
    return lax.dot_general(a, b, (((1,), (1,)), ((), ())), preferred_element_type=F32)


def split(v):
    high = v.astype(BF16)
    return high, (v - high.astype(F32)).astype(BF16)


def rotary_table(length):
    half = HD // 2
    rate = np.exp(np.arange(half) * (-2.0 * math.log(10000.0) / HD))
    angle = np.arange(length)[:, None] * rate[None, :]
    return (np.concatenate([np.cos(angle), np.sin(angle)], 1) * SCALE).astype(np.float32)


def rotary_lanes(tab):
    half = HD // 2
    lane = lax.broadcasted_iota(jnp.int32, (1, 128), 1)
    first = lane % HD < half
    cos = jnp.concatenate([tab[:, :half]] * 4, axis=1)
    sin = jnp.concatenate([tab[:, half:]] * 4, axis=1)
    table = jnp.concatenate([cos, jnp.where(first, -sin, 0.0), jnp.where(first, 0.0, sin)], axis=1)
    high = table.astype(BF16)
    rest = table - high.astype(F32)
    middle = rest.astype(BF16)
    return high, middle, (rest - middle.astype(F32)).astype(BF16)


def lane_mask(head_in_group):
    lane = lax.broadcasted_iota(jnp.int32, (1, 128), 1)
    return jnp.where(lane // FEAT == head_in_group, 1.0, 0.0).astype(BF16)


def norm_parts(v):
    centred = v - jnp.mean(v, -1, keepdims=True)
    scale = lax.rsqrt(jnp.mean(centred * centred, -1, keepdims=True) + EPS)
    return centred * scale, scale


def norm_back(grad, hat, scale, gain):
    hat_grad = grad * gain
    return scale * (
        hat_grad
        - jnp.mean(hat_grad, -1, keepdims=True)
        - hat * jnp.mean(hat_grad * hat, -1, keepdims=True)
    )


def label_column(seg):
    rows = seg.shape[1]
    return jnp.transpose(jnp.broadcast_to(seg[...].astype(F32), (128, rows)))


def block_projection(proj):
    tall = jnp.concatenate([proj[...]] * 4, axis=0)
    wide = jnp.concatenate([tall] * 4, axis=1)
    group = lax.broadcasted_iota(jnp.int32, (256, 128), 0) // HD
    feat = lax.broadcasted_iota(jnp.int32, (256, 128), 1) // FEAT
    return jnp.where(group == feat, wide, 0.0), jnp.where(group == feat, 1.0, 0.0).astype(BF16)


def turn(u, cos, sin_a, sin_b):
    return u * cos + pltpu.roll(u, 96, 1) * sin_a + pltpu.roll(u, 32, 1) * sin_b


def turn_back(u, cos, sin_a, sin_b):
    return u * cos - pltpu.roll(u, 96, 1) * sin_a - pltpu.roll(u, 32, 1) * sin_b


class Feed:
    def __init__(self, pairs, sems):
        self.sems, self.copies, self.left = sems, [], []
        for src, dst in pairs:
            self.add(src, dst)

    def add(self, src, dst):
        copy = pltpu.make_async_copy(src, dst, self.sems.at[len(self.copies)])
        copy.start()
        self.left.append(len(self.copies))
        self.copies.append(copy)

    def need(self, *which):
        for n in which or list(self.left):
            if n in self.left:
                self.copies[n].wait()
                self.left.remove(n)


def call(kernel, name, ins, outs, scratch, limit, sems, flops, smem=0, far=(), far_out=(), alias=None):
    return pl.pallas_call(
        kernel,
        out_shape=outs,
        in_specs=[SMEM if n < smem else ANY if n in far else VM for n in range(len(ins))],
        out_specs=[ANY if n in far_out else VM for n in range(len(outs))],
        scratch_shapes=list(scratch) + ([pltpu.SemaphoreType.DMA((sems,))] if sems else []),
        input_output_aliases=alias or {},
        compiler_params=pltpu.CompilerParams(vmem_limit_bytes=limit << 20),
        cost_estimate=pl.CostEstimate(flops=flops, bytes_accessed=1000, transcendentals=0),
        name=name,
    )(*ins)


TILE = 256
TOKEN_LIMIT = 44


def attn_fwd_kernel(seg, fg, fb, bq, bk, bv, bo, sg, sb, proj, tok_i, wv_i, wq_i, tab_i, wk_i, wo_i,
                    normed_i, s_i, f_i, v_i, rot_i, c0_o, ctx_o, dinv_o, mid_o, sec_o,
                    col_s, normed_o, s_o, f_o, v_o, rot_o, tok, wv, wq, tab, wk, wo, sems):
    feed = Feed([(tab_i, tab), (tok_i, tok), (wv_i, wv)], sems)
    rows, width = tok.shape
    col_s[...] = label_column(seg)
    seg_row = seg[...].astype(F32)
    less = jnp.where(seg_row < col_s[:, :1], 1.0, 0.0)
    start = jnp.sum(less, axis=1, keepdims=True)
    place = lax.broadcasted_iota(jnp.int32, (rows, 1), 0).astype(F32) - start
    length = tab.shape[0]
    ladder = lax.broadcasted_iota(jnp.int32, (rows, length), 1).astype(F32)
    one_hot = jnp.where(ladder == place, 1.0, 0.0).astype(BF16)
    p_wide, blocks = block_projection(proj)
    p_hi, p_lo = split(p_wide)
    halves = blocks * 0.5
    feed.need(0)
    parts = rotary_lanes(tab[...])
    rot_o[...] = nn(one_hot, parts[0]) + nn(one_hot, parts[1]) + nn(one_hot, parts[2])
    feed.need(1, 2)
    for src, dst in ((wq_i, wq), (wk_i, wk), (wo_i, wo)):
        feed.add(src, dst)

    def first(i, _):
        at = pl.ds(pl.multiple_of(i * TILE, TILE), TILE)
        x = tok[at, :].astype(F32)
        hat, _scale = norm_parts(x)
        normed = (hat * fg[...] + fb[...]).astype(BF16)
        normed_o[at, :] = normed
        v_o[at, :] = nn(normed, wv[...]).astype(BF16)
        return 0

    lax.fori_loop(0, rows // TILE, first, 0)

    def rotated(i, which, w, b):
        at = pl.ds(pl.multiple_of(i * TILE, TILE), TILE)
        cos, sin_a, sin_b = rot_o[at, 0:128], rot_o[at, 128:256], rot_o[at, 256:384]
        u = nn(normed_o[at, :], w[...]) + b[...]
        for g in range(width // 256):
            s = jnp.concatenate([turn(u[:, k:k + 128], cos, sin_a, sin_b) for k in (256 * g, 256 * g + 128)], 1)
            s_hi, s_lo = split(s)
            s_o[which, at, 256 * g:256 * g + 256] = s_hi
            q_hi, q_lo = split(s * s)
            e = nn(s_hi, p_hi) + nn(s_lo, p_hi) + nn(s_hi, p_lo) - nn(q_hi, halves) - nn(q_lo, halves)
            f_o[which, at, 128 * g:128 * g + 128] = (jnp.exp(e) * FEAT ** -0.5).astype(BF16)
        return 0

    feed.need(3)
    lax.fori_loop(0, rows // TILE, lambda i, _: rotated(i, 0, wq, bq), 0)
    feed.need(4)
    lax.fori_loop(0, rows // TILE, lambda i, _: rotated(i, 1, wk, bk), 0)
    feed.need()
    for held, kept in ((normed_o, normed_i), (s_o, s_i), (f_o, f_i), (v_o, v_i), (rot_o, rot_i)):
        feed.add(held, kept)

    ones = jnp.ones((rows, 128), BF16)
    even = lax.broadcasted_iota(jnp.int32, (1, 128), 1) < HD

    def second(i, _):
        at = pl.ds(pl.multiple_of(i * TILE, TILE), TILE)
        same = col_s[at, :1] == seg_row
        for j in range(HEADS // 2):
            g = j // 2
            vals = jnp.concatenate([v_o[:, 128 * j:128 * j + 128], ones], 1)
            qf = f_o[0, at, 128 * g:128 * g + 128]
            kf = f_o[1, :, 128 * g:128 * g + 128]
            res = []
            for h in range(2):
                scores = nt(qf * lane_mask(2 * (j % 2) + h), kf)
                weights = jnp.where(same, scores, 0.0).astype(BF16)
                res.append(nn(weights, vals))
            num = jnp.where(even, res[0][:, :128], res[1][:, :128])
            inv = 1.0 / jnp.where(even, res[0][:, 128:], res[1][:, 128:])
            lanes = slice(128 * j, 128 * j + 128)
            ctx = num * inv
            dinv_o[at, lanes] = inv
            c0_o[at, lanes] = ctx
            ctx_o[at, lanes] = (ctx + bv[:, lanes]).astype(BF16)
        middle = tok[at, :].astype(F32) + nn(ctx_o[at, :], wo[...]) + bo[...]
        mid_o[at, :] = middle
        hat, _scale = norm_parts(middle)
        sec_o[at, :] = (hat * sg[...] + sb[...]).astype(BF16)
        return 0

    lax.fori_loop(0, rows // TILE, second, 0)
    feed.need()


def attn_fwd(tok, seg, tab, proj, fg, fb, wq, wk, wv, wo, bq, bk, bv, bo, sg, sb):
    rows, width = tok.shape
    sd, v = jax.ShapeDtypeStruct, pltpu.VMEM
    outs = (
        sd((rows, width), BF16),
        sd((2, rows, width), BF16),
        sd((2, rows, HEADS * FEAT), BF16),
        sd((rows, width), BF16),
        sd((rows, 384), F32),
        sd((rows, width), F32),
        sd((rows, width), BF16),
        sd((rows, width), F32),
        sd((rows, width), F32),
        sd((rows, width), BF16),
    )
    near = (seg, fg, fb, bq, bk, bv, bo, sg, sb, proj)
    far = (tok, wv, wq, tab, wk, wo)
    scratch = [v((rows, 128), F32)] + [v(a.shape, a.dtype) for a in outs[:5] + far]
    return call(attn_fwd_kernel, "attn_fwd", near + far, outs, scratch, 48, len(far) + 5, 5520000000,
                far=range(len(near), len(near) + len(far)), far_out=range(5))


FFN_STEP = 256


def ffn_kernel(first, last, place, sec, cot, *refs):
    n_in = 5 if first else 8
    ins, refs = refs[:n_in], refs[n_in:]
    out_o, sg_o, send_o, keep_o, gb_o, wu, wd, secT, hidT, acc, sems = refs
    x, y, c = place[0], place[1], place[2]
    rows, width = sec.shape
    quarter, half = width // 4, width // 2

    def part(a, core):
        return pl.ds(pl.multiple_of((2 * a + core) * quarter, quarter), quarter)

    if first:
        bu, oacc, bd, wu_i, wd_i = ins
        feed = Feed([(wu_i, wu), (wd_i, wd), (oacc, acc)], sems)
        bias = bu[...]
        early = (0,)
    else:
        own, own_x, own_y, far, far_x, far_y, oacc, sacc = ins
        up, down = pl.ds(0, quarter), pl.ds(quarter, quarter)
        feed = Feed([
            (own.at[up], wu.at[part(x, c)]), (own_x, wu.at[part(1 - x, c)]),
            (far.at[up], wu.at[part(x, 1 - c)]), (far_x, wu.at[part(1 - x, 1 - c)]),
            (own.at[down], wd.at[part(y, c)]), (own_y, wd.at[part(1 - y, c)]),
            (far.at[down], wd.at[part(y, 1 - c)]), (far_y, wd.at[part(1 - y, 1 - c)]),
        ], sems)
        tail = own[2 * quarter:2 * quarter + 16, :].astype(F32)
        bias = tail[0:1, :] + tail[1:2, :] + tail[2:3, :]
        early = (0, 1, 2, 3)
    mine = pl.ds(pl.multiple_of(c * half, half), half)
    other = pl.ds(pl.multiple_of((1 - c) * half, half), half)
    secT[...] = jnp.transpose(sec[...])
    feed.need(*early)
    cut = FFN_STEP // 2
    for n, at in enumerate(range(0, width, FFN_STEP)):
        cs = slice(at, at + FFN_STEP)
        inner = nn(sec[...], wu[:, cs]) + bias[:, cs]
        cdf = 0.5 + 0.5 * lax.erf(inner * math.sqrt(0.5))
        slope = cdf + inner * (jnp.exp(-0.5 * inner * inner) * (1.0 / math.sqrt(2.0 * math.pi)))
        hidden = (inner * cdf).astype(BF16)
        feed.need()
        grad = (nt(cot[...], wd[cs, :]) * slope).astype(BF16)
        gb_o[:, cs] = jnp.sum(grad.astype(F32), 0, keepdims=True)
        more_out = nn(hidden, wd[cs, :])
        more_sg = nt(grad, wu[:, cs])
        if n == 0:
            acc[...] = (acc[...] + bd[...] if first else oacc[...]) + more_out
            sg_o[...] = more_sg if first else sacc[...] + more_sg
        else:
            acc[...] += more_out
            sg_o[...] += more_sg
        hidT[...] = jnp.transpose(hidden)
        piece = slice(n * cut, n * cut + cut)
        keep_o[1, piece, :] = nn(hidT[pl.ds(pl.multiple_of(c * cut, cut), cut), :], cot[...]).astype(BF16)
        send_o[1, piece, :] = nn(hidT[pl.ds(pl.multiple_of((1 - c) * cut, cut), cut), :], cot[...]).astype(BF16)
        keep_o[0, :, cs] = nn(secT[mine, :], grad).astype(BF16)
        send_o[0, :, cs] = nn(secT[other, :], grad).astype(BF16)
    out_o[...] = acc[...].astype(out_o.dtype)


def ffn(first, last, place, sec, cot, *ins):
    rows, width = sec.shape
    sd, v = jax.ShapeDtypeStruct, pltpu.VMEM
    outs = (
        sd((rows, width), BF16 if last else F32),
        sd((rows, width), F32),
        sd((2, width // 2, width), BF16),
        sd((2, width // 2, width), BF16),
        sd((1, width), F32),
    )
    scratch = [v((width, width), BF16), v((width, width), BF16), v((width, rows), BF16), v((FFN_STEP, rows), BF16),
               v((rows, width), F32)]
    return call(partial(ffn_kernel, first, last), "ffn", (place, sec, cot) + ins, outs, scratch, 14, 8, 690000000, smem=1,
                far=(4, 6, 7) if first else (), alias=None if first else {10: 1})


def out_bwd_kernel(place, sgrad, mid, sg, cot, ctx, dinv, c0, wo_i,
                   send_o, keep_o, low_o, hi_o, lo_o, mg_o, vec, wo, tr_s, cg_s, sems):
    feed = Feed([(wo_i, wo)], sems)
    c = place[2]
    rows, width = mid.shape
    half = width // 2
    tr_s[...] = jnp.transpose(ctx[...])
    hat, scale = norm_parts(mid[...])
    up = sgrad[...]
    vec[...] = jnp.zeros_like(vec)
    vec[0:1, :] = jnp.sum(up * hat, 0, keepdims=True)
    vec[1:2, :] = jnp.sum(up, 0, keepdims=True)
    g = cot[...].astype(F32)
    vec[2:3, :] = jnp.sum(g, 0, keepdims=True)
    mg = g + norm_back(up, hat, scale, sg[...])
    mg_o[...] = mg
    og = mg.astype(BF16)
    vec[3:4, :] = jnp.sum(og.astype(F32), 0, keepdims=True)
    feed.need()
    cg_s[...] = nt(og, wo[...])
    keep_o[...] = nn(tr_s[pl.ds(pl.multiple_of(c * half, half), half), :], og).astype(BF16)
    send_o[...] = nn(tr_s[pl.ds(pl.multiple_of((1 - c) * half, half), half), :], og).astype(BF16)
    for j in range(HEADS // 2):
        lanes = slice(128 * j, 128 * j + 128)
        low = (cg_s[:, lanes] * dinv[:, lanes]).astype(BF16)
        low_o[:, lanes] = low
        less = -(low.astype(F32) * c0[:, lanes])
        hi = less.astype(BF16)
        hi_o[:, lanes] = hi
        lo_o[:, lanes] = pltpu.roll(less - hi.astype(F32), 64, 1).astype(BF16)


def out_bwd(place, sgrad, mid, sg, cot, ctx, dinv, c0, wo):
    rows, width = mid.shape
    sd, v = jax.ShapeDtypeStruct, pltpu.VMEM
    outs = (
        sd((width // 2, width), BF16),
        sd((width // 2, width), BF16),
        sd((rows, width), BF16),
        sd((rows, width), BF16),
        sd((rows, width), BF16),
        sd((rows, width), F32),
        sd((16, width), F32),
    )
    scratch = [v((width, width), BF16), v((width, rows), BF16), v((rows, width), F32)]
    return call(out_bwd_kernel, "out_bwd", (place, sgrad, mid, sg, cot, ctx, dinv, c0, wo), outs, scratch, 12, 1, 575000000, smem=1, far=(8,))


def value_bwd_kernel(place, seg, low, f, normed, send_o, keep_o, gv_o, normT_o, vec, col_s):
    c = place[2]
    rows, width = low.shape
    half = width // 2
    col_s[...] = label_column(seg)
    seg_row = seg[...].astype(F32)
    lane = lax.broadcasted_iota(jnp.int32, (1, 128), 1)

    def heads(i, _):
        at = pl.ds(pl.multiple_of(i * TILE, TILE), TILE)
        same = col_s[at, :1] == seg_row
        for j in range(HEADS // 2):
            lanes = slice(128 * j, 128 * j + 128)
            flanes = slice(128 * (j // 2), 128 * (j // 2) + 128)
            res = []
            for h in range(2):
                fm = lane_mask(2 * (j % 2) + h)
                wT = jnp.where(same, nt(f[1, at, flanes] * fm, f[0, :, flanes]), 0.0).astype(BF16)
                res.append(nn(wT, low[:, lanes]))
            gv_o[at, lanes] = jnp.where(lane < HD, res[0], res[1]).astype(BF16)
        return 0

    lax.fori_loop(0, rows // TILE, heads, 0)
    normT_o[...] = jnp.transpose(normed[...])
    vec[...] = jnp.zeros_like(vec)
    vec[6:7, :] = jnp.sum(gv_o[...].astype(F32), 0, keepdims=True)
    keep_o[...] = nn(normT_o[pl.ds(pl.multiple_of(c * half, half), half), :], gv_o[...]).astype(BF16)
    send_o[...] = nn(normT_o[pl.ds(pl.multiple_of((1 - c) * half, half), half), :], gv_o[...]).astype(BF16)


def value_bwd(place, seg, low, f, normed):
    rows, width = low.shape
    sd, v = jax.ShapeDtypeStruct, pltpu.VMEM
    outs = (
        sd((width // 2, width), BF16),
        sd((width // 2, width), BF16),
        sd((rows, width), BF16),
        sd((width, rows), BF16),
        sd((16, width), F32),
    )
    return call(value_bwd_kernel, "value_bwd", (place, seg, low, f, normed), outs, [v((rows, 128), F32)], 12, 0, 920000000, smem=1)


def score_bwd_kernel(seg, low, hi, lo, vals, f, de_o, col_s):
    rows, width = low.shape
    col_s[...] = label_column(seg)
    seg_row = seg[...].astype(F32)
    ones = jnp.ones((rows, 128), BF16)
    lane = lax.broadcasted_iota(jnp.int32, (1, 128), 1)

    def heads(i, _):
        at = pl.ds(pl.multiple_of(i * TILE, TILE), TILE)
        same = col_s[at, :1] == seg_row
        for j in range(HEADS // 2):
            gr = j // 2
            lanes = slice(128 * j, 128 * j + 128)
            flanes = slice(128 * gr, 128 * gr + 128)
            v_all = jnp.concatenate([vals[:, lanes], ones], 1)
            v_at = jnp.concatenate([vals[at, lanes], ones[:TILE]], 1)
            qf_all, kf_all = f[0, :, flanes], f[1, :, flanes]
            dq, dk = None, None
            for h in range(2):
                fm = lane_mask(2 * (j % 2) + h).astype(F32)
                own = jnp.where(lane // HD == h, 1.0, 0.0).astype(BF16)
                rest = 1.0 - own

                def pair(span):
                    return jnp.concatenate([low[span, lanes] * own, hi[span, lanes] * own + lo[span, lanes] * rest], 1)

                dwT = jnp.where(same, nt(v_at, pair(slice(None))), 0.0).astype(BF16)
                gk = nn(dwT, qf_all) * fm
                dk = gk if dk is None else dk + gk
                dw = jnp.where(same, nt(pair(at), v_all), 0.0).astype(BF16)
                gq = nn(dw, kf_all) * fm
                dq = gq if dq is None else dq + gq
            if j % 2 == 0:
                de_o[0, at, flanes] = dq
                de_o[1, at, flanes] = dk
            else:
                de_o[0, at, flanes] = (de_o[0, at, flanes] + dq) * f[0, at, flanes].astype(F32)
                de_o[1, at, flanes] = (de_o[1, at, flanes] + dk) * f[1, at, flanes].astype(F32)
        return 0

    lax.fori_loop(0, rows // TILE, heads, 0)


def score_bwd(seg, low, hi, lo, vals, f):
    rows = low.shape[0]
    outs = (jax.ShapeDtypeStruct((2, rows, HEADS * FEAT), F32),)
    return call(score_bwd_kernel, "score_bwd", (seg, low, hi, lo, vals, f), outs, [pltpu.VMEM((rows, 128), F32)], 12, 0, 1380000000)[0]


def key_bwd_kernel(place, de, s, rot, proj, normT, send_o, keep_o, grads_o, vec):
    c = place[2]
    rows = s.shape[1]
    width = s.shape[2]
    half = width // 2
    p_wide, blocks = block_projection(proj)
    p_hi, p_lo = split(p_wide)

    def back(i, _):
        at = pl.ds(pl.multiple_of(i * TILE, TILE), TILE)
        cos, sin_a, sin_b = rot[at, 0:128], rot[at, 128:256], rot[at, 256:384]
        for which in range(2):
            for gr in range(width // 256):
                d_hi, d_lo = split(de[which, at, 128 * gr:128 * gr + 128])
                s_at = s[which, at, 256 * gr:256 * gr + 256].astype(F32)
                ds = nt(d_hi, p_hi) + nt(d_lo, p_hi) + nt(d_hi, p_lo) - s_at * (nt(d_hi, blocks) + nt(d_lo, blocks))
                for k in range(2):
                    du = turn_back(ds[:, 128 * k:128 * k + 128], cos, sin_a, sin_b)
                    lanes = slice(256 * gr + 128 * k, 256 * gr + 128 * k + 128)
                    grads_o[which, at, lanes] = du.astype(BF16)
        return 0

    lax.fori_loop(0, rows // TILE, back, 0)
    vec[...] = jnp.zeros_like(vec)
    for which in range(2):
        vec[4 + which:5 + which, :] = jnp.sum(grads_o[which].astype(F32), 0, keepdims=True)
        keep_o[which] = nn(normT[pl.ds(pl.multiple_of(c * half, half), half), :], grads_o[which]).astype(BF16)
        send_o[which] = nn(normT[pl.ds(pl.multiple_of((1 - c) * half, half), half), :], grads_o[which]).astype(BF16)


def key_bwd(place, de, s, rot, proj, normT):
    width, rows = normT.shape
    sd = jax.ShapeDtypeStruct
    outs = (
        sd((2, width // 2, width), BF16),
        sd((2, width // 2, width), BF16),
        sd((2, rows, width), BF16),
        sd((16, width), F32),
    )
    return call(key_bwd_kernel, "key_bwd", (place, de, s, rot, proj, normT), outs, [], 12, 0, 460000000, smem=1)


def token_bwd_kernel(slopes, which, grads, gv, mg, fg, *refs):
    vecs, slope, refs = refs[:3], refs[3:3 + slopes], refs[3 + slopes:]
    tok_i, wq_i, wk_i, wv_i, gtok_o, vec, tok, wq, wk, wv, sems = refs
    feed = Feed([(tok_i, tok), (wv_i, wv), (wq_i, wq), (wk_i, wk)], sems)
    feed.need(0)
    hat, scale = norm_parts(tok[...].astype(F32))
    feed.need(1)
    ng = nt(gv[...], wv[...])
    feed.need()
    ng = ng + nt(grads[0], wq[...]) + nt(grads[1], wk[...])
    vec[...] = jnp.zeros_like(vec)
    vec[0:16, :] = vecs[0][...] + vecs[1][...] + vecs[2][...]
    vec[7:8, :] = jnp.sum(ng * hat, 0, keepdims=True)
    vec[8:9, :] = jnp.sum(ng, 0, keepdims=True)
    for n in range(slopes):
        vec[pl.ds(16 + which[n], 1), :] = slope[n][...]
    gtok_o[...] = (mg[...] + norm_back(ng, hat, scale, fg[...])).astype(BF16)


def token_bwd(which, grads, gv, mg, fg, vecs, slopes, tok, wq, wk, wv):
    rows, width = tok.shape
    n = len(slopes)
    sd, v = jax.ShapeDtypeStruct, pltpu.VMEM
    outs = (sd((rows, width), BF16), sd((16 + -(-n // 8) * 8, width), F32))
    ins = (which, grads, gv, mg, fg) + tuple(vecs) + tuple(slopes) + (tok, wq, wk, wv)
    return call(partial(token_bwd_kernel, n), "token_bwd", ins, outs,
                [v((rows, width), BF16)] + [v((width, width), BF16)] * 3, TOKEN_LIMIT, 4, 460_000_000, smem=1, far=range(len(ins) - 4, len(ins)))


def pack_kernel(place, wu, wd, bu, out, sems):
    quarter = wu.shape[1] // 4
    x, y, c = place[0], place[1], place[2]
    feed = Feed([
        (wu.at[pl.ds(pl.multiple_of((2 * x + c) * quarter, quarter), quarter)], out.at[pl.ds(0, quarter)]),
        (wd.at[pl.ds(pl.multiple_of((2 * y + c) * quarter, quarter), quarter)], out.at[pl.ds(quarter, quarter)]),
    ], sems)
    left, parts = jnp.concatenate([bu[n:n + 1, :] for n in range(bu.shape[0])], axis=1), []
    for _ in range(3):
        parts.append(left.astype(BF16).astype(F32))
        left = left - parts[-1]
    parts.append(jnp.zeros((13, left.shape[1]), F32))
    out[2 * quarter:2 * quarter + 16, :] = jnp.concatenate(parts, 0).astype(BF16)
    feed.need()


def pack(place, wu, wd, bu):
    width = wu.shape[1]
    outs = (jax.ShapeDtypeStruct((width // 2 + 16, width), BF16),)
    return call(pack_kernel, "pack", (place, wu, wd, bu), outs, [], 58, 2, 115000000, smem=1, far=(1, 2))[0]


def split_kernel(items, place, *refs):
    send, own = refs[-2:]
    step = send.shape[1]
    for n, (side, terms) in enumerate(items):
        here = place[side]
        for out, at in ((send, 1 - here), (own, here)):
            rows = pl.ds(pl.multiple_of(at * step, step), step)
            total = None
            for m, e in terms:
                term = (refs[m][rows, :] if e is None else refs[m][e, rows, :]).astype(F32)
                total = term if total is None else total + term
            out[n] = total.astype(BF16)


def split_sums(place, *sums):
    arrays, items = [], []
    for side, *terms in sums:
        at = []
        for v, e in terms:
            m = next((n for n, u in enumerate(arrays) if u is v), len(arrays))
            if m == len(arrays):
                arrays.append(v)
            at.append((m, e))
        items.append((side, tuple(at)))
    rows, width = arrays[0].shape[-2:]
    outs = (jax.ShapeDtypeStruct((len(sums), rows // 2, width), BF16),) * 2
    return call(partial(split_kernel, tuple(items)), "split_sums", (place,) + tuple(arrays), outs, [], 8, 0, 100_000_000, smem=1)


def finish_kernel(woven, place, *refs):
    mats = len(woven)
    parts, outs, (held, sems) = refs[:-mats - 2], refs[-mats - 2:-2], refs[-2:]
    c = place[2]
    rows = held.shape[2]
    feed = Feed([], sems)
    cut = FFN_STEP // 2
    per = len(parts) // 2
    for m in range(mats):
        for side, core in ((0, c), (1, 1 - c)):
            ref, entry = parts[side * per + m * per // mats], m % (mats // per)
            held[m, side] = ref[entry].astype(F32)
            if woven[m]:
                for k in range(rows // cut):
                    feed.add(held.at[m, side, pl.ds(k * cut, cut)], outs[m].at[pl.ds(pl.multiple_of(2 * k * cut + core * cut, cut), cut)])
            else:
                feed.add(held.at[m, side], outs[m].at[pl.ds(pl.multiple_of(core * rows, rows), rows)])
    feed.need()


def finish(place, mine, got, woven):
    n = len(woven)
    rows, width = mine[0].shape[1:]
    outs = (jax.ShapeDtypeStruct((2 * rows, width), F32),) * n
    return call(partial(finish_kernel, woven), "finish", (place,) + tuple(mine) + tuple(got), outs,
                [pltpu.VMEM((n, 2, rows, width), F32)], 20,
                sum(2 * (rows // (FFN_STEP // 2) if w else 1) for w in woven), 230_000_000, smem=1, far_out=range(n))


def add_low(*parts):
    total = parts[0].astype(F32)
    for part in parts[1:]:
        total = total + part.astype(F32)
    return total.astype(parts[0].dtype)


def ordered(first, then):
    return lax.optimization_barrier((first, then))[1]


class Links:
    def __init__(self, first):
        self.dp, self.ring = lax.axis_size("dp"), lax.axis_size("tensor")
        at, z = lax.axis_index("dp"), lax.axis_index("tensor")
        self.bits = [1 << n for n in range(1, self.dp.bit_length() - 1)]
        order = [1] + self.bits
        sides = [(at // bit) % 2 for bit in order]
        place = jnp.stack([sides[1], sides[-1], sides[0]]).astype(jnp.int32)
        steps = jnp.arange(self.ring, dtype=jnp.int32)
        which = (z - steps) % self.ring
        low, self.place, self.which, self.mine, self.first = lax.optimization_barrier(
            ([side == 0 for side in sides], place, which, (steps == z).astype(F32)[:, None], first))
        self.low = dict(zip(order, low))

    def swap(self, v, bit):
        return lax.ppermute(v, "dp", [(i, i ^ bit) for i in range(self.dp)])

    def shift(self, v, by=1):
        return lax.ppermute(v, "tensor", [(i, (i + by) % self.ring) for i in range(self.ring)])

    def near(self, v, bit):
        return lax.ppermute(v, "tensor", [(i, i ^ bit) for i in range(self.ring)])

    def join(self, v, got, bit, axis=None):
        low = self.low[bit]
        axis = v.ndim - 2 if axis is None else axis
        if axis < v.ndim - 2 and v.shape[axis] > 1:
            v, got = jnp.expand_dims(v, axis), jnp.expand_dims(got, axis)
        return jnp.concatenate([jnp.where(low, v, got), jnp.where(low, got, v)], axis)


def fence(*values):
    return lax.optimization_barrier(values)


def halve(links, v, bit):
    rows = v.shape[-2] // 2
    first, second = v[..., :rows, :], v[..., rows:, :]
    low = links.low[bit]
    return add_low(jnp.where(low, first, second), links.swap(jnp.where(low, second, first), bit))


def body(tokens, cotangent, segment, projection, first_gain, first_bias, w_query, w_key, w_value, w_out,
         b_query, b_key, b_value, b_out, second_gain, second_bias, w_up, b_up, w_down, b_down):
    links = Links(tokens)
    tokens, place = links.first, links.place
    rows, width = tokens.shape
    low_bit, top_bit = links.bits[0], links.bits[-1]
    order = [low_bit, top_bit] + links.bits[1:-1]
    core_low = links.low[1]
    quarter = width // 4

    def line(v):
        return v.reshape(1, -1)

    share = links.shift(pack(place, w_up, w_down, b_up.reshape(-1, 128)))
    table = jnp.asarray(rotary_table(256))
    normed, s, f, vals, rot, c0, ctx, dinv, mid, second = attn_fwd(
        tokens, segment, table, projection, line(first_gain), line(first_bias), w_query, w_key, w_value, w_out,
        line(b_query), line(b_key), line(b_value), line(b_out), line(second_gain), line(second_bias))

    def beside(share):
        return links.swap(share[:quarter], low_bit), links.swap(share[quarter:2 * quarter], top_bit)

    def own_ffn(first, last, parts, acc):
        ins = (line(b_up), mid, line(b_down), w_up, w_down) if first else parts + acc
        return ffn(first, last, place, second, cotangent, *ins)

    share, second = fence(share, second)
    swapped, coming = beside(share), links.shift(share)
    out, sgrad, send, keep, slope = own_ffn(True, False, (), ())
    swapped, out, send = fence(swapped, out, send)
    slopes, keeps, sends = [slope], [keep], [send]
    across = tuple(links.swap(v, 1) for v in (share,) + swapped)
    for n in range(1, links.ring):
        last = n == links.ring - 1
        parts = (share,) + swapped + across
        if not last:
            parts, share, out = fence(parts, coming, out)
            swapped = beside(share)
            coming = links.shift(share) if n < links.ring - 2 else share
        sends[-1] = links.swap(sends[-1], 1)
        if last:
            up_send, up_own = split_sums(place, *[(0, (keeps[k], 0), (sends[k], 0)) for k in range(2)])
            up_send, up_own, down, out = fence(up_send, up_own, add_low(keeps[1][1], sends[1][1]), out)
            up_got, down = links.swap(up_send, low_bit), links.shift(down)
        out, sgrad, send, keep, slope = own_ffn(False, last, parts, (out, sgrad))
        slopes.append(slope)
        keeps.append(keep)
        sends.append(send)
        if not last:
            swapped, coming, out = fence(swapped, coming, out)
            across = tuple(links.swap(v, 1) for v in (share,) + swapped)
            across, sends[-1] = fence(across, sends[-1])

    sgrad, up_got, down, send = fence(sgrad, up_got, down, sends[-1])
    sends[-1] = links.swap(send, 1)
    send_o, keep_o, low, hi, lo, mg, vec_o = out_bwd(
        place, sgrad, mid, line(second_gain), cotangent, ctx, dinv, c0, w_out)
    low, sends = fence(low, sends)
    up_send, up_more = split_sums(place, *[(0, (keeps[k], 0), (sends[k], 0)) for k in range(2, links.ring)])
    low, up_send, up_more, down = fence(low, up_send, up_more, add_low(down, keeps[2][1], sends[2][1]))
    down, up_last = links.shift(down), links.swap(up_send, low_bit)
    far_o = links.swap(send_o, 1)
    send_v, keep_v, gv, normT, vec_v = value_bwd(place, segment, low, f, normed)
    gv, low, down, up_last, send_v = fence(gv, low, down, up_last, send_v)
    far_v = links.swap(send_v, 1)
    up_send, up_own = split_sums(
        place, *[(1, (up_own, n), (up_got, n)) for n in range(2)], *[(1, (up_more, n), (up_last, n)) for n in range(links.ring - 2)])
    far_o, far_v, up_send, up_own, down, low = fence(far_o, far_v, up_send, up_own, add_low(down, keeps[3][1], sends[3][1]), low)
    ov_send, ov_own = split_sums(place, (0, (keep_v, None), (far_v, None)), (0, (keep_o, None), (far_o, None)))
    ov_send, ov_own, low = fence(ov_send, ov_own, low)
    down, up_got, ov_got = links.shift(down), links.swap(up_send, order[1]), links.swap(ov_send, low_bit)
    de = score_bwd(segment, low, hi, lo, vals, f)
    de, down, up_got, ov_got = fence(de, down, up_got, ov_got)
    for n in range(4, links.ring):
        down = links.shift(add_low(down, keeps[n][1], sends[n][1]))
    ov_send, ov_own = split_sums(place, *[(1, (ov_own, n), (ov_got, n)) for n in range(2)])
    down_send, down_own = split_sums(place, (0, (down, None), (keeps[0], 1), (sends[0], 1)))
    up = add_low(up_own, up_got)
    for bit in order[2:]:
        up = halve(links, up, bit)
    ov_send, ov_own, down_send, down_own, up, de = fence(ov_send, ov_own, down_send, down_own, up, de)
    ov_got, up_way, down_got = links.swap(ov_send, order[1]), links.shift(up[1]), links.swap(down_send, low_bit)
    send_k, keep_k, grads, vec_k = key_bwd(place, de, s, rot, projection, normT)
    ov_got, up_way, down_got, send_k, grads = fence(ov_got, up_way, down_got, send_k, grads)

    far_k = links.swap(send_k, 1)
    ov = add_low(ov_own, ov_got)
    for bit in order[2:]:
        ov = halve(links, ov, bit)
    ov_got = links.near(ov, 1)
    down_send, down_own = split_sums(place, (1, (down_own, 0), (down_got, 0)))
    far_k, down_send, down_own, up_way, grads = fence(far_k, down_send, down_own, add_low(up_way, up[2]), grads)
    qk_send, qk_own = split_sums(place, *[(n, (keep_k, n), (far_k, n)) for n in range(2)])
    qk_send, qk_own, grads = fence(qk_send, qk_own, grads)
    way_a, way_b = [low_bit, top_bit], [top_bit, low_bit]

    def both_ways(v, level):
        return links.swap(v[0], way_a[level]), links.swap(v[1], way_b[level])

    got_qk = both_ways(qk_send, 0)
    down_got, up_way = links.swap(down_send, order[1]), links.shift(up_way)
    ov, = fence(add_low(ov, ov_got))
    ov_got = links.near(ov, 2)
    got_qk, up_way, down_got, grads = fence(got_qk, up_way, down_got, grads)

    qk_send, qk_own = split_sums(place, *[(1 - n, (qk_own, n), (got_qk[n], None)) for n in range(2)])
    down = add_low(down_own, down_got)
    for bit in order[2:]:
        down = halve(links, down, bit)
    qk_send, qk_own, up_way, down, grads = fence(qk_send, qk_own, add_low(up_way, up[3]), down[0], grads)
    got_qk = both_ways(qk_send, 1)
    up_way = links.shift(up_way)
    gtok, vec = token_bwd(links.which, grads, gv, mg, line(first_gain), (vec_o, vec_v, vec_k), slopes, tokens, w_query, w_key, w_value)
    got_qk, up_way, vec, ov_got = fence(got_qk, up_way, vec, ov_got)

    def back_first(v):
        for bit in order[:1:-1]:
            v = links.join(v, links.swap(v, bit), bit)
        return v

    qk = jnp.stack([add_low(qk_own[n], got_qk[n]) for n in range(2)])
    for bit in order[2:]:
        qk = halve(links, qk, bit)
    for n in range(4, links.ring):
        up_way = links.shift(add_low(up_way, up[n]))
    ov = add_low(ov, ov_got)
    qk, vec, one, two = fence(
        qk, vec, back_first(jnp.stack([add_low(up_way, up[0]), ov[0]])), back_first(jnp.stack([down, ov[1]])))
    got_qk = links.near(qk, 1)
    one_got, two_got = links.swap(one, order[1]), links.swap(two, low_bit)
    vec = vec + links.swap(vec, 1)
    got_vec = links.swap(vec, low_bit)
    got_qk, one_got, two_got, got_vec = fence(got_qk, one_got, two_got, got_vec)

    qk, vec, one, two = fence(
        add_low(qk, got_qk), vec + got_vec, links.join(one, one_got, order[1]), links.join(two[:, None], two_got[:, None], low_bit, 1))
    got_qk = links.near(qk, 2)
    one_got, two_got = links.swap(one, low_bit), links.swap(two, order[1])
    got_vec = links.swap(vec, order[1])
    got_qk, one_got, two_got, got_vec = fence(got_qk, one_got, two_got, got_vec)

    qk = add_low(qk, got_qk)
    qk = [back_first(qk[n]) for n in range(2)]
    qk, vec, one, two = fence(
        qk, vec + got_vec, links.join(one, one_got, low_bit), links.join(two, two_got, order[1]).reshape(one.shape[0], -1, width))
    got_qk = both_ways(qk, 1)
    one_got, two_got = links.swap(one, 1), links.swap(two, 1)
    for bit in order[2:]:
        vec = vec + links.swap(vec, bit)
    got_vec = links.near(vec, 1)
    got_qk, one_got, two_got, got_vec = fence(got_qk, one_got, two_got, got_vec)

    def qk_in(pair, got, level):
        return [links.join(v, g, way[level]) for v, g, way in zip(pair, got, (way_a, way_b))]

    qk, vec = fence(qk_in(qk, got_qk, 1), vec + got_vec)
    got_qk = both_ways(qk, 0)
    got_vec = links.near(vec, 2)
    grad_w_up, grad_w_value, grad_w_down, grad_w_out = finish(place, [one, two], [one_got, two_got], (False, False, True, False))
    got_qk, got_vec, grad_w_up, grad_w_down, grad_w_value, grad_w_out = fence(
        got_qk, got_vec, grad_w_up, grad_w_down, grad_w_value, grad_w_out)

    qk, vec = fence([v[None] for v in qk_in(qk, got_qk, 0)], vec + got_vec)
    grad_w_query, grad_w_key = finish(place, qk, [links.swap(v, 1) for v in qk], (False, False))

    grad_b_up = jnp.sum(vec[16:16 + links.ring] * links.mine, 0)
    return (
        out, gtok, vec[7], vec[8], grad_w_query, grad_w_key, grad_w_value, grad_w_out,
        vec[4], vec[5], vec[6], vec[3], vec[0], vec[1], grad_w_up, grad_b_up, grad_w_down, vec[2],
    )


def solution(mesh):
    rows = P(("dp", "tensor"), None)
    whole = P()
    return jax.shard_map(
        body,
        mesh=mesh,
        in_specs=(rows,) * 3 + (whole,) * 13 + (P(None, "tensor"), P("tensor"), P("tensor", None), whole),
        out_specs=(rows,) * 2 + (whole,) * 12 + (P(None, "tensor"), P("tensor"), P("tensor", None), whole),
        check_vma=False,
    )
```

```python
from functools import partial
import math

import jax
import jax.numpy as jnp
import numpy as np
from jax import lax
from jax.experimental import pallas as pl
from jax.experimental.pallas import tpu as pltpu
from jax.sharding import PartitionSpec as P

HEADS = 12
HD = 64
FEAT = 32
EPS = 1e-05
F32 = jnp.float32
BF16 = jnp.bfloat16
ANY = pl.BlockSpec(memory_space=pltpu.HBM)
VM = pl.BlockSpec(memory_space=pltpu.VMEM)
SMEM = pl.BlockSpec(memory_space=pltpu.SMEM)
SCALE = HD ** -0.25


def nn(a, b):
    return lax.dot_general(a, b, (((1,), (0,)), ((), ())), preferred_element_type=F32)


def nt(a, b):
    return lax.dot_general(a, b, (((1,), (1,)), ((), ())), preferred_element_type=F32)


def split(v):
    high = v.astype(BF16)
    return high, (v - high.astype(F32)).astype(BF16)


def rotary_table(length):
    half = HD // 2
    rate = np.exp(np.arange(half) * (-2.0 * math.log(10000.0) / HD))
    angle = np.arange(length)[:, None] * rate[None, :]
    return (np.concatenate([np.cos(angle), np.sin(angle)], 1) * SCALE).astype(np.float32)


def rotary_lanes(tab):
    half = HD // 2
    lane = lax.broadcasted_iota(jnp.int32, (1, 128), 1)
    first = lane % HD < half
    cos = jnp.concatenate([tab[:, :half]] * 4, axis=1)
    sin = jnp.concatenate([tab[:, half:]] * 4, axis=1)
    table = jnp.concatenate([cos, jnp.where(first, -sin, 0.0), jnp.where(first, 0.0, sin)], axis=1)
    high = table.astype(BF16)
    rest = table - high.astype(F32)
    middle = rest.astype(BF16)
    return high, middle, (rest - middle.astype(F32)).astype(BF16)


def lane_mask(head_in_group):
    lane = lax.broadcasted_iota(jnp.int32, (1, 128), 1)
    return jnp.where(lane // FEAT == head_in_group, 1.0, 0.0).astype(BF16)


def norm_parts(v):
    centred = v - jnp.mean(v, -1, keepdims=True)
    scale = lax.rsqrt(jnp.mean(centred * centred, -1, keepdims=True) + EPS)
    return centred * scale, scale


def norm_back(grad, hat, scale, gain):
    hat_grad = grad * gain
    return scale * (
        hat_grad
        - jnp.mean(hat_grad, -1, keepdims=True)
        - hat * jnp.mean(hat_grad * hat, -1, keepdims=True)
    )


def label_column(seg):
    rows = seg.shape[1]
    return jnp.transpose(jnp.broadcast_to(seg[...].astype(F32), (128, rows)))


def block_projection(proj):
    tall = jnp.concatenate([proj[...]] * 4, axis=0)
    wide = jnp.concatenate([tall] * 4, axis=1)
    group = lax.broadcasted_iota(jnp.int32, (256, 128), 0) // HD
    feat = lax.broadcasted_iota(jnp.int32, (256, 128), 1) // FEAT
    return jnp.where(group == feat, wide, 0.0), jnp.where(group == feat, 1.0, 0.0).astype(BF16)


def turn(u, cos, sin_a, sin_b):
    return u * cos + pltpu.roll(u, 96, 1) * sin_a + pltpu.roll(u, 32, 1) * sin_b


def turn_back(u, cos, sin_a, sin_b):
    return u * cos - pltpu.roll(u, 96, 1) * sin_a - pltpu.roll(u, 32, 1) * sin_b


class Feed:
    def __init__(self, pairs, sems):
        self.sems, self.copies, self.left = sems, [], []
        for src, dst in pairs:
            self.add(src, dst)

    def add(self, src, dst):
        copy = pltpu.make_async_copy(src, dst, self.sems.at[len(self.copies)])
        copy.start()
        self.left.append(len(self.copies))
        self.copies.append(copy)

    def need(self, *which):
        for n in which or list(self.left):
            if n in self.left:
                self.copies[n].wait()
                self.left.remove(n)


def call(kernel, name, ins, outs, scratch, limit, sems, flops, smem=0, far=(), far_out=(), alias=None):
    return pl.pallas_call(
        kernel,
        out_shape=outs,
        in_specs=[SMEM if n < smem else ANY if n in far else VM for n in range(len(ins))],
        out_specs=[ANY if n in far_out else VM for n in range(len(outs))],
        scratch_shapes=list(scratch) + ([pltpu.SemaphoreType.DMA((sems,))] if sems else []),
        input_output_aliases=alias or {},
        compiler_params=pltpu.CompilerParams(vmem_limit_bytes=limit << 20),
        cost_estimate=pl.CostEstimate(flops=flops, bytes_accessed=1000, transcendentals=0),
        name=name,
    )(*ins)


TILE = 256
WHOLE = 512
TOKEN_LIMIT = 44


def attn_fwd_kernel(seg, fg, fb, bq, bk, bv, bo, sg, sb, proj, tok_i, wv_i, wq_i, tab_i, wk_i, wo_i,
                    normed_i, s_i, f_i, v_i, rot_i, c0_o, ctx_o, dinv_o, mid_o, sec_o,
                    col_s, normed_o, s_o, f_o, v_o, rot_o, tok, wv, wq, tab, wk, wo, sems):
    feed = Feed([(tab_i, tab), (tok_i, tok), (wv_i, wv)], sems)
    rows, width = tok.shape
    col_s[...] = label_column(seg)
    seg_row = seg[...].astype(F32)
    less = jnp.where(seg_row < col_s[:, :1], 1.0, 0.0)
    start = jnp.sum(less, axis=1, keepdims=True)
    place = lax.broadcasted_iota(jnp.int32, (rows, 1), 0).astype(F32) - start
    length = tab.shape[0]
    ladder = lax.broadcasted_iota(jnp.int32, (rows, length), 1).astype(F32)
    one_hot = jnp.where(ladder == place, 1.0, 0.0).astype(BF16)
    p_wide, blocks = block_projection(proj)
    p_hi, p_lo = split(p_wide)
    halves = blocks * 0.5
    feed.need(0)
    parts = rotary_lanes(tab[...])
    rot_o[...] = nn(one_hot, parts[0]) + nn(one_hot, parts[1]) + nn(one_hot, parts[2])
    feed.need(1, 2)
    for src, dst in ((wq_i, wq), (wk_i, wk), (wo_i, wo)):
        feed.add(src, dst)

    def first(i, _):
        at = pl.ds(pl.multiple_of(i * TILE, TILE), TILE)
        x = tok[at, :].astype(F32)
        hat, _scale = norm_parts(x)
        normed = (hat * fg[...] + fb[...]).astype(BF16)
        normed_o[at, :] = normed
        v_o[at, :] = nn(normed, wv[...]).astype(BF16)
        return 0

    lax.fori_loop(0, rows // TILE, first, 0)

    def rotated(i, which, w, b):
        at = pl.ds(pl.multiple_of(i * TILE, TILE), TILE)
        cos, sin_a, sin_b = rot_o[at, 0:128], rot_o[at, 128:256], rot_o[at, 256:384]
        u = nn(normed_o[at, :], w[...]) + b[...]
        for g in range(width // 256):
            s = jnp.concatenate([turn(u[:, k:k + 128], cos, sin_a, sin_b) for k in (256 * g, 256 * g + 128)], 1)
            s_hi, s_lo = split(s)
            s_o[which, at, 256 * g:256 * g + 256] = s_hi
            q_hi, q_lo = split(s * s)
            e = nn(s_hi, p_hi) + nn(s_lo, p_hi) + nn(s_hi, p_lo) - nn(q_hi, halves) - nn(q_lo, halves)
            f_o[which, at, 128 * g:128 * g + 128] = (jnp.exp(e) * FEAT ** -0.5).astype(BF16)
        return 0

    feed.need(3)
    lax.fori_loop(0, rows // TILE, lambda i, _: rotated(i, 0, wq, bq), 0)
    feed.need(4)
    lax.fori_loop(0, rows // TILE, lambda i, _: rotated(i, 1, wk, bk), 0)
    feed.need()
    for held, kept in ((normed_o, normed_i), (s_o, s_i), (f_o, f_i), (v_o, v_i), (rot_o, rot_i)):
        feed.add(held, kept)

    ones = jnp.ones((rows, 128), BF16)
    even = lax.broadcasted_iota(jnp.int32, (1, 128), 1) < HD

    def second(i, _):
        at = pl.ds(pl.multiple_of(i * TILE, TILE), TILE)
        same = col_s[at, :1] == seg_row
        for j in range(HEADS // 2):
            g = j // 2
            vals = jnp.concatenate([v_o[:, 128 * j:128 * j + 128], ones], 1)
            qf = f_o[0, at, 128 * g:128 * g + 128]
            kf = f_o[1, :, 128 * g:128 * g + 128]
            res = []
            for h in range(2):
                scores = nt(qf * lane_mask(2 * (j % 2) + h), kf)
                weights = jnp.where(same, scores, 0.0).astype(BF16)
                res.append(nn(weights, vals))
            num = jnp.where(even, res[0][:, :128], res[1][:, :128])
            inv = 1.0 / jnp.where(even, res[0][:, 128:], res[1][:, 128:])
            lanes = slice(128 * j, 128 * j + 128)
            ctx = num * inv
            dinv_o[at, lanes] = inv
            c0_o[at, lanes] = ctx
            ctx_o[at, lanes] = (ctx + bv[:, lanes]).astype(BF16)
        middle = tok[at, :].astype(F32) + nn(ctx_o[at, :], wo[...]) + bo[...]
        mid_o[at, :] = middle
        hat, _scale = norm_parts(middle)
        sec_o[at, :] = (hat * sg[...] + sb[...]).astype(BF16)
        return 0

    lax.fori_loop(0, rows // TILE, second, 0)
    feed.need()


def attn_fwd(tok, seg, tab, proj, fg, fb, wq, wk, wv, wo, bq, bk, bv, bo, sg, sb):
    rows, width = tok.shape
    sd, v = jax.ShapeDtypeStruct, pltpu.VMEM
    outs = (
        sd((rows, width), BF16),
        sd((2, rows, width), BF16),
        sd((2, rows, HEADS * FEAT), BF16),
        sd((rows, width), BF16),
        sd((rows, 384), F32),
        sd((rows, width), F32),
        sd((rows, width), BF16),
        sd((rows, width), F32),
        sd((rows, width), F32),
        sd((rows, width), BF16),
    )
    near = (seg, fg, fb, bq, bk, bv, bo, sg, sb, proj)
    far = (tok, wv, wq, tab, wk, wo)
    scratch = [v((rows, 128), F32)] + [v(a.shape, a.dtype) for a in outs[:5] + far]
    return call(attn_fwd_kernel, "attn_fwd", near + far, outs, scratch, 48, len(far) + 5, 5520000000,
                far=range(len(near), len(near) + len(far)), far_out=range(5))


FFN_STEP = 256


def ffn_kernel(first, last, place, sec, cot, *refs):
    n_in = 5 if first else 8
    ins, refs = refs[:n_in], refs[n_in:]
    out_o, sg_o, send_o, keep_o, gb_o, wu, wd, secT, hidT, acc, sems = refs
    x, y, c = place[0], place[1], place[2]
    rows, width = sec.shape
    quarter, half = width // 4, width // 2

    def part(a, core):
        return pl.ds(pl.multiple_of((2 * a + core) * quarter, quarter), quarter)

    if first:
        bu, oacc, bd, wu_i, wd_i = ins
        feed = Feed([(wu_i, wu), (wd_i, wd), (oacc, acc)], sems)
        bias = bu[...]
        early = (0,)
    else:
        own, own_x, own_y, far, far_x, far_y, oacc, sacc = ins
        up, down = pl.ds(0, quarter), pl.ds(quarter, quarter)
        feed = Feed([
            (own.at[up], wu.at[part(x, c)]), (own_x, wu.at[part(1 - x, c)]),
            (far.at[up], wu.at[part(x, 1 - c)]), (far_x, wu.at[part(1 - x, 1 - c)]),
            (own.at[down], wd.at[part(y, c)]), (own_y, wd.at[part(1 - y, c)]),
            (far.at[down], wd.at[part(y, 1 - c)]), (far_y, wd.at[part(1 - y, 1 - c)]),
        ], sems)
        tail = own[2 * quarter:2 * quarter + 16, :].astype(F32)
        bias = tail[0:1, :] + tail[1:2, :] + tail[2:3, :]
        early = (0, 1, 2, 3)
    mine = pl.ds(pl.multiple_of(c * half, half), half)
    other = pl.ds(pl.multiple_of((1 - c) * half, half), half)
    secT[...] = jnp.transpose(sec[...])
    feed.need(*early)
    cut = FFN_STEP // 2
    for n, at in enumerate(range(0, width, FFN_STEP)):
        cs = slice(at, at + FFN_STEP)
        inner = nn(sec[...], wu[:, cs]) + bias[:, cs]
        cdf = 0.5 + 0.5 * lax.erf(inner * math.sqrt(0.5))
        slope = cdf + inner * (jnp.exp(-0.5 * inner * inner) * (1.0 / math.sqrt(2.0 * math.pi)))
        hidden = (inner * cdf).astype(BF16)
        feed.need()
        grad = (nt(cot[...], wd[cs, :]) * slope).astype(BF16)
        gb_o[:, cs] = jnp.sum(grad.astype(F32), 0, keepdims=True)
        more_out = nn(hidden, wd[cs, :])
        more_sg = nt(grad, wu[:, cs])
        if n == 0:
            acc[...] = (acc[...] + bd[...] if first else oacc[...]) + more_out
            sg_o[...] = more_sg if first else sacc[...] + more_sg
        else:
            acc[...] += more_out
            sg_o[...] += more_sg
        hidT[...] = jnp.transpose(hidden)
        piece = slice(n * cut, n * cut + cut)
        keep_o[1, piece, :] = nn(hidT[pl.ds(pl.multiple_of(c * cut, cut), cut), :], cot[...]).astype(BF16)
        send_o[1, piece, :] = nn(hidT[pl.ds(pl.multiple_of((1 - c) * cut, cut), cut), :], cot[...]).astype(BF16)
        keep_o[0, :, cs] = nn(secT[mine, :], grad).astype(BF16)
        send_o[0, :, cs] = nn(secT[other, :], grad).astype(BF16)
    out_o[...] = acc[...].astype(out_o.dtype)


def ffn(first, last, place, sec, cot, *ins):
    rows, width = sec.shape
    sd, v = jax.ShapeDtypeStruct, pltpu.VMEM
    outs = (
        sd((rows, width), BF16 if last else F32),
        sd((rows, width), F32),
        sd((2, width // 2, width), BF16),
        sd((2, width // 2, width), BF16),
        sd((1, width), F32),
    )
    scratch = [v((width, width), BF16), v((width, width), BF16), v((width, rows), BF16), v((FFN_STEP, rows), BF16),
               v((rows, width), F32)]
    return call(partial(ffn_kernel, first, last), "ffn", (place, sec, cot) + ins, outs, scratch, 14, 8, 690000000, smem=1,
                far=(4, 6, 7) if first else (), alias=None if first else {10: 1})


def out_bwd_kernel(place, sgrad, mid, sg, cot, ctx, dinv, c0, wo_i,
                   send_o, keep_o, low_o, hi_o, lo_o, mg_o, vec, wo, tr_s, cg_s, sems):
    feed = Feed([(wo_i, wo)], sems)
    c = place[2]
    rows, width = mid.shape
    half = width // 2
    tr_s[...] = jnp.transpose(ctx[...])
    hat, scale = norm_parts(mid[...])
    up = sgrad[...]
    vec[...] = jnp.zeros_like(vec)
    vec[0:1, :] = jnp.sum(up * hat, 0, keepdims=True)
    vec[1:2, :] = jnp.sum(up, 0, keepdims=True)
    g = cot[...].astype(F32)
    vec[2:3, :] = jnp.sum(g, 0, keepdims=True)
    mg = g + norm_back(up, hat, scale, sg[...])
    mg_o[...] = mg
    og = mg.astype(BF16)
    vec[3:4, :] = jnp.sum(og.astype(F32), 0, keepdims=True)
    feed.need()
    cg_s[...] = nt(og, wo[...])
    keep_o[...] = nn(tr_s[pl.ds(pl.multiple_of(c * half, half), half), :], og).astype(BF16)
    send_o[...] = nn(tr_s[pl.ds(pl.multiple_of((1 - c) * half, half), half), :], og).astype(BF16)
    for j in range(HEADS // 2):
        lanes = slice(128 * j, 128 * j + 128)
        low = (cg_s[:, lanes] * dinv[:, lanes]).astype(BF16)
        low_o[:, lanes] = low
        less = -(low.astype(F32) * c0[:, lanes])
        hi = less.astype(BF16)
        hi_o[:, lanes] = hi
        lo_o[:, lanes] = pltpu.roll(less - hi.astype(F32), 64, 1).astype(BF16)


def out_bwd(place, sgrad, mid, sg, cot, ctx, dinv, c0, wo):
    rows, width = mid.shape
    sd, v = jax.ShapeDtypeStruct, pltpu.VMEM
    outs = (
        sd((width // 2, width), BF16),
        sd((width // 2, width), BF16),
        sd((rows, width), BF16),
        sd((rows, width), BF16),
        sd((rows, width), BF16),
        sd((rows, width), F32),
        sd((16, width), F32),
    )
    scratch = [v((width, width), BF16), v((width, rows), BF16), v((rows, width), F32)]
    return call(out_bwd_kernel, "out_bwd", (place, sgrad, mid, sg, cot, ctx, dinv, c0, wo), outs, scratch, 12, 1, 575000000, smem=1, far=(8,))


def value_bwd_kernel(place, seg, low, f, normed, send_o, keep_o, gv_o, normT_o, vec, col_s):
    c = place[2]
    rows, width = low.shape
    half = width // 2
    col_s[...] = label_column(seg)
    seg_row = seg[...].astype(F32)
    lane = lax.broadcasted_iota(jnp.int32, (1, 128), 1)

    def heads(i, _):
        at = pl.ds(pl.multiple_of(i * TILE, TILE), TILE)
        same = col_s[at, :1] == seg_row
        for j in range(HEADS // 2):
            lanes = slice(128 * j, 128 * j + 128)
            flanes = slice(128 * (j // 2), 128 * (j // 2) + 128)
            res = []
            for h in range(2):
                fm = lane_mask(2 * (j % 2) + h)
                wT = jnp.where(same, nt(f[1, at, flanes] * fm, f[0, :, flanes]), 0.0).astype(BF16)
                res.append(nn(wT, low[:, lanes]))
            gv_o[at, lanes] = jnp.where(lane < HD, res[0], res[1]).astype(BF16)
        return 0

    lax.fori_loop(0, rows // TILE, heads, 0)
    normT_o[...] = jnp.transpose(normed[...])
    vec[...] = jnp.zeros_like(vec)
    vec[6:7, :] = jnp.sum(gv_o[...].astype(F32), 0, keepdims=True)
    keep_o[...] = nn(normT_o[pl.ds(pl.multiple_of(c * half, half), half), :], gv_o[...]).astype(BF16)
    send_o[...] = nn(normT_o[pl.ds(pl.multiple_of((1 - c) * half, half), half), :], gv_o[...]).astype(BF16)


def value_bwd(place, seg, low, f, normed):
    rows, width = low.shape
    sd, v = jax.ShapeDtypeStruct, pltpu.VMEM
    outs = (
        sd((width // 2, width), BF16),
        sd((width // 2, width), BF16),
        sd((rows, width), BF16),
        sd((width, rows), BF16),
        sd((16, width), F32),
    )
    return call(value_bwd_kernel, "value_bwd", (place, seg, low, f, normed), outs, [v((rows, 128), F32)], 12, 0, 920000000, smem=1)


def score_bwd_kernel(seg, low, hi, lo, vals, f, de_o, col_s):
    rows, width = low.shape
    col_s[...] = label_column(seg)
    seg_row = seg[...].astype(F32)
    ones = jnp.ones((rows, 128), BF16)
    lane = lax.broadcasted_iota(jnp.int32, (1, 128), 1)

    def heads(i, _):
        at = pl.ds(pl.multiple_of(i * WHOLE, WHOLE), WHOLE)
        same = col_s[at, :1] == seg_row
        for j in range(HEADS // 2):
            gr = j // 2
            lanes = slice(128 * j, 128 * j + 128)
            flanes = slice(128 * gr, 128 * gr + 128)
            v_all = jnp.concatenate([vals[:, lanes], ones], 1)
            v_at = jnp.concatenate([vals[at, lanes], ones[:WHOLE]], 1)
            qf_all, kf_all = f[0, :, flanes], f[1, :, flanes]
            dq, dk = None, None
            for h in range(2):
                fm = lane_mask(2 * (j % 2) + h).astype(F32)
                own = jnp.where(lane // HD == h, 1.0, 0.0).astype(BF16)
                rest = 1.0 - own

                def pair(span):
                    return jnp.concatenate([low[span, lanes] * own, hi[span, lanes] * own + lo[span, lanes] * rest], 1)

                dwT = jnp.where(same, nt(v_at, pair(slice(None))), 0.0).astype(BF16)
                gk = nn(dwT, qf_all) * fm
                dk = gk if dk is None else dk + gk
                dw = jnp.where(same, nt(pair(at), v_all), 0.0).astype(BF16)
                gq = nn(dw, kf_all) * fm
                dq = gq if dq is None else dq + gq
            if j % 2 == 0:
                de_o[0, at, flanes] = dq
                de_o[1, at, flanes] = dk
            else:
                de_o[0, at, flanes] = (de_o[0, at, flanes] + dq) * f[0, at, flanes].astype(F32)
                de_o[1, at, flanes] = (de_o[1, at, flanes] + dk) * f[1, at, flanes].astype(F32)
        return 0

    lax.fori_loop(0, rows // WHOLE, heads, 0)


def score_bwd(seg, low, hi, lo, vals, f):
    rows = low.shape[0]
    outs = (jax.ShapeDtypeStruct((2, rows, HEADS * FEAT), F32),)
    return call(score_bwd_kernel, "score_bwd", (seg, low, hi, lo, vals, f), outs, [pltpu.VMEM((rows, 128), F32)], 12, 0, 1380000000)[0]


def key_bwd_kernel(place, de, s, rot, proj, normT, send_o, keep_o, grads_o, vec):
    c = place[2]
    rows = s.shape[1]
    width = s.shape[2]
    half = width // 2
    p_wide, blocks = block_projection(proj)
    p_hi, p_lo = split(p_wide)

    def back(i, _):
        at = pl.ds(pl.multiple_of(i * WHOLE, WHOLE), WHOLE)
        cos, sin_a, sin_b = rot[at, 0:128], rot[at, 128:256], rot[at, 256:384]
        for which in range(2):
            for gr in range(width // 256):
                d_hi, d_lo = split(de[which, at, 128 * gr:128 * gr + 128])
                s_at = s[which, at, 256 * gr:256 * gr + 256].astype(F32)
                ds = nt(d_hi, p_hi) + nt(d_lo, p_hi) + nt(d_hi, p_lo) - s_at * (nt(d_hi, blocks) + nt(d_lo, blocks))
                for k in range(2):
                    du = turn_back(ds[:, 128 * k:128 * k + 128], cos, sin_a, sin_b)
                    lanes = slice(256 * gr + 128 * k, 256 * gr + 128 * k + 128)
                    grads_o[which, at, lanes] = du.astype(BF16)
        return 0

    lax.fori_loop(0, rows // WHOLE, back, 0)
    vec[...] = jnp.zeros_like(vec)
    for which in range(2):
        vec[4 + which:5 + which, :] = jnp.sum(grads_o[which].astype(F32), 0, keepdims=True)
        keep_o[which] = nn(normT[pl.ds(pl.multiple_of(c * half, half), half), :], grads_o[which]).astype(BF16)
        send_o[which] = nn(normT[pl.ds(pl.multiple_of((1 - c) * half, half), half), :], grads_o[which]).astype(BF16)


def key_bwd(place, de, s, rot, proj, normT):
    width, rows = normT.shape
    sd = jax.ShapeDtypeStruct
    outs = (
        sd((2, width // 2, width), BF16),
        sd((2, width // 2, width), BF16),
        sd((2, rows, width), BF16),
        sd((16, width), F32),
    )
    return call(key_bwd_kernel, "key_bwd", (place, de, s, rot, proj, normT), outs, [], 12, 0, 460000000, smem=1)


def token_bwd_kernel(slopes, which, grads, gv, mg, fg, *refs):
    vecs, slope, refs = refs[:3], refs[3:3 + slopes], refs[3 + slopes:]
    tok_i, wq_i, wk_i, wv_i, gtok_o, vec, tok, wq, wk, wv, sems = refs
    feed = Feed([(tok_i, tok), (wv_i, wv), (wq_i, wq), (wk_i, wk)], sems)
    feed.need(0)
    hat, scale = norm_parts(tok[...].astype(F32))
    feed.need(1)
    ng = nt(gv[...], wv[...])
    feed.need()
    ng = ng + nt(grads[0], wq[...]) + nt(grads[1], wk[...])
    vec[...] = jnp.zeros_like(vec)
    vec[0:16, :] = vecs[0][...] + vecs[1][...] + vecs[2][...]
    vec[7:8, :] = jnp.sum(ng * hat, 0, keepdims=True)
    vec[8:9, :] = jnp.sum(ng, 0, keepdims=True)
    for n in range(slopes):
        vec[pl.ds(16 + which[n], 1), :] = slope[n][...]
    gtok_o[...] = (mg[...] + norm_back(ng, hat, scale, fg[...])).astype(BF16)


def token_bwd(which, grads, gv, mg, fg, vecs, slopes, tok, wq, wk, wv):
    rows, width = tok.shape
    n = len(slopes)
    sd, v = jax.ShapeDtypeStruct, pltpu.VMEM
    outs = (sd((rows, width), BF16), sd((16 + -(-n // 8) * 8, width), F32))
    ins = (which, grads, gv, mg, fg) + tuple(vecs) + tuple(slopes) + (tok, wq, wk, wv)
    return call(partial(token_bwd_kernel, n), "token_bwd", ins, outs,
                [v((rows, width), BF16)] + [v((width, width), BF16)] * 3, TOKEN_LIMIT, 4, 460_000_000, smem=1, far=range(len(ins) - 4, len(ins)))


def pack_kernel(place, wu, wd, bu, out, sems):
    quarter = wu.shape[1] // 4
    x, y, c = place[0], place[1], place[2]
    feed = Feed([
        (wu.at[pl.ds(pl.multiple_of((2 * x + c) * quarter, quarter), quarter)], out.at[pl.ds(0, quarter)]),
        (wd.at[pl.ds(pl.multiple_of((2 * y + c) * quarter, quarter), quarter)], out.at[pl.ds(quarter, quarter)]),
    ], sems)
    left, parts = jnp.concatenate([bu[n:n + 1, :] for n in range(bu.shape[0])], axis=1), []
    for _ in range(3):
        parts.append(left.astype(BF16).astype(F32))
        left = left - parts[-1]
    parts.append(jnp.zeros((13, left.shape[1]), F32))
    out[2 * quarter:2 * quarter + 16, :] = jnp.concatenate(parts, 0).astype(BF16)
    feed.need()


def pack(place, wu, wd, bu):
    width = wu.shape[1]
    outs = (jax.ShapeDtypeStruct((width // 2 + 16, width), BF16),)
    return call(pack_kernel, "pack", (place, wu, wd, bu), outs, [], 58, 2, 115000000, smem=1, far=(1, 2))[0]


def split_kernel(items, place, *refs):
    send, own = refs[-2:]
    step = send.shape[1]
    for n, (side, terms) in enumerate(items):
        here = place[side]
        for out, at in ((send, 1 - here), (own, here)):
            rows = pl.ds(pl.multiple_of(at * step, step), step)
            total = None
            for m, e in terms:
                term = (refs[m][rows, :] if e is None else refs[m][e, rows, :]).astype(F32)
                total = term if total is None else total + term
            out[n] = total.astype(BF16)


def split_sums(place, *sums):
    arrays, items = [], []
    for side, *terms in sums:
        at = []
        for v, e in terms:
            m = next((n for n, u in enumerate(arrays) if u is v), len(arrays))
            if m == len(arrays):
                arrays.append(v)
            at.append((m, e))
        items.append((side, tuple(at)))
    rows, width = arrays[0].shape[-2:]
    outs = (jax.ShapeDtypeStruct((len(sums), rows // 2, width), BF16),) * 2
    return call(partial(split_kernel, tuple(items)), "split_sums", (place,) + tuple(arrays), outs, [], 8, 0, 100_000_000, smem=1)


def finish_kernel(woven, place, *refs):
    mats = len(woven)
    parts, outs, (held, sems) = refs[:-mats - 2], refs[-mats - 2:-2], refs[-2:]
    c = place[2]
    rows = held.shape[2]
    feed = Feed([], sems)
    cut = FFN_STEP // 2
    per = len(parts) // 2
    for m in range(mats):
        for side, core in ((0, c), (1, 1 - c)):
            ref, entry = parts[side * per + m * per // mats], m % (mats // per)
            held[m, side] = ref[entry].astype(F32)
            if woven[m]:
                for k in range(rows // cut):
                    feed.add(held.at[m, side, pl.ds(k * cut, cut)], outs[m].at[pl.ds(pl.multiple_of(2 * k * cut + core * cut, cut), cut)])
            else:
                feed.add(held.at[m, side], outs[m].at[pl.ds(pl.multiple_of(core * rows, rows), rows)])
    feed.need()


def finish(place, mine, got, woven):
    n = len(woven)
    rows, width = mine[0].shape[1:]
    outs = (jax.ShapeDtypeStruct((2 * rows, width), F32),) * n
    return call(partial(finish_kernel, woven), "finish", (place,) + tuple(mine) + tuple(got), outs,
                [pltpu.VMEM((n, 2, rows, width), F32)], 20,
                sum(2 * (rows // (FFN_STEP // 2) if w else 1) for w in woven), 230_000_000, smem=1, far_out=range(n))


def add_low(*parts):
    total = parts[0].astype(F32)
    for part in parts[1:]:
        total = total + part.astype(F32)
    return total.astype(parts[0].dtype)


def ordered(first, then):
    return lax.optimization_barrier((first, then))[1]


class Links:
    def __init__(self, first):
        self.dp, self.ring = lax.axis_size("dp"), lax.axis_size("tensor")
        at, z = lax.axis_index("dp"), lax.axis_index("tensor")
        self.bits = [1 << n for n in range(1, self.dp.bit_length() - 1)]
        order = [1] + self.bits
        sides = [(at // bit) % 2 for bit in order]
        place = jnp.stack([sides[1], sides[-1], sides[0]]).astype(jnp.int32)
        steps = jnp.arange(self.ring, dtype=jnp.int32)
        which = (z - steps) % self.ring
        low, self.place, self.which, self.mine, self.first = lax.optimization_barrier(
            ([side == 0 for side in sides], place, which, (steps == z).astype(F32)[:, None], first))
        self.low = dict(zip(order, low))

    def swap(self, v, bit):
        return lax.ppermute(v, "dp", [(i, i ^ bit) for i in range(self.dp)])

    def shift(self, v, by=1):
        return lax.ppermute(v, "tensor", [(i, (i + by) % self.ring) for i in range(self.ring)])

    def near(self, v, bit):
        return lax.ppermute(v, "tensor", [(i, i ^ bit) for i in range(self.ring)])

    def join(self, v, got, bit, axis=None):
        low = self.low[bit]
        axis = v.ndim - 2 if axis is None else axis
        if axis < v.ndim - 2 and v.shape[axis] > 1:
            v, got = jnp.expand_dims(v, axis), jnp.expand_dims(got, axis)
        return jnp.concatenate([jnp.where(low, v, got), jnp.where(low, got, v)], axis)


def fence(*values):
    return lax.optimization_barrier(values)


def halve(links, v, bit):
    rows = v.shape[-2] // 2
    first, second = v[..., :rows, :], v[..., rows:, :]
    low = links.low[bit]
    return add_low(jnp.where(low, first, second), links.swap(jnp.where(low, second, first), bit))


def body(tokens, cotangent, segment, projection, first_gain, first_bias, w_query, w_key, w_value, w_out,
         b_query, b_key, b_value, b_out, second_gain, second_bias, w_up, b_up, w_down, b_down):
    links = Links(tokens)
    tokens, place = links.first, links.place
    rows, width = tokens.shape
    low_bit, top_bit = links.bits[0], links.bits[-1]
    order = [low_bit, top_bit] + links.bits[1:-1]
    core_low = links.low[1]
    quarter = width // 4

    def line(v):
        return v.reshape(1, -1)

    share = links.shift(pack(place, w_up, w_down, b_up.reshape(-1, 128)))
    table = jnp.asarray(rotary_table(256))
    normed, s, f, vals, rot, c0, ctx, dinv, mid, second = attn_fwd(
        tokens, segment, table, projection, line(first_gain), line(first_bias), w_query, w_key, w_value, w_out,
        line(b_query), line(b_key), line(b_value), line(b_out), line(second_gain), line(second_bias))

    def beside(share):
        return links.swap(share[:quarter], low_bit), links.swap(share[quarter:2 * quarter], top_bit)

    def own_ffn(first, last, parts, acc):
        ins = (line(b_up), mid, line(b_down), w_up, w_down) if first else parts + acc
        return ffn(first, last, place, second, cotangent, *ins)

    share, second = fence(share, second)
    swapped, coming = beside(share), links.shift(share)
    out, sgrad, send, keep, slope = own_ffn(True, False, (), ())
    swapped, out, send = fence(swapped, out, send)
    slopes, keeps, sends = [slope], [keep], [send]
    across = tuple(links.swap(v, 1) for v in (share,) + swapped)
    for n in range(1, links.ring):
        last = n == links.ring - 1
        parts = (share,) + swapped + across
        if not last:
            parts, share, out = fence(parts, coming, out)
            swapped = beside(share)
            coming = links.shift(share) if n < links.ring - 2 else share
        sends[-1] = links.swap(sends[-1], 1)
        if last:
            up_send, up_own = split_sums(place, *[(0, (keeps[k], 0), (sends[k], 0)) for k in range(2)])
            up_send, up_own, down, out = fence(up_send, up_own, add_low(keeps[1][1], sends[1][1]), out)
            up_got, down = links.swap(up_send, low_bit), links.shift(down)
        out, sgrad, send, keep, slope = own_ffn(False, last, parts, (out, sgrad))
        slopes.append(slope)
        keeps.append(keep)
        sends.append(send)
        if not last:
            swapped, coming, out = fence(swapped, coming, out)
            across = tuple(links.swap(v, 1) for v in (share,) + swapped)
            across, sends[-1] = fence(across, sends[-1])

    sgrad, up_got, down, send = fence(sgrad, up_got, down, sends[-1])
    sends[-1] = links.swap(send, 1)
    send_o, keep_o, low, hi, lo, mg, vec_o = out_bwd(
        place, sgrad, mid, line(second_gain), cotangent, ctx, dinv, c0, w_out)
    low, sends = fence(low, sends)
    up_send, up_more = split_sums(place, *[(0, (keeps[k], 0), (sends[k], 0)) for k in range(2, links.ring)])
    low, up_send, up_more, down = fence(low, up_send, up_more, add_low(down, keeps[2][1], sends[2][1]))
    down, up_last = links.shift(down), links.swap(up_send, low_bit)
    far_o = links.swap(send_o, 1)
    send_v, keep_v, gv, normT, vec_v = value_bwd(place, segment, low, f, normed)
    gv, low, down, up_last, send_v = fence(gv, low, down, up_last, send_v)
    far_v = links.swap(send_v, 1)
    up_send, up_own = split_sums(
        place, *[(1, (up_own, n), (up_got, n)) for n in range(2)], *[(1, (up_more, n), (up_last, n)) for n in range(links.ring - 2)])
    far_o, far_v, up_send, up_own, down, low = fence(far_o, far_v, up_send, up_own, add_low(down, keeps[3][1], sends[3][1]), low)
    ov_send, ov_own = split_sums(place, (0, (keep_v, None), (far_v, None)), (0, (keep_o, None), (far_o, None)))
    ov_send, ov_own, low = fence(ov_send, ov_own, low)
    down, up_got, ov_got = links.shift(down), links.swap(up_send, order[1]), links.swap(ov_send, low_bit)
    de = score_bwd(segment, low, hi, lo, vals, f)
    de, down, up_got, ov_got = fence(de, down, up_got, ov_got)
    for n in range(4, links.ring):
        down = links.shift(add_low(down, keeps[n][1], sends[n][1]))
    ov_send, ov_own = split_sums(place, *[(1, (ov_own, n), (ov_got, n)) for n in range(2)])
    down_send, down_own = split_sums(place, (0, (down, None), (keeps[0], 1), (sends[0], 1)))
    up = add_low(up_own, up_got)
    for bit in order[2:]:
        up = halve(links, up, bit)
    ov_send, ov_own, down_send, down_own, up, de = fence(ov_send, ov_own, down_send, down_own, up, de)
    ov_got, up_way, down_got = links.swap(ov_send, order[1]), links.shift(up[1]), links.swap(down_send, low_bit)
    send_k, keep_k, grads, vec_k = key_bwd(place, de, s, rot, projection, normT)
    ov_got, up_way, down_got, send_k, grads = fence(ov_got, up_way, down_got, send_k, grads)

    far_k = links.swap(send_k, 1)
    ov = add_low(ov_own, ov_got)
    for bit in order[2:]:
        ov = halve(links, ov, bit)
    ov_got = links.near(ov, 1)
    down_send, down_own = split_sums(place, (1, (down_own, 0), (down_got, 0)))
    far_k, down_send, down_own, up_way, grads = fence(far_k, down_send, down_own, add_low(up_way, up[2]), grads)
    qk_send, qk_own = split_sums(place, *[(n, (keep_k, n), (far_k, n)) for n in range(2)])
    qk_send, qk_own, grads = fence(qk_send, qk_own, grads)
    way_a, way_b = [low_bit, top_bit], [top_bit, low_bit]

    def both_ways(v, level):
        return links.swap(v[0], way_a[level]), links.swap(v[1], way_b[level])

    got_qk = both_ways(qk_send, 0)
    down_got, up_way = links.swap(down_send, order[1]), links.shift(up_way)
    ov, = fence(add_low(ov, ov_got))
    ov_got = links.near(ov, 2)
    got_qk, up_way, down_got, grads = fence(got_qk, up_way, down_got, grads)

    qk_send, qk_own = split_sums(place, *[(1 - n, (qk_own, n), (got_qk[n], None)) for n in range(2)])
    down = add_low(down_own, down_got)
    for bit in order[2:]:
        down = halve(links, down, bit)
    qk_send, qk_own, up_way, down, grads = fence(qk_send, qk_own, add_low(up_way, up[3]), down[0], grads)
    got_qk = both_ways(qk_send, 1)
    up_way = links.shift(up_way)
    gtok, vec = token_bwd(links.which, grads, gv, mg, line(first_gain), (vec_o, vec_v, vec_k), slopes, tokens, w_query, w_key, w_value)
    got_qk, up_way, vec, ov_got = fence(got_qk, up_way, vec, ov_got)

    def back_first(v):
        for bit in order[:1:-1]:
            v = links.join(v, links.swap(v, bit), bit)
        return v

    qk = jnp.stack([add_low(qk_own[n], got_qk[n]) for n in range(2)])
    for bit in order[2:]:
        qk = halve(links, qk, bit)
    for n in range(4, links.ring):
        up_way = links.shift(add_low(up_way, up[n]))
    ov = add_low(ov, ov_got)
    qk, vec, one, two = fence(
        qk, vec, back_first(jnp.stack([add_low(up_way, up[0]), ov[0]])), back_first(jnp.stack([down, ov[1]])))
    got_qk = links.near(qk, 1)
    one_got, two_got = links.swap(one, order[1]), links.swap(two, low_bit)
    vec = vec + links.swap(vec, 1)
    got_vec = links.swap(vec, low_bit)
    got_qk, one_got, two_got, got_vec = fence(got_qk, one_got, two_got, got_vec)

    qk, vec, one, two = fence(
        add_low(qk, got_qk), vec + got_vec, links.join(one, one_got, order[1]), links.join(two[:, None], two_got[:, None], low_bit, 1))
    got_qk = links.near(qk, 2)
    one_got, two_got = links.swap(one, low_bit), links.swap(two, order[1])
    got_vec = links.swap(vec, order[1])
    got_qk, one_got, two_got, got_vec = fence(got_qk, one_got, two_got, got_vec)

    qk = add_low(qk, got_qk)
    qk = [back_first(qk[n]) for n in range(2)]
    qk, vec, one, two = fence(
        qk, vec + got_vec, links.join(one, one_got, low_bit), links.join(two, two_got, order[1]).reshape(one.shape[0], -1, width))
    got_qk = both_ways(qk, 1)
    one_got, two_got = links.swap(one, 1), links.swap(two, 1)
    for bit in order[2:]:
        vec = vec + links.swap(vec, bit)
    got_vec = links.near(vec, 1)
    got_qk, one_got, two_got, got_vec = fence(got_qk, one_got, two_got, got_vec)

    def qk_in(pair, got, level):
        return [links.join(v, g, way[level]) for v, g, way in zip(pair, got, (way_a, way_b))]

    qk, vec = fence(qk_in(qk, got_qk, 1), vec + got_vec)
    got_qk = both_ways(qk, 0)
    got_vec = links.near(vec, 2)
    grad_w_up, grad_w_value, grad_w_down, grad_w_out = finish(place, [one, two], [one_got, two_got], (False, False, True, False))
    got_qk, got_vec, grad_w_up, grad_w_down, grad_w_value, grad_w_out = fence(
        got_qk, got_vec, grad_w_up, grad_w_down, grad_w_value, grad_w_out)

    qk, vec = fence([v[None] for v in qk_in(qk, got_qk, 0)], vec + got_vec)
    grad_w_query, grad_w_key = finish(place, qk, [links.swap(v, 1) for v in qk], (False, False))

    grad_b_up = jnp.sum(vec[16:16 + links.ring] * links.mine, 0)
    return (
        out, gtok, vec[7], vec[8], grad_w_query, grad_w_key, grad_w_value, grad_w_out,
        vec[4], vec[5], vec[6], vec[3], vec[0], vec[1], grad_w_up, grad_b_up, grad_w_down, vec[2],
    )


def solution(mesh):
    rows = P(("dp", "tensor"), None)
    whole = P()
    return jax.shard_map(
        body,
        mesh=mesh,
        in_specs=(rows,) * 3 + (whole,) * 13 + (P(None, "tensor"), P("tensor"), P("tensor", None), whole),
        out_specs=(rows,) * 2 + (whole,) * 12 + (P(None, "tensor"), P("tensor"), P("tensor", None), whole),
        check_vma=False,
    )
```
